128 devices in a mesh: ctx: 16 (over z, x_hi, core), shard: 8 (over x_lo, y).
Axes of the slice: x: 4 (x_hi: 2, x_lo: 2; x = x_hi * 2 + x_lo), y: 4, z: 4, core: 2. Of those that a mesh axis runs over, the one named last changes fastest.
Arguments:
- streams: bfloat16 [8, 4, 2048, 1024], P('shard', None, 'ctx'), may hold values from -6 to 6
- segments: int32 [8, 2048], P('shard', 'ctx'), may hold values from 0 to 4, as said below
- stream_mix: float32 [2, 4, 6], replicated, may hold values from -0.3 to 1.5
- qkv_weight: bfloat16 [3, 1024, 1024], P(None, 'shard'), may hold values from -0.1875 to 0.1875
- out_weight: bfloat16 [1024, 1024], P('shard'), may hold values from -3 to 3
- gate_up_weight: bfloat16 [2, 1024, 2816], P(None, 'shard'), may hold values from -0.1875 to 0.1875
- down_weight: bfloat16 [2816, 1024], P('shard'), may hold values from -0.109375 to 0.109375
- cotangent: bfloat16 [8, 4, 2048, 1024], P('shard', None, 'ctx'), may hold values from -6 to 6
Outputs:
- out_streams: bfloat16 [8, 4, 2048, 1024], P('shard', None, 'ctx')
- streams_grad: bfloat16 [8, 4, 2048, 1024], P('shard', None, 'ctx')
- qkv_grad: float32 [3, 1024, 1024], P(None, 'shard')
- out_grad: float32 [1024, 1024], P('shard')
- gate_up_grad: float32 [2, 1024, 2816], P(None, 'shard')
- down_grad: float32 [2816, 1024], P('shard')
- mix_grad: float32 [2, 4, 6], replicated
The draws below stay inside these ranges and needn't reach their ends.
Inputs may be any that keep to these rules, and one draw needn't show every extreme that they name: `segments`: each micro-batch holds documents 1, 2, 3 and 4 in this order, then padding 0 at its end; each document holds 102 to 1024 tokens, document 2 exactly 1024; padding holds 1 to 52 tokens.
All inputs are finite; a program needn't handle non-finite values.
Results may differ from the reference program's by a relative error of at most 0.03.
Values may be sent and summed in bfloat16 or wider, within the bound.
No kernel may reach another device: no remote copies, remote signals or barrier semaphores. Data moves between devices by JAX's collectives and lax.ppermute only.
A program may use at most 192 MiB of HBM per device.

```python
import jax
import jax.numpy as jnp
from jax import lax

D = 1024
HEADS = 16
HD = 64
FF = 2816
STREAMS = 4
GROUP = 2048
MICRO = 8


def draw_segments(key, part):
    key = jax.random.fold_in(key, 5)
    first_key, second_key, third_key = jax.random.split(key, 3)
    least = GROUP // 20
    start_long = jax.random.randint(first_key, (MICRO, 1), least, GROUP // 4 + 1)
    end_long = start_long + GROUP // 2
    padding = jax.random.randint(second_key, (MICRO, 1), 1, GROUP // 40 + 2)
    end_docs = GROUP - padding
    split_at = jax.random.randint(third_key, (MICRO, 1), end_long + least, end_docs - least + 1)
    place = jnp.arange(GROUP, dtype=jnp.int32)[None, :]
    result = jnp.where(place < end_docs, 4, 0)
    result = jnp.where(place < split_at, 3, result)
    result = jnp.where(place < end_long, 2, result)
    result = jnp.where(place < start_long, 1, result)
    return result.astype(jnp.int32)


def draw_stream_mix(key, part):
    key = jax.random.fold_in(key, 11)
    first_key, second_key, third_key, fourth_key = jax.random.split(key, 4)
    inputs = jax.random.uniform(first_key, (2, STREAMS, 1), jnp.float32, 0.3, 1.0)
    diagonal = jax.random.uniform(second_key, (2, STREAMS), jnp.float32, 0.6, 1.0)
    spread = jax.random.uniform(third_key, (2, STREAMS, STREAMS), jnp.float32, -0.3, 0.3)
    mixing = spread + diagonal[:, :, None] * jnp.eye(STREAMS, dtype=jnp.float32)[None]
    outputs = jax.random.uniform(fourth_key, (2, STREAMS, 1), jnp.float32, 0.5, 1.5)
    return jnp.concatenate([inputs, mixing, outputs], axis=2)


def block_scale(rng, extent, shards, smallest, high):
    level = 1.0
    for dim, shards_of in shards:
        steps = jax.random.uniform(jax.random.fold_in(jax.random.fold_in(rng, 6), dim), (shards_of,), jnp.float32, smallest / len(shards), high / len(shards))
        level = level * jnp.repeat(jnp.exp(steps), extent[dim] // shards_of).reshape((-1,) + (1,) * (len(extent) - 1 - dim))
    return level


def gaussian(rng, shape, scale, bound, pieces=(), kind=jnp.bfloat16):
    factor_of = block_scale(rng, shape, pieces, -0.22, 0.18) if pieces else 1.0
    values = jax.random.normal(rng, shape, jnp.float32) * scale * factor_of
    return jnp.minimum(jnp.maximum(values, -bound), bound).astype(kind)


def setup_inputs(seed: int = 0) -> dict:
    seeds = jax.random.split(jax.random.key(seed), 9)
    streams = gaussian(seeds[0], (MICRO, STREAMS, GROUP, D), 1.0, 6.0, ((0, 8), (2, 16)))
    segments = draw_segments(jax.random.fold_in(seeds[8], 71), 0)
    stream_mix = draw_stream_mix(jax.random.fold_in(seeds[8], 71), 0)
    qkv_weight = gaussian(seeds[3], (3, D, D), D ** -0.5, 0.1875, ((1, 8),))
    out_weight = gaussian(seeds[4], (D, D), 4 ** -0.5, 3.0, ((0, 8),))
    gate_up_weight = gaussian(seeds[5], (2, D, FF), D ** -0.5, 0.1875, ((1, 8),))
    down_weight = gaussian(seeds[6], (FF, D), FF ** -0.5, 0.109375, ((0, 8),))
    cotangent = gaussian(seeds[7], (MICRO, STREAMS, GROUP, D), 1.0, 6.0, ((0, 8), (2, 16)))
    return dict(streams=streams, segments=segments, stream_mix=stream_mix, qkv_weight=qkv_weight, out_weight=out_weight, gate_up_weight=gate_up_weight, down_weight=down_weight, cotangent=cotangent)


@jax.custom_vjp
def low(v):
    return lax.optimization_barrier(v.astype(jnp.bfloat16)).astype(jnp.float32)

@jax.custom_vjp
def low_back(v):
    return v

def low_keep(v):
    return (low(v), None)

def low_pass(kept, grad):
    return (grad,)

def back_keep(v):
    return (v, None)

def back_low(kept, grad):
    return (low(grad),)
low.defvjp(low_keep, low_pass)
low_back.defvjp(back_keep, back_low)
eps = 1e-05
rope_base = 1000000.0
neg_big = -1e+30
highest = lax.Precision.HIGHEST

def matmul(left, right):
    return jnp.dot(left, right, precision=highest)

def normalize(values):
    centered = values - lax.optimization_barrier(jnp.mean(values, axis=-1, keepdims=True))
    return centered * lax.rsqrt(lax.optimization_barrier(jnp.mean(centered * centered, axis=-1, keepdims=True)) + eps)

def tables(count):
    half = HD // 2
    freq = rope_base ** (-(jnp.arange(half, dtype=jnp.float32) * 2.0) / HD)
    angle = jnp.arange(count, dtype=jnp.float32)[:, None] * freq[None, :]
    angle = jnp.concatenate([angle, angle], axis=1)
    return (jnp.cos(angle)[:, None, :], jnp.sin(angle)[:, None, :])

def rotate(values, cosine, sine):
    half = values.shape[-1] // 2
    turned = jnp.concatenate([-values[..., half:], values[..., :half]], axis=-1)
    return values * cosine + turned * sine

def attend(query, key, value, seg):
    block = min(512, GROUP)
    count = GROUP // block
    scale = HD ** (-0.5)
    key_pos = jnp.arange(GROUP, dtype=jnp.int32)

    def one(index):
        start = index * block
        part = lax.dynamic_slice_in_dim(query, start, block, 0)
        part_seg = lax.dynamic_slice_in_dim(seg, start, block, 0)
        part_pos = start + jnp.arange(block, dtype=jnp.int32)
        raw = low_back(jnp.einsum('qhd,khd->hqk', part, key, precision=highest))
        allowed = (part_seg[:, None] == seg[None, :]) & (part_pos[:, None] >= key_pos[None, :])
        scores = jnp.where(allowed[None], raw * scale, neg_big)
        top = lax.optimization_barrier(jnp.max(scores, axis=-1, keepdims=True))
        weights = jnp.exp(scores - top)
        probs = low(weights / lax.optimization_barrier(jnp.sum(weights, axis=-1, keepdims=True)))
        return jnp.einsum('hqk,khd->qhd', probs, value, precision=highest).reshape(block, D)
    mixed = lax.map(jax.checkpoint(one), jnp.arange(count, dtype=jnp.int32))
    return mixed.reshape(GROUP, D)

def forward(hin, mix, qkv_w, out_w, gu_w, down_w, seg):
    live = (seg > 0).astype(jnp.float32)[:, None]
    cosine, sine = tables(GROUP)
    first = jnp.einsum('s,std->td', mix[0, :, 0], hin, precision=highest)
    normed1 = low(normalize(first))
    query = low(rotate(low_back(matmul(normed1, qkv_w[0])).reshape(GROUP, HEADS, HD), cosine, sine))
    key = low(rotate(low_back(matmul(normed1, qkv_w[1])).reshape(GROUP, HEADS, HD), cosine, sine))
    value = low(low_back(matmul(normed1, qkv_w[2]))).reshape(GROUP, HEADS, HD)
    context = low(low_back(attend(query, key, value, seg)))
    branch1 = low_back(live * matmul(context, out_w))
    mid = jnp.einsum('sr,rtd->std', mix[0, :, 1:STREAMS + 1], hin, precision=highest) + mix[0, :, STREAMS + 1][:, None, None] * branch1[None]
    second = jnp.einsum('s,std->td', mix[1, :, 0], mid, precision=highest)
    normed2 = low(normalize(second))
    gate = low_back(matmul(normed2, gu_w[0]))
    up = low_back(matmul(normed2, gu_w[1]))
    hidden = low(jax.nn.silu(gate) * up)
    branch2 = low_back(live * matmul(hidden, down_w))
    return jnp.einsum('sr,rtd->std', mix[1, :, 1:STREAMS + 1], mid, precision=highest) + mix[1, :, STREAMS + 1][:, None, None] * branch2[None]

def reference(streams, segments, stream_mix, qkv_weight, out_weight, gate_up_weight, down_weight, cotangent):
    weights = tuple((w.astype(jnp.float32) for w in (qkv_weight, out_weight, gate_up_weight, down_weight)))

    def step(totals, item):
        hin, seg, cot = item

        def run(values, mix, first_w, second_w, third_w, fourth_w):
            return forward(values, mix, first_w, second_w, third_w, fourth_w, seg)
        result, pull = jax.vjp(run, hin.astype(jnp.float32), stream_mix, *weights)
        grads = pull(cot.astype(jnp.float32))
        totals = tuple((t + g for t, g in zip(totals, grads[1:])))
        return (totals, (result.astype(jnp.bfloat16), grads[0].astype(jnp.bfloat16)))
    zeros = (jnp.zeros_like(stream_mix),) + tuple((jnp.zeros_like(w) for w in weights))
    totals, (outs, backs) = lax.scan(step, zeros, (streams, segments, cotangent))
    return (outs, backs, totals[1], totals[2], totals[3], totals[4], totals[0])
```

```python
import functools

import jax
import jax.numpy as jnp
import numpy as np
from jax import lax
from jax.experimental import pallas as pl
from jax.experimental.pallas import tpu as pltpu
from jax.sharding import Mesh
from jax.sharding import PartitionSpec as P

HEADS = 16
HD = 64
TILE = 256
eps = 1e-05
rope_base = 1000000.0
neg_big = -1e30
bf16 = jnp.bfloat16
f32 = jnp.float32

AXES = (("z", 4), ("xh", 2), ("co", 2), ("xl", 2), ("y", 4))
SIZE = dict(AXES)
CTX = ("z", "xh", "co")
SHARD = ("xl", "y")
TEAM = ("co", "z")


def shift(values, axis, amount):
    count = SIZE[axis]
    return lax.ppermute(values, axis, [(i, (i + amount) % count) for i in range(count)])


def swap_index(values):
    pairs = []
    for z in range(4):
        for core in range(2):
            for xl in range(2):
                for y in range(4):
                    here = ((z * 2 + core) * 2 + xl) * 4 + y
                    pairs.append((here, ((y * 2 + xl) * 2 + core) * 4 + z))
    return lax.ppermute(values, ("z", "co", "xl", "y"), pairs)


def team_gather(values):
    parts = [values] + [shift(values, "z", k) for k in range(1, 4)]
    own = jnp.stack(parts)
    other = shift(own, "co", 1)
    return jnp.stack([own, other], axis=1)


def team_scatter(partial):
    other = shift(partial[:, 1].astype(bf16), "co", 1)
    total = (partial[:, 0].astype(f32) + other.astype(f32)).astype(bf16)
    result = total[0].astype(f32)
    for k in range(1, 4):
        result = result + shift(total[k], "z", -k).astype(f32)
    return result


def normalize(values):
    centered = values - jnp.mean(values, axis=-1, keepdims=True)
    inverse = lax.rsqrt(jnp.mean(centered * centered, axis=-1, keepdims=True) + eps)
    return (centered * inverse, inverse)


def norm_back(grad, normed, inverse):
    return inverse * (
        grad
        - jnp.mean(grad, axis=-1, keepdims=True)
        - normed * jnp.mean(grad * normed, axis=-1, keepdims=True)
    )


def contract(left, right, dims):
    return lax.dot_general(left, right, (dims, ((), ())), preferred_element_type=f32)


def combine(weights, values):
    return jnp.sum(weights[:, None, None] * values, axis=0)


def remix(matrix, values):
    return jnp.sum(matrix[:, :, None, None] * values[None], axis=1)


def remix_back(matrix, grad):
    return jnp.sum(matrix[:, :, None, None] * grad[:, None], axis=0)


def pair_sums(left, right):
    return jnp.sum(left[:, None] * right[None], axis=(2, 3))


def tile_mask(scalars, k_tile, q_tile):
    core = scalars[2]
    local_k = lax.broadcasted_iota(jnp.int32, (TILE, 1), 0)
    local_q = lax.broadcasted_iota(jnp.int32, (1, TILE), 1)
    local_k = (local_k + core * 128) % TILE
    local_q = (local_q + core * 128) % TILE
    k_pos = local_k + k_tile * TILE
    q_pos = local_q + q_tile * TILE
    start = jnp.zeros_like(q_pos)
    for d in range(4):
        edge = scalars[3 + d]
        start = jnp.where(q_pos >= edge, edge, start)
    return (k_pos >= start) & (k_pos <= q_pos)


def first_tile(scalars, q_tile):
    place = q_tile * TILE
    start = jnp.int32(0)
    for d in range(4):
        edge = scalars[3 + d]
        start = jnp.where(place >= edge, edge, start)
    return start // TILE


def tile_place(scalars, tile):
    z, half = scalars[0], scalars[1]
    part = ((tile % 2) + half) % 2
    back = (z - tile // 2 + 4) % 4
    return part, pl.ds(pl.multiple_of(back * TILE, TILE), TILE)


def attend_kernel(scalars, qkv, context, context_wide, logsum):
    core = scalars[2]

    @pl.loop(0, 8)
    def _(q_tile):
        q_part, q_lanes = tile_place(scalars, q_tile)
        query = qkv[q_part, 0:HD, q_lanes]

        def step(k_tile, carry):
            top, total, mixed = carry
            k_part, k_lanes = tile_place(scalars, k_tile)
            key = qkv[k_part, HD : 2 * HD, k_lanes]
            value = qkv[k_part, 2 * HD : 3 * HD, k_lanes]
            raw = contract(key, query, ((0,), (0,)))
            raw = jnp.where(tile_mask(scalars, k_tile, q_tile), raw, neg_big)
            new_top = jnp.maximum(top, jnp.max(raw, axis=0, keepdims=True))
            weights = jnp.exp(raw - new_top)
            fade = jnp.exp(top - new_top)
            total = total * fade + jnp.sum(weights, axis=0, keepdims=True)
            mixed = mixed * fade + contract(value, weights.astype(bf16), ((1,), (0,)))
            return new_top, total, mixed

        init = (
            jnp.full((1, TILE), neg_big, f32),
            jnp.zeros((1, TILE), f32),
            jnp.zeros((HD, TILE), f32),
        )
        top, total, mixed = lax.fori_loop(first_tile(scalars, q_tile), q_tile + 1, step, init)
        mixed = mixed / total
        context_wide[q_part, :, q_lanes] = mixed
        logsum[q_part, :, q_lanes] = jnp.broadcast_to(top + jnp.log(total), (8, TILE))
        low = mixed.astype(bf16)
        context[q_tile * 2 + core] = low[:, :128]
        context[q_tile * 2 + 1 - core] = low[:, 128:]


def attend_back_kernel(
    scalars, qkv, context_wide, logsum, grad_context, cosine, sine, grads, dk_acc, dv_acc
):
    core = scalars[2]
    dk_acc[...] = jnp.zeros_like(dk_acc)
    dv_acc[...] = jnp.zeros_like(dv_acc)

    def turn_back(grad, part, lanes):
        cos, sin = cosine[part, :, lanes], sine[part, :, lanes]
        one, two = grad[:32], grad[32:]
        return jnp.concatenate([one * cos + two * sin, two * cos - one * sin], axis=0).astype(bf16)

    @pl.loop(0, 8)
    def _(q_tile):
        q_part, q_lanes = tile_place(scalars, q_tile)
        query = qkv[q_part, 0:HD, q_lanes]
        grad = jnp.concatenate(
            [grad_context[q_tile * 2 + core], grad_context[q_tile * 2 + 1 - core]], axis=1
        )
        delta = jnp.sum(
            grad.astype(f32) * context_wide[q_part, :, q_lanes], axis=0, keepdims=True
        )
        norm = logsum[q_part, 0:1, q_lanes]

        def step(k_tile, dq):
            k_part, k_lanes = tile_place(scalars, k_tile)
            key = qkv[k_part, HD : 2 * HD, k_lanes]
            value = qkv[k_part, 2 * HD : 3 * HD, k_lanes]
            raw = contract(key, query, ((0,), (0,)))
            raw = jnp.where(tile_mask(scalars, k_tile, q_tile), raw, neg_big)
            probs = jnp.exp(raw - norm)
            dprobs = contract(value, grad, ((0,), (0,)))
            draw = (probs * (dprobs - delta)).astype(bf16)
            dv_acc[k_tile] += contract(grad, probs.astype(bf16), ((1,), (1,)))
            dk_acc[k_tile] += contract(query, draw, ((1,), (1,)))
            return dq + contract(key, draw, ((1,), (0,)))

        dq = lax.fori_loop(
            first_tile(scalars, q_tile), q_tile + 1, step, jnp.zeros((HD, TILE), f32)
        )
        grads[q_part, 0:HD, q_lanes] = turn_back(dq * 0.125, q_part, q_lanes)

    @pl.loop(0, 8)
    def _(tile):
        part, lanes = tile_place(scalars, tile)
        grads[part, HD : 2 * HD, lanes] = turn_back(dk_acc[tile], part, lanes)
        grads[part, 2 * HD : 3 * HD, lanes] = dv_acc[tile].astype(bf16)


smem = pl.BlockSpec(memory_space=pltpu.SMEM)
vmem = pl.BlockSpec(memory_space=pltpu.VMEM)


def attend(scalars, qkv):
    return pl.pallas_call(
        attend_kernel,
        out_shape=(
            jax.ShapeDtypeStruct((16, HD, 128), bf16),
            jax.ShapeDtypeStruct((2, HD, 1024), f32),
            jax.ShapeDtypeStruct((2, 8, 1024), f32),
        ),
        in_specs=[smem, vmem],
        out_specs=(vmem, vmem, vmem),
        compiler_params=pltpu.CompilerParams(vmem_limit_bytes=32 * 1024 * 1024),
        cost_estimate=pl.CostEstimate(flops=10**9, bytes_accessed=10**7, transcendentals=10**6),
        name="attend",
    )(scalars, qkv)


def attend_back(scalars, qkv, context_wide, logsum, grad_context, cosine, sine):
    return pl.pallas_call(
        attend_back_kernel,
        out_shape=jax.ShapeDtypeStruct((2, 3 * HD, 1024), bf16),
        in_specs=[smem] + [vmem] * 6,
        out_specs=vmem,
        scratch_shapes=[pltpu.VMEM((8, HD, TILE), f32), pltpu.VMEM((8, HD, TILE), f32)],
        compiler_params=pltpu.CompilerParams(vmem_limit_bytes=32 * 1024 * 1024),
        cost_estimate=pl.CostEstimate(flops=3 * 10**9, bytes_accessed=10**7, transcendentals=10**6),
        name="attend_back",
    )(scalars, qkv, context_wide, logsum, grad_context, cosine, sine)


def turn(values, cosine, sine):
    one, two = values[:32], values[32:]
    return jnp.concatenate([one * cosine - two * sine, two * cosine + one * sine], axis=0)


def shards(
    streams, segments, stream_mix, qkv_weight, out_weight, gate_up_weight, down_weight, cotangent
):
    z, half, core = lax.axis_index("z"), lax.axis_index("xh"), lax.axis_index("co")
    team = lax.axis_index(TEAM)
    tokens, width = 128, 1024
    ff = down_weight.shape[0]
    hin = streams[0].astype(f32)
    seg = segments[0]
    live = (seg > 0).astype(f32)[:, None]
    first_mix, second_mix = stream_mix[0], stream_mix[1]
    p1, r1, g1 = first_mix[:, 0], first_mix[:, 1:5], first_mix[:, 5]
    p2, r2, g2 = second_mix[:, 0], second_mix[:, 1:5], second_mix[:, 5]

    counts = jnp.stack([jnp.sum((seg == d).astype(jnp.int32)) for d in range(1, 5)])
    counts = jnp.broadcast_to(counts[:, None], (4, 128))
    counts = counts + shift(counts, "co", 1)
    counts = counts + shift(counts, "xh", 1)
    counts = counts + shift(counts, "z", 1) + shift(counts, "z", 2) + shift(counts, "z", 3)
    edges = jnp.cumsum(counts[:, 0])
    scalars = jnp.concatenate([jnp.stack([z, half, core]), edges]).astype(jnp.int32)

    freq = rope_base ** (-(jnp.arange(32, dtype=f32) * 2.0) / HD)
    back, near, place = jnp.arange(4), jnp.arange(2), jnp.arange(128)
    positions = (
        512 * ((z - back[None, :, None, None] + 4) % 4)
        + 256 * ((half + near[:, None, None, None]) % 2)
        + 128 * ((core + near[None, None, :, None]) % 2)
        + place[None, None, None, :]
    ).reshape(2, 1, 1024)
    angle = positions.astype(f32) * freq[None, :, None]
    cosine, sine = jnp.cos(angle), jnp.sin(angle)

    qkv_cols = lax.dynamic_slice_in_dim(qkv_weight, team * 128, 128, 2)
    qkv_cols = qkv_cols.reshape(3, 128, 2, HD).transpose(2, 0, 3, 1).reshape(384, 128)
    qkv_all = lax.all_gather(qkv_cols, SHARD, axis=1, tiled=True)
    qkv_all = qkv_all.reshape(2, 192, width)
    kept = lax.dynamic_index_in_dim(qkv_all, half, 0, False)
    sent = lax.dynamic_index_in_dim(qkv_all, 1 - half, 0, False)
    qkv_pair = jnp.concatenate([kept, sent], axis=0)
    out_all = lax.all_gather(out_weight, SHARD, axis=0, tiled=True)
    gu_cols = lax.dynamic_slice_in_dim(gate_up_weight, team * (ff), ff, 2)
    gu_all = lax.all_gather(gu_cols, SHARD, axis=1, tiled=True)
    down_rows = swap_index(down_weight)

    first = combine(p1, hin)
    normed1, inverse1 = normalize(first)
    normed1_team = team_gather(normed1.astype(bf16)).reshape(1024, width)

    grad_out = cotangent[0].astype(f32)
    grad_branch2 = (live * combine(g2, grad_out)).astype(bf16)

    projected = contract(qkv_pair, normed1_team, ((1,), (1,)))

    def turned(block):
        return jnp.concatenate(
            [
                turn(block[:64], cosine[0], sine[0]).astype(bf16) * 0.125,
                turn(block[64:128], cosine[0], sine[0]).astype(bf16),
                block[128:].astype(bf16),
            ],
            axis=0,
        )

    own_part = turned(projected[:192])
    sent_part = turned(projected[192:])
    qkv = jnp.stack([own_part, shift(sent_part, "xh", 1)])
    context_blocks, context_wide, logsum = attend(scalars, qkv)
    context = lax.all_to_all(context_blocks, CTX, 0, 0, tiled=True)
    context = context.reshape(4, 2, 2, HD, tokens).transpose(2, 0, 1, 3, 4).reshape(width, tokens)

    branch1 = live * contract(context, out_all, ((0,), (0,)))
    mid = remix(r1, hin) + g1[:, None, None] * branch1[None]
    second = combine(p2, mid)
    normed2, inverse2 = normalize(second)
    normed2_team = team_gather(normed2.astype(bf16)).reshape(1024, width)
    grad_branch2_team = team_gather(grad_branch2).reshape(1024, width)

    gate = contract(normed2_team, gu_all[0], ((1,), (0,)))
    up = contract(normed2_team, gu_all[1], ((1,), (0,)))
    sigma = jax.nn.sigmoid(gate)
    silu = gate * sigma
    hidden = (silu * up).astype(bf16)
    grad_hidden = contract(grad_branch2_team, down_rows, ((1,), (1,)))
    grad_gate = (grad_hidden * up * sigma * (1.0 + gate * (1.0 - sigma))).astype(bf16)
    grad_up = (grad_hidden * silu).astype(bf16)
    grad_normed2 = contract(grad_gate, gu_all[0], ((1,), (1,))) + contract(
        grad_up, gu_all[1], ((1,), (1,))
    )
    grad_normed2 = team_scatter(grad_normed2.reshape(4, 2, tokens, width))
    branch2 = contract(hidden, down_rows, ((1,), (0,)))
    branch2 = live * team_scatter(branch2.reshape(4, 2, tokens, width))
    result = remix(r2, mid) + g2[:, None, None] * branch2[None]
    out_streams = result.astype(bf16)[None]
    grad_r2 = pair_sums(grad_out, mid)
    grad_g2 = jnp.sum(grad_out * branch2[None], axis=(1, 2))

    gu_tile = jnp.concatenate(
        [contract(normed2_team, grad_gate, ((0,), (0,))), contract(normed2_team, grad_up, ((0,), (0,)))],
        axis=1,
    ).astype(bf16)
    down_tile = contract(hidden, grad_branch2_team, ((0,), (0,))).astype(bf16)

    def finish_rows(tile):
        mine = lax.psum_scatter(tile, SHARD, scatter_dimension=0, tiled=True)
        mine = (mine.astype(f32) + shift(mine, "xh", 1).astype(f32)).astype(bf16)
        return lax.all_gather(mine, TEAM, axis=0)

    def finish_cols(tile):
        mine = lax.psum_scatter(tile, SHARD, scatter_dimension=1, tiled=True)
        mine = (mine.astype(f32) + shift(mine, "xh", 1).astype(f32)).astype(bf16)
        return lax.all_gather(swap_index(mine), TEAM, axis=1, tiled=True)

    gu_done = finish_rows(gu_tile)
    gate_up_grad = gu_done.reshape(8, 128, 2, ff).transpose(2, 1, 0, 3).reshape(2, 128, 8 * ff)
    gate_up_grad = gate_up_grad.astype(f32)

    grad_mid = remix_back(r2, grad_out)
    grad_second = norm_back(grad_normed2, normed2, inverse2)
    grad_p2 = jnp.sum(mid * grad_second[None], axis=(1, 2))
    grad_mid = grad_mid + p2[:, None, None] * grad_second[None]
    grad_r1 = pair_sums(grad_mid, hin)
    grad_g1 = jnp.sum(grad_mid * branch1[None], axis=(1, 2))
    grad_in = remix_back(r1, grad_mid)
    grad_branch1 = (live * combine(g1, grad_mid)).astype(bf16)
    grad_context = contract(out_all, grad_branch1, ((1,), (1,))).astype(bf16)
    grad_context = (
        grad_context.reshape(2, 4, 2, HD, tokens).transpose(1, 2, 0, 3, 4).reshape(16, HD, tokens)
    )
    grad_context = lax.all_to_all(grad_context, CTX, 0, 0, tiled=True)

    grads = attend_back(scalars, qkv, context_wide, logsum, grad_context, cosine, sine)
    grad_pair = jnp.concatenate([grads[0], shift(grads[1], "xh", 1)], axis=0)
    grad_normed1 = contract(grad_pair, qkv_pair, ((0,), (0,)))
    grad_normed1 = team_scatter(grad_normed1.reshape(4, 2, tokens, width))

    grad_branch1_team = team_gather(grad_branch1).reshape(1024, width)
    wide = context_wide.astype(bf16)
    other_head = shift(wide[1], "xh", 1)
    heads = jnp.where(
        half == 0,
        jnp.concatenate([wide[0], other_head], axis=0),
        jnp.concatenate([other_head, wide[0]], axis=0),
    )
    out_tile = contract(heads, grad_branch1_team, ((1,), (0,))).astype(bf16)
    rows = finish_cols(jnp.concatenate([down_tile, out_tile], axis=0)).astype(f32)
    down_grad, out_grad = rows[:ff], rows[ff:]

    qkv_tile = contract(normed1_team, grad_pair, ((0,), (1,)))
    kept_tile, sent_tile = qkv_tile[:, :192], qkv_tile[:, 192:]
    qkv_tile = jnp.where(
        half == 0,
        jnp.concatenate([kept_tile, sent_tile], axis=1),
        jnp.concatenate([sent_tile, kept_tile], axis=1),
    ).astype(bf16)
    qkv_done = finish_rows(qkv_tile)
    qkv_grad = qkv_done.reshape(8, 128, 2, 3, HD).transpose(3, 1, 0, 2, 4).reshape(3, 128, width)
    qkv_grad = qkv_grad.astype(f32)

    grad_first = norm_back(grad_normed1, normed1, inverse1)
    grad_p1 = jnp.sum(hin * grad_first[None], axis=(1, 2))
    grad_in = grad_in + p1[:, None, None] * grad_first[None]
    streams_grad = grad_in.astype(bf16)[None]
    first_grad = jnp.concatenate([grad_p1[:, None], grad_r1, grad_g1[:, None]], axis=1)
    second_grad = jnp.concatenate([grad_p2[:, None], grad_r2, grad_g2[:, None]], axis=1)
    mix = jnp.stack([first_grad, second_grad]).reshape(1, 48)
    mix = jnp.pad(mix, ((0, 0), (0, 80)))
    mix = mix + shift(mix, "co", 1)
    mix = mix + shift(mix, "xl", 1)
    mix = mix + shift(mix, "xh", 1)
    mix = (mix + shift(mix, "z", 2)) + (shift(mix, "z", 1) + shift(mix, "z", 3))
    mix = (mix + shift(mix, "y", 2)) + (shift(mix, "y", 1) + shift(mix, "y", 3))
    mix_grad = mix[0, :48].reshape(2, 4, 6)
    return (out_streams, streams_grad, qkv_grad, out_grad, gate_up_grad, down_grad, mix_grad)


def solution(mesh):
    fine = Mesh(
        np.asarray(mesh.devices).reshape([n for _, n in AXES]), tuple(name for name, _ in AXES)
    )
    in_specs = (
        P(SHARD, None, CTX, None),
        P(SHARD, CTX),
        P(),
        P(None, SHARD, None),
        P(SHARD, None),
        P(None, SHARD, None),
        P(SHARD, None),
        P(SHARD, None, CTX, None),
    )
    out_specs = (
        P(SHARD, None, CTX, None),
        P(SHARD, None, CTX, None),
        P(None, SHARD, None),
        P(SHARD, None),
        P(None, SHARD, None),
        P(SHARD, None),
        P(),
    )
    return jax.shard_map(shards, mesh=fine, in_specs=in_specs, out_specs=out_specs, check_vma=False)
```

```python
import jax
import jax.numpy as jnp
import numpy as np
from jax import lax
from jax.experimental import pallas as pl
from jax.experimental.pallas import tpu as pltpu
from jax.sharding import Mesh
from jax.sharding import PartitionSpec as P

HD = 64
TILE = 256
VMEM = 24 * 1024 * 1024
COST = 1.2e6
PIECE = 44
PLACE = 48
SLICE = 8 * PLACE
eps = 1e-05
rope_base = 1000000.0
neg_big = -1e30
bf16 = jnp.bfloat16
f32 = jnp.float32
smem = pl.BlockSpec(memory_space=pltpu.SMEM)
vmem = pl.BlockSpec(memory_space=pltpu.VMEM)
anywhere = pl.BlockSpec(memory_space=pl.ANY)
hbm = pl.BlockSpec(memory_space=pltpu.HBM)

AXES = (("z", 4), ("xh", 2), ("co", 2), ("xl", 2), ("y", 4))
SIZE = dict(AXES)
CTX = ("z", "xh", "co")
SHARD = ("xl", "y")
TEAM = ("co", "z")
HEAD_OF = [8 * (c % 2) + 2 * (c // 4) + (c // 2) % 2 for c in range(16)]


def shift(values, axis, amount):
    count = SIZE[axis]
    return lax.ppermute(values, axis, [(i, (i + amount) % count) for i in range(count)])


def z_issue(values):
    return [shift(values, "z", k) for k in range(1, 4)]


def call(kernel, outs, ins, name, us, scratch=(), order=()):
    ends = len(ins), len(ins) + len(order), len(ins) + len(order) + len(outs)
    near = [k for k, (_, place) in enumerate(ins) if place == "hbm"]
    far = [k for k, out in enumerate(outs) if len(out) > 2]

    def body(*refs):
        given, results, rest = list(refs[: ends[0]]), list(refs[ends[1] : ends[2]]), refs[ends[2] :]
        rest, sems = (rest[:-1], rest[-1]) if near or far else (rest, None)
        loaded = rest[len(scratch) : len(scratch) + len(near)]
        staged = rest[len(scratch) + len(near) :]
        copies = []
        for j, (k, ref) in enumerate(zip(near, loaded)):
            copies.append(pltpu.make_async_copy(given[k], ref, sems.at[j]))
            given[k] = ref
        for copy in copies:
            copy.start()
        for copy in copies:
            copy.wait()
        copies = []
        for j, (k, ref) in enumerate(zip(far, staged)):
            copies.append(pltpu.make_async_copy(ref, results[k], sems.at[len(near) + j]))
            results[k] = ref
        kernel(*given, *results, *rest[: len(scratch)])
        for copy in copies:
            copy.start()
        for copy in copies:
            copy.wait()

    extra = [pltpu.VMEM(ins[k][0].shape, ins[k][0].dtype) for k in near]
    extra += [pltpu.VMEM(outs[k][0], outs[k][1]) for k in far]
    if near or far:
        extra.append(pltpu.SemaphoreType.DMA((len(near) + len(far),)))

    def in_hbm(value):
        return pltpu.with_memory_space_constraint(value, pltpu.HBM)

    def out_type(out):
        if len(out) > 2:
            return pltpu.HBM(out[0], out[1])
        return jax.ShapeDtypeStruct(out[0], out[1])

    return pl.pallas_call(
        body,
        out_shape=tuple(out_type(out) for out in outs),
        in_specs=[hbm if place == "hbm" else place for _, place in ins] + [hbm] * len(order),
        out_specs=tuple(
            hbm if len(out) > 2 else smem if out[1] == jnp.int32 else vmem for out in outs
        ),
        scratch_shapes=list(scratch) + extra,
        compiler_params=pltpu.CompilerParams(vmem_limit_bytes=VMEM),
        cost_estimate=pl.CostEstimate(
            flops=0, bytes_accessed=int(us * COST), transcendentals=0
        ),
        name=name,
    )(*[in_hbm(value) if place == "hbm" else value for value, place in ins], *[in_hbm(x) for x in order])


def contract(left, right, dims):
    return lax.dot_general(left, right, (dims, ((), ())), preferred_element_type=f32)


def normalize(values):
    centered = values - jnp.mean(values, axis=-1, keepdims=True)
    inverse = lax.rsqrt(jnp.mean(centered * centered, axis=-1, keepdims=True) + eps)
    return (centered * inverse, inverse)


def norm_back(grad, normed, inverse):
    return inverse * (
        grad
        - jnp.mean(grad, axis=-1, keepdims=True)
        - normed * jnp.mean(grad * normed, axis=-1, keepdims=True)
    )


def weighted(terms):
    total = None
    for weight, values in terms:
        part = weight * values
        total = part if total is None else total + part
    return total


def live_column(segments):
    wide = jnp.broadcast_to((segments[...] > 0).astype(f32), (128, 128))
    return wide.T[:, 0:1]


class Mix:
    def __init__(self, ref):
        self.p = [[ref[m, s, 0] for s in range(4)] for m in range(2)]
        self.r = [[[ref[m, s, 1 + r] for r in range(4)] for s in range(4)] for m in range(2)]
        self.g = [[ref[m, s, 5] for s in range(4)] for m in range(2)]

    def second_of_streams(self, r):
        return sum(self.p[1][s] * self.r[0][s][r] for s in range(4))

    def second_of_branch(self):
        return sum(self.p[1][s] * self.g[0][s] for s in range(4))


def core_add_kernel(own, received, first, *rest):
    first[...] = own[0].astype(f32) + received[0].astype(f32)
    for k, target in enumerate(rest, 1):
        target[...] = (own[k].astype(f32) + received[k].astype(f32)).astype(bf16)


def first_norm_kernel(mix_ref, streams, segments, out):
    mix = Mix(mix_ref)
    for c in range(4):
        rows = slice(32 * c, 32 * c + 32)
        first = weighted([(mix.p[0][s], streams[s, rows].astype(f32)) for s in range(4)])
        out[rows] = normalize(first)[0].astype(bf16)
    out[128:144] = jnp.zeros((16, 1024), bf16)
    out[128:144, 0:128] = jnp.broadcast_to(segments[...].astype(f32), (16, 128)).astype(bf16)


def pick_heads_kernel(_, weights, out):
    for s in range(8):
        out[s] = weights[...]


def pick_heads(team, weights):
    return pl.pallas_call(
        pick_heads_kernel,
        grid_spec=pltpu.PrefetchScalarGridSpec(
            num_scalar_prefetch=1,
            grid=(1,),
            in_specs=[pl.BlockSpec((3, 128, 128), lambda _, team: (0, 0, team[0]))],
            out_specs=pl.BlockSpec((8, 3, 128, 128), lambda _, team: (0, 0, 0, 0)),
        ),
        out_shape=pltpu.HBM((8, 3, 128, 128), bf16),
        compiler_params=pltpu.CompilerParams(vmem_limit_bytes=VMEM),
        cost_estimate=pl.CostEstimate(flops=0, bytes_accessed=int(COST), transcendentals=0),
        name="pick_heads",
    )(team, pltpu.with_memory_space_constraint(weights, pltpu.HBM))


def pieces(d):
    start, place, result = PLACE * d, 0, []
    while place < PLACE:
        count = min(PLACE - place, 128 - start % 128)
        result.append((place, start // 128, start % 128, count))
        start, place = start + count, place + count
    return result


def pick_rows_kernel(places, out_weight, down, wide):
    team, core = places[4], places[2]
    own, _ = halves(core)
    wide[:, 0:512] = out_weight[:, own]
    place = lax.broadcasted_iota(jnp.int32, (PLACE, 8 * PIECE), 0)
    unit = lax.broadcasted_iota(jnp.int32, (PLACE, 8 * PIECE), 1)
    picked = jnp.where((unit == team * PIECE + place) & (place < PIECE), 1.0, 0.0).astype(bf16)
    rows = contract(picked, down[...], ((1,), (0,))).astype(bf16)
    for d in range(8):
        for place, tile, start, count in pieces(d):
            lanes = slice(512 + 128 * tile, 512 + 128 * tile + 128)
            wide[start : start + count, lanes] = rows[
                place : place + count, 128 * d : 128 * d + 128
            ]


def pick_columns_kernel(places, gate_up, wide):
    team = places[4]
    units = gate_up.shape[2]
    unit = lax.broadcasted_iota(jnp.int32, (units, SLICE), 0)
    place = lax.broadcasted_iota(jnp.int32, (units, SLICE), 1)
    piece = lax.rem(place, PLACE)
    wanted = (place // PLACE) * (8 * PIECE) + team * PIECE + piece
    picked = jnp.where((unit == wanted) & (piece < PIECE), 1.0, 0.0).astype(bf16)
    for j in range(2):
        columns = contract(gate_up[j], picked, ((1,), (0,)))
        wide[:, SLICE * j : SLICE * j + SLICE] = columns.astype(bf16)


def unpack_rows_kernel(rows, out_half, down):
    out_half[...] = rows[:, 0:512]
    for s in range(8):
        for d in range(8):
            for place, tile, start, count in pieces(d):
                lanes = slice(512 + 128 * tile, 512 + 128 * tile + 128)
                down[
                    PLACE * s + place : PLACE * s + place + count, 128 * d : 128 * d + 128
                ] = rows[128 * s + start : 128 * s + start + count, lanes]


def grad_branch2_kernel(mix_ref, cotangent, segments, out):
    mix = Mix(mix_ref)
    live = live_column(segments)
    for c in range(4):
        rows = slice(32 * c, 32 * c + 32)
        total = weighted([(mix.g[1][s], cotangent[s, rows].astype(f32)) for s in range(4)])
        out[rows] = (live[rows] * total).astype(bf16)


def turn(values, cosine, sine):
    one, two = values[:32], values[32:]
    return jnp.concatenate([one * cosine - two * sine, two * cosine + one * sine], axis=0)


def turn_back(grad, cosine, sine):
    one, two = grad[:32], grad[32:]
    return jnp.concatenate([one * cosine + two * sine, two * cosine - one * sine], axis=0)


def turn_heads_kernel(weights, out):
    for s in range(8):
        for j in range(3):
            out[128 * j : 128 * j + 128, 128 * s : 128 * s + 128] = weights[s, j].T


def stack_kernel(first, second, third, fourth, out):
    for k, part in enumerate((first, second, third, fourth)):
        out[k] = part[...]


def project_kernel(places, own, other, wide, cosine, sine, kept, sent):
    half = places[1]

    def rows(head):
        return [wide[pl.ds(pl.multiple_of(128 * j + HD * head, HD), HD), :] for j in range(3)]

    mine = jnp.concatenate(rows(half) + rows(1 - half), axis=0)
    for near, tokens in enumerate((own, other)):
        blocks = contract(mine, tokens[:, 0:128].reshape(512, 1024), ((1,), (1,)))
        for back in range(4):
            lanes = slice(back * TILE + near * 128, back * TILE + near * 128 + 128)
            block = blocks[:, 128 * back : 128 * back + 128]
            segs = tokens[back, 128:144, 0:128]
            cos, sin = cosine[0, :, lanes], sine[0, :, lanes]
            for target, base in ((kept, 0), (sent, 192)):
                query = turn(block[base : base + 64], cos, sin).astype(bf16)
                target[0:64, lanes] = (query.astype(f32) * 0.125).astype(bf16)
                target[64:128, lanes] = turn(block[base + 64 : base + 128], cos, sin).astype(bf16)
                target[128:192, lanes] = block[base + 128 : base + 192].astype(bf16)
                target[192:208, lanes] = segs


def tile_mask(core, edges, k_tile, q_tile):
    local_k = lax.broadcasted_iota(jnp.int32, (TILE, 1), 0)
    local_q = lax.broadcasted_iota(jnp.int32, (1, TILE), 1)
    k_pos = (local_k + core * 128) % TILE + k_tile * TILE
    q_pos = (local_q + core * 128) % TILE + q_tile * TILE
    start = jnp.zeros_like(q_pos)
    for edge in edges:
        start = jnp.where(q_pos >= edge, edge, start)
    return (k_pos >= start) & (k_pos <= q_pos)


def first_tile(edges, q_tile):
    place = q_tile * TILE
    start = jnp.int32(0)
    for edge in edges:
        start = jnp.where(place >= edge, edge, start)
    return start // TILE


def tile_place(places, tile):
    part = lax.rem(lax.rem(tile, 2) + places[1], 2)
    back = lax.rem(places[0] - tile // 2 + 4, 4)
    return part, pl.ds(pl.multiple_of(back * TILE, TILE), TILE)


def attend_kernel(places, kept, received, qkv, context, context_wide, logsum, edges_out):
    core = places[2]
    qkv[0] = kept[0:192]
    qkv[1] = received[0:192]
    seg_own = kept[192:208].astype(f32)
    seg_far = received[192:208].astype(f32)
    edges = []
    for d in range(1, 5):
        count = jnp.float32(0)
        for seg in (seg_own, seg_far):
            inside = (seg > 0.5) & (seg < d + 0.5)
            count = count + jnp.sum(jnp.where(inside, 0.0625, 0.0))
        edge = count.astype(jnp.int32)
        edges_out[d - 1] = edge
        edges.append(edge)

    @pl.loop(0, 8)
    def _(q_tile):
        q_part, q_lanes = tile_place(places, q_tile)
        query = qkv[q_part, 0:HD, q_lanes]

        def step(k_tile, carry):
            top, total, mixed = carry
            k_part, k_lanes = tile_place(places, k_tile)
            key = qkv[k_part, HD : 2 * HD, k_lanes]
            value = qkv[k_part, 2 * HD : 3 * HD, k_lanes]
            raw = contract(key, query, ((0,), (0,)))
            raw = jnp.where(tile_mask(core, edges, k_tile, q_tile), raw, neg_big)
            new_top = jnp.maximum(top, jnp.max(raw, axis=0, keepdims=True))
            weights = jnp.exp(raw - new_top)
            fade = jnp.exp(top - new_top)
            total = total * fade + jnp.sum(weights, axis=0, keepdims=True)
            mixed = mixed * fade + contract(value, weights.astype(bf16), ((1,), (0,)))
            return new_top, total, mixed

        init = (
            jnp.full((1, TILE), neg_big, f32),
            jnp.zeros((1, TILE), f32),
            jnp.zeros((HD, TILE), f32),
        )
        top, total, mixed = lax.fori_loop(first_tile(edges, q_tile), q_tile + 1, step, init)
        mixed = mixed / total
        context_wide[q_part, :, q_lanes] = mixed
        logsum[q_part, :, q_lanes] = jnp.broadcast_to(top + jnp.log(total), (8, TILE))
        low = mixed.astype(bf16)
        context[q_tile * 2 + core] = low[:, :128]
        context[q_tile * 2 + 1 - core] = low[:, 128:]


def attend_back_kernel(
    places, edge_ref, qkv, context_wide, logsum, grad_context, cosine, sine, columns,
    grads_own, grads_far, columns_out, dk_acc, dv_acc, grads,
):
    core = places[2]
    columns_out[...] = columns[...]
    edges = [edge_ref[d] for d in range(4)]
    dk_acc[...] = jnp.zeros_like(dk_acc)
    dv_acc[...] = jnp.zeros_like(dv_acc)

    def put(tile, rows, values):
        part, lanes = tile_place(places, tile)
        grads[part, rows, lanes] = values.astype(bf16)

    @pl.loop(0, 8)
    def _(q_tile):
        q_part, q_lanes = tile_place(places, q_tile)
        query = qkv[q_part, 0:HD, q_lanes]
        grad = jnp.concatenate(
            [grad_context[q_tile * 2 + core], grad_context[q_tile * 2 + 1 - core]], axis=1
        )
        delta = jnp.sum(
            grad.astype(f32) * context_wide[q_part, :, q_lanes], axis=0, keepdims=True
        )
        norm = logsum[q_part, 0:1, q_lanes]

        def step(k_tile, dq):
            k_part, k_lanes = tile_place(places, k_tile)
            key = qkv[k_part, HD : 2 * HD, k_lanes]
            value = qkv[k_part, 2 * HD : 3 * HD, k_lanes]
            raw = contract(key, query, ((0,), (0,)))
            raw = jnp.where(tile_mask(core, edges, k_tile, q_tile), raw, neg_big)
            probs = jnp.exp(raw - norm)
            dprobs = contract(value, grad, ((0,), (0,)))
            draw = (probs * (dprobs - delta)).astype(bf16)
            dv_acc[k_tile] += contract(grad, probs.astype(bf16), ((1,), (1,)))
            dk_acc[k_tile] += contract(query, draw, ((1,), (1,)))
            return dq + contract(key, draw, ((1,), (0,)))

        dq = lax.fori_loop(
            first_tile(edges, q_tile), q_tile + 1, step, jnp.zeros((HD, TILE), f32)
        )
        cos, sin = cosine[q_part, :, q_lanes], sine[q_part, :, q_lanes]
        put(q_tile, slice(0, HD), turn_back(dq * 0.125, cos, sin))

    @pl.loop(0, 8)
    def _(tile):
        part, lanes = tile_place(places, tile)
        cos, sin = cosine[part, :, lanes], sine[part, :, lanes]
        put(tile, slice(HD, 2 * HD), turn_back(dk_acc[tile], cos, sin))
        put(tile, slice(2 * HD, 3 * HD), dv_acc[tile])

    grads_own[...] = grads[0]
    grads_far[...] = grads[1]


def halves(core):
    own = pl.ds(pl.multiple_of(core * 512, 512), 512)
    other = pl.ds(pl.multiple_of((1 - core) * 512, 512), 512)
    return own, other


def post_attend_kernel(
    places, mix_ref, blocks, out_own, out_other, streams, segments, normed2, branch1, context
):
    mix = Mix(mix_ref)
    live = live_column(segments)
    for c in range(16):
        context[HD * HEAD_OF[c] : HD * HEAD_OF[c] + HD] = blocks[c]
    turned = context[...]
    own, other = halves(places[2])
    branch1[:, own] = live * contract(turned, out_own[...], ((0,), (0,)))
    branch1[:, other] = live * contract(turned, out_other[...], ((0,), (0,)))
    of_streams = [mix.second_of_streams(r) for r in range(4)]
    of_branch = mix.second_of_branch()
    for c in range(4):
        rows = slice(32 * c, 32 * c + 32)
        second = weighted(
            [(of_streams[r], streams[r, rows].astype(f32)) for r in range(4)]
            + [(of_branch, branch1[rows])]
        )
        normed2[rows] = normalize(second)[0].astype(bf16)


def feed_forward_kernel(normed, grad_branch, weights, down, grad_normed, hidden, grad_gate, grad_up):
    for c in range(2):
        rows = slice(256 * c, 256 * c + 256)
        tokens = normed[2 * c : 2 * c + 2].reshape(256, 1024)
        grad = contract(grad_branch[2 * c : 2 * c + 2].reshape(256, 1024), down[...], ((1,), (1,)))
        gate = contract(tokens, weights[:, 0:SLICE], ((1,), (0,)))
        up = contract(tokens, weights[:, SLICE : 2 * SLICE], ((1,), (0,)))
        sigma = jax.nn.sigmoid(gate)
        silu = gate * sigma
        hidden[rows] = (silu * up).astype(bf16)
        grad_of_gate = (grad * up * sigma * (1.0 + gate * (1.0 - sigma))).astype(bf16)
        grad_of_up = (grad * silu).astype(bf16)
        grad_gate[rows] = grad_of_gate
        grad_up[rows] = grad_of_up
        total = contract(grad_of_gate, weights[:, 0:SLICE], ((1,), (1,)))
        total = total + contract(grad_of_up, weights[:, SLICE : 2 * SLICE], ((1,), (1,)))
        grad_normed[2 * c : 2 * c + 2] = total.astype(bf16).reshape(2, 128, 1024)


def branch2_kernel(hidden_own, hidden_other, down, own, other):
    own[...] = contract(hidden_own[...], down[...], ((1,), (0,))).astype(bf16).reshape(4, 128, 1024)
    other[...] = (
        contract(hidden_other[...], down[...], ((1,), (0,))).astype(bf16).reshape(4, 128, 1024)
    )


def wide_tiles_kernel(
    normed_own, normed_other, grad_own, grad_other,
    gate_own, gate_other, up_own, up_other, hidden_own, hidden_other, out,
):
    normed = [normed_own[...].reshape(512, 1024), normed_other[...].reshape(512, 1024)]
    grads = [grad_own[...].reshape(512, 1024), grad_other[...].reshape(512, 1024)]
    for j, (left_own, left_other) in enumerate([(gate_own, gate_other), (up_own, up_other)]):
        tile = contract(left_own[...], normed[0], ((0,), (0,)))
        tile = tile + contract(left_other[...], normed[1], ((0,), (0,)))
        for s in range(8):
            out[s, SLICE * j : SLICE * j + SLICE] = tile[:, 128 * s : 128 * s + 128].astype(bf16)
    tile = contract(hidden_own[...], grads[0], ((0,), (0,)))
    tile = tile + contract(hidden_other[...], grads[1], ((0,), (0,)))
    tile = tile.astype(bf16)
    for s in range(8):
        rows = tile[PLACE * s : PLACE * s + PLACE]
        for d in range(8):
            start = 2 * SLICE + PLACE * d
            out[s, start : start + PLACE] = rows[:, 128 * d : 128 * d + 128]


def second_back_kernel(
    places, mix_ref, t0, t1, t2, t3, streams, cotangent, branch1, segments, out_own, out_other,
    context, grad_second, grad_columns, grad_context, context_out, low,
):
    context_out[...] = context[...]
    mix = Mix(mix_ref)
    live = live_column(segments)
    of_streams = [mix.second_of_streams(r) for r in range(4)]
    of_branch = mix.second_of_branch()
    of_grad = [sum(mix.g[0][s] * mix.r[1][q][s] for s in range(4)) for q in range(4)]
    for c in range(4):
        rows = slice(32 * c, 32 * c + 32)
        second = weighted(
            [(of_streams[r], streams[r, rows].astype(f32)) for r in range(4)]
            + [(of_branch, branch1[rows])]
        )
        normed, inverse = normalize(second)
        grad = (t0[rows] + t1[rows].astype(f32)) + (t2[rows].astype(f32) + t3[rows].astype(f32))
        back = norm_back(grad, normed, inverse)
        grad_second[rows] = back
        branch = weighted(
            [(of_grad[q], cotangent[q, rows].astype(f32)) for q in range(4)] + [(of_branch, back)]
        )
        low[rows] = (live[rows] * branch).astype(bf16)
    own, other = halves(places[2])
    total = contract(out_own[...], low[:, own], ((1,), (1,)))
    total = total + contract(out_other[...], low[:, other], ((1,), (1,)))
    for c in range(16):
        grad_context[c] = total[HD * HEAD_OF[c] : HD * HEAD_OF[c] + HD].astype(bf16)
    for i in range(8):
        grad_columns[2 * (i % 4) + i // 4] = low[:, 128 * i : 128 * i + 128]


def mix_sums_kernel(mix_ref, streams, cotangent, branch1, grad_second, out, acc):
    mix = Mix(mix_ref)
    acc[...] = jnp.zeros_like(acc)

    def fold(values):
        return sum(values[:8, 128 * j : 128 * j + 128] for j in range(2)) + sum(
            values[8:, 128 * j : 128 * j + 128] for j in range(2)
        )

    @pl.loop(0, 8)
    def _(r):
        rows = pl.ds(pl.multiple_of(r * 16, 16), 16)

        @pl.loop(0, 4)
        def _(l):
            lanes = pl.ds(pl.multiple_of(l * 256, 256), 256)
            hin = [streams[s, rows, lanes].astype(f32) for s in range(4)]
            top = [cotangent[s, rows, lanes].astype(f32) for s in range(4)]
            branch, back = branch1[rows, lanes], grad_second[rows, lanes]
            mid = [
                weighted([(mix.r[0][s][q], hin[q]) for q in range(4)] + [(mix.g[0][s], branch)])
                for s in range(4)
            ]
            grad = [
                weighted([(mix.r[1][q][s], top[q]) for q in range(4)] + [(mix.p[1][s], back)])
                for s in range(4)
            ]
            for s in range(4):
                for q in range(4):
                    acc[s * 6 + 1 + q] += fold(grad[s] * hin[q])
                    acc[24 + s * 6 + 1 + q] += fold(top[s] * mid[q])
                acc[s * 6 + 5] += fold(grad[s] * branch)
                acc[24 + s * 6] += fold(mid[s] * back)

    out[...] = jnp.sum(acc[...], axis=1)


def out_streams_kernel(
    mix_ref, t0, t1, t2, t3, streams, cotangent, branch1, segments, out, sums
):
    mix = Mix(mix_ref)
    live = live_column(segments)
    acc = [jnp.zeros((1, 1024), f32) for _ in range(4)]
    for c in range(4):
        rows = slice(32 * c, 32 * c + 32)
        branch2 = live[rows] * (
            (t0[rows] + t1[rows].astype(f32)) + (t2[rows].astype(f32) + t3[rows].astype(f32))
        )
        hin = [streams[s, rows].astype(f32) for s in range(4)]
        branch = branch1[rows]
        mid = [
            weighted([(mix.r[0][s][q], hin[q]) for q in range(4)] + [(mix.g[0][s], branch)])
            for s in range(4)
        ]
        for s in range(4):
            total = weighted(
                [(mix.r[1][s][q], mid[q]) for q in range(4)] + [(mix.g[1][s], branch2)]
            )
            out[s, rows] = total.astype(bf16)
            acc[s] = acc[s] + jnp.sum(
                cotangent[s, rows].astype(f32) * branch2, axis=0, keepdims=True
            )
    for s in range(4):
        sums[s : s + 1] = sum(acc[s][:, 128 * j : 128 * j + 128] for j in range(8))


def near_lanes(values, near):
    return jnp.concatenate(
        [values[:, TILE * k + 128 * near : TILE * k + 128 * near + 128] for k in range(4)], axis=1
    )


def pair_back_kernel(places, own, far, weights, grad_own, grad_other, pair):
    half = places[1]
    for j in range(3):
        rows = slice(HD * j, HD * j + HD)
        pair[pl.ds(pl.multiple_of(128 * j + HD * half, HD), HD), :] = own[rows]
        pair[pl.ds(pl.multiple_of(128 * j + HD * (1 - half), HD), HD), :] = far[rows]
    for near, target in ((1, grad_other), (0, grad_own)):
        total = contract(near_lanes(pair, near), weights[...], ((0,), (0,)))
        target[...] = total.astype(bf16).reshape(4, 128, 1024)


def narrow_tiles_kernel(
    places, pair, normed_own, normed_other, columns, context_own, context_other, out
):
    z, core = places[0], places[2]
    tile = jnp.zeros((384, 1024), f32)
    for near, tokens in enumerate((normed_own, normed_other)):
        tokens = tokens[:, 0:128].reshape(512, 1024)
        tile = tile + contract(near_lanes(pair, near), tokens, ((1,), (0,)))
    for s in range(8):
        out[s, 0:384] = tile[:, 128 * s : 128 * s + 128].astype(bf16)
    tile = jnp.zeros((128, 1024), f32)
    for back in range(4):
        for near in range(2):
            source = columns[2 * lax.rem(z - back + 4, 4) + lax.rem(core + near, 2)]
            context = (context_own if near == 0 else context_other)[back]
            tile = tile + contract(source, context, ((0,), (1,)))
    for s in range(8):
        out[s, 384:512] = tile[:, 128 * s : 128 * s + 128].astype(bf16)


def fold_kernel(blocks, *outs):
    start = 0
    for out in outs:
        rows = slice(start, start + out.shape[0])
        total = blocks[0, rows].astype(f32)
        for s in range(1, 8):
            total = total + blocks[s, rows].astype(f32)
        out[...] = total.astype(bf16)
        start += out.shape[0]


def member(places, own, other, index):
    back = lax.rem(places[0] - index % 4 + 4, 4)
    return jnp.where(places[2] == index // 4, own[back].astype(f32), other[back].astype(f32))


def finish_wide_kernel(places, own, other, gate_up, down, rows):
    for i in range(8):
        block = member(places, own, other, i)
        for s in range(8):
            for j in range(2):
                start = SLICE * j + PLACE * s
                unit = 8 * PIECE * s + PIECE * i
                rows[j, unit : unit + PIECE] = block[start : start + PIECE]
        for d in range(8):
            start = 2 * SLICE + PLACE * d
            down[PIECE * i : PIECE * i + PIECE, 128 * d : 128 * d + 128] = block[
                start : start + PIECE
            ]
    for j in range(2):
        for k in range(rows.shape[1] // 128):
            lanes = slice(128 * k, 128 * k + 128)
            gate_up[j, :, lanes] = rows[j, lanes].T


def finish_narrow_kernel(places, own, other, qkv, out):
    for i in range(8):
        block = member(places, own, other, i)
        for j in range(3):
            qkv[j, :, 128 * i : 128 * i + 128] = block[128 * j : 128 * j + 128].T
        out[:, 128 * i : 128 * i + 128] = block[384:].T


def first_back_kernel(
    mix_ref, t0, t1, t2, t3, streams, cotangent, grad_second, sums, branch_sums, streams_grad, mix_rows
):
    mix = Mix(mix_ref)
    of_top = [
        [sum(mix.r[1][q][s] * mix.r[0][s][r] for s in range(4)) for q in range(4)]
        for r in range(4)
    ]
    of_back = [sum(mix.r[0][s][r] * mix.p[1][s] for s in range(4)) for r in range(4)]
    total = [jnp.zeros((1, 1024), f32) for _ in range(4)]
    for c in range(4):
        rows = slice(32 * c, 32 * c + 32)
        hin = [streams[s, rows].astype(f32) for s in range(4)]
        top = [cotangent[s, rows].astype(f32) for s in range(4)]
        normed, inverse = normalize(weighted([(mix.p[0][s], hin[s]) for s in range(4)]))
        grad = (t0[rows] + t1[rows].astype(f32)) + (t2[rows].astype(f32) + t3[rows].astype(f32))
        back1 = norm_back(grad, normed, inverse)
        back2 = grad_second[rows]
        for r in range(4):
            value = weighted(
                [(of_top[r][q], top[q]) for q in range(4)]
                + [(of_back[r], back2), (mix.p[0][r], back1)]
            )
            streams_grad[r, rows] = value.astype(bf16)
            total[r] = total[r] + jnp.sum(hin[r] * back1, axis=0, keepdims=True)
    mix_rows[...] = sums[...]
    for s in range(4):
        row = sum(total[s][:, 128 * k : 128 * k + 128] for k in range(8))
        mix_rows[s * 6 : s * 6 + 1] = row
        mix_rows[24 + s * 6 + 5 : 24 + s * 6 + 6] = branch_sums[s : s + 1]


def shards(
    streams, segments, stream_mix, qkv_weight, out_weight, gate_up_weight, down_weight, cotangent
):
    z, half, core = lax.axis_index("z"), lax.axis_index("xh"), lax.axis_index("co")
    team, row = lax.axis_index(TEAM), lax.axis_index(SHARD)
    width = streams.shape[3]
    ff = down_weight.shape[0]
    places = (jnp.stack([z, half, core, row, team]).astype(jnp.int32), smem)
    mix = (stream_mix, smem)
    streams, cotangent, segments = (streams[0], "hbm"), (cotangent[0], "hbm"), (segments, vmem)
    token = ((128, width), bf16)
    token4 = ((4, 128, width), bf16)

    def v(*values):
        return [(value, vmem) for value in values]

    def h(*values):
        return [(value, "hbm") for value in values]

    def stack(values, parts, name, order=()):
        shape = (4,) + values.shape
        (result,) = call(
            stack_kernel, [(shape, bf16, "hbm")], v(values, *parts), name, 1, order=order
        )
        return result

    qkv_blocks = pick_heads(team.astype(jnp.int32)[None], qkv_weight)
    (normed1,) = call(
        first_norm_kernel,
        [((144, width), bf16, "hbm")],
        [mix, streams, segments],
        "first_norm",
        1.5,
        order=[qkv_blocks],
    )
    qkv_blocks = lax.all_to_all(qkv_blocks, SHARD, 0, 0, tiled=True)
    (row_weights,) = call(
        pick_rows_kernel,
        [((128, 896), bf16, "hbm")],
        [places] + h(out_weight, down_weight),
        "pick_rows",
        1.5,
        order=[normed1],
    )
    pick_rows = row_weights
    row_weights = lax.all_gather(row_weights, SHARD, axis=0, tiled=True)
    normed1_z = z_issue(normed1)
    (gu_weights,) = call(
        pick_columns_kernel,
        [((128, 2 * SLICE), bf16, "hbm")],
        [places] + h(gate_up_weight),
        "pick_columns",
        3,
        order=[pick_rows],
    )
    gu_all = lax.all_gather(gu_weights, SHARD, axis=0, tiled=True)

    freq = rope_base ** (-(jnp.arange(32, dtype=f32) * 2.0) / HD)
    back, near, place = jnp.arange(4), jnp.arange(2), jnp.arange(128)
    positions = (
        512 * ((z - back[None, :, None, None] + 4) % 4)
        + 256 * ((half + near[:, None, None, None]) % 2)
        + 128 * ((core + near[None, None, :, None]) % 2)
        + place[None, None, None, :]
    ).reshape(2, 1, 1024)
    angle = positions.astype(f32) * freq[None, :, None]
    cosine, sine = jnp.cos(angle), jnp.sin(angle)

    normed1_own = stack(normed1, normed1_z, "stack_normed1")
    normed1_other = shift(normed1_own, "co", 1)
    (pair_weights,) = call(
        turn_heads_kernel, [((384, width), bf16, "hbm")], v(qkv_blocks), "turn_heads", 1
    )
    kept, sent = call(
        project_kernel,
        [((208, 1024), bf16, "hbm"), ((208, 1024), bf16, "hbm")],
        [places] + h(normed1_own, normed1_other, pair_weights) + v(cosine, sine),
        "project",
        4,
        order=[gu_weights],
    )
    received = shift(sent, "xh", 1)
    (grad_branch2,) = call(
        grad_branch2_kernel,
        [token + ("hbm",)],
        [mix, cotangent, segments],
        "grad_branch2",
        1.5,
        order=[kept],
    )
    grad2_z = z_issue(grad_branch2)

    qkv, context_blocks, context_wide, logsum, edges = call(
        attend_kernel,
        [
            ((2, 192, 1024), bf16, "hbm"),
            ((16, HD, 128), bf16, "hbm"),
            ((2, HD, 1024), f32, "hbm"),
            ((2, 8, 1024), f32, "hbm"),
            ((4,), jnp.int32),
        ],
        [places] + h(kept) + v(received),
        "attend",
        12,
        order=[grad_branch2],
    )
    context_mine = lax.all_to_all(context_blocks, CTX, 0, 0, tiled=True)
    out_own, down = call(
        unpack_rows_kernel,
        [((width, 512), bf16, "hbm"), ((SLICE, width), bf16, "hbm")],
        h(row_weights),
        "unpack_rows",
        1.5,
        order=[context_blocks],
    )
    out_other = shift(out_own, "co", 1)
    grad2_own = stack(grad_branch2, grad2_z, "stack_grad2", [out_own])
    grad2_other = shift(grad2_own, "co", 1)

    normed2, branch1, context = call(
        post_attend_kernel,
        [token, ((128, width), f32, "hbm"), ((width, 128), bf16, "hbm")],
        [places, mix] + v(context_mine) + h(out_own, out_other) + [streams, segments],
        "post_attend",
        3,
        order=[grad2_own],
    )
    normed2_own = stack(normed2, z_issue(normed2), "stack_normed2")
    normed2_other = shift(normed2_own, "co", 1)
    acts = [token4] + [((512, SLICE), bf16, "hbm")] * 3
    grad_own, hidden_own, gate_own, up_own = call(
        feed_forward_kernel,
        acts,
        h(normed2_own, grad2_own, gu_all, down),
        "feed_forward_own",
        5,
    )
    grad_other, hidden_other, gate_other, up_other = call(
        feed_forward_kernel,
        acts,
        h(normed2_other, grad2_other, gu_all, down),
        "feed_forward_other",
        5,
        order=[hidden_own],
    )

    def core_add(own, other, name, order):
        return call(
            core_add_kernel,
            [((128, width), f32, "hbm")] + [token] * 3,
            v(own, shift(other, "co", 1)),
            name,
            1,
            order=order,
        )

    def z_terms(terms):
        return [terms[0]] + [shift(term, "z", -k) for k, term in enumerate(terms[1:], 1)]

    half_own, half_other = call(
        branch2_kernel,
        [token4 + ("hbm",), token4 + ("hbm",)],
        h(hidden_own, hidden_other, down),
        "branch2",
        2,
        order=[hidden_other],
    )
    terms = core_add(grad_own, grad_other, "core_add_second", [half_own])
    grad_normed2 = z_terms(terms)

    (wide_tiles,) = call(
        wide_tiles_kernel,
        [((8, 3 * SLICE, 128), bf16, "hbm")],
        h(
            normed2_own, normed2_other, grad2_own, grad2_other,
            gate_own, gate_other, up_own, up_other, hidden_own, hidden_other,
        ),
        "wide_tiles",
        6,
        order=[terms[0]],
    )
    wide_mine = lax.psum_scatter(wide_tiles, SHARD, scatter_dimension=0, tiled=True)[0]
    grad_second, grad_columns, grad_context, context = call(
        second_back_kernel,
        [
            ((128, width), f32, "hbm"),
            ((8, 128, 128), bf16, "hbm"),
            ((16, HD, 128), bf16, "hbm"),
            ((width, 128), bf16, "hbm"),
        ],
        [places, mix]
        + h(grad_normed2[0])
        + v(*grad_normed2[1:])
        + [streams, cotangent]
        + h(branch1)
        + [segments]
        + h(out_own, out_other, context),
        "second_back",
        4,
        [pltpu.VMEM((128, width), bf16)],
        [wide_tiles],
    )
    grad_context = lax.all_to_all(grad_context, CTX, 0, 0, tiled=True)
    context_z = z_issue(context)
    (sums,) = call(
        mix_sums_kernel,
        [((48, 128), f32, "hbm")],
        [mix, streams, cotangent] + h(branch1, grad_second),
        "mix_sums",
        5,
        [pltpu.VMEM((48, 8, 128), f32)],
    )

    grads_own, grads_far, columns = call(
        attend_back_kernel,
        [((192, 1024), bf16, "hbm"), ((192, 1024), bf16, "hbm"), ((8, 128, 128), bf16, "hbm")],
        [places, (edges, smem)]
        + h(qkv, context_wide, logsum)
        + v(grad_context, cosine, sine)
        + h(grad_columns),
        "attend_back",
        12,
        [
            pltpu.VMEM((8, HD, TILE), f32),
            pltpu.VMEM((8, HD, TILE), f32),
            pltpu.VMEM((2, 192, 1024), bf16),
        ],
        [sums],
    )
    received = shift(grads_far, "xh", 1)
    columns = lax.all_to_all(columns, ("z", "co"), 0, 0, tiled=True)
    terms = core_add(half_own, half_other, "core_add_branch2", [grads_own])
    branch2 = z_terms(terms)
    context_own = stack(context, context_z, "stack_context", [terms[0]])
    context_other = shift(context_own, "co", 1)

    grad_own, grad_other, pair = call(
        pair_back_kernel,
        [token4, token4 + ("hbm",), ((384, 1024), bf16, "hbm")],
        [places] + h(grads_own) + v(received) + h(pair_weights),
        "pair_back",
        3,
        order=[context_own],
    )
    terms = core_add(grad_own, grad_other, "core_add_first", [])
    grad_normed1 = z_terms(terms)

    (narrow_tiles,) = call(
        narrow_tiles_kernel,
        [((8, 512, 128), bf16, "hbm")],
        [places]
        + h(pair, normed1_own, normed1_other)
        + v(columns)
        + h(context_own, context_other),
        "narrow_tiles",
        4,
        order=[terms[0]],
    )
    narrow_order = narrow_tiles
    narrow_tiles = lax.all_to_all(narrow_tiles, SHARD, 0, 0, tiled=True)
    out_streams, branch_sums = call(
        out_streams_kernel,
        [token4 + ("hbm",), ((4, 128), f32, "hbm")],
        [mix]
        + h(branch2[0])
        + v(*branch2[1:])
        + [streams, cotangent]
        + h(branch1)
        + [segments],
        "out_streams",
        4,
        order=[narrow_order],
    )
    streams_grad, rows = call(
        first_back_kernel,
        [token4 + ("hbm",), ((48, 128), f32)],
        [mix]
        + h(grad_normed1[0])
        + v(*grad_normed1[1:])
        + [streams, cotangent]
        + h(grad_second, sums, branch_sums),
        "first_back",
        4,
    )
    wide_rows = (wide_mine.astype(f32) + shift(wide_mine, "xh", 1).astype(f32)).astype(bf16)
    wide_own = stack(wide_rows, z_issue(wide_rows), "stack_wide")
    wide_other = shift(wide_own, "co", 1)
    (mine,) = call(
        fold_kernel,
        [((512, 128), bf16, "hbm")],
        v(narrow_tiles),
        "fold_narrow",
        1,
        order=[streams_grad],
    )
    narrow_rows = (mine.astype(f32) + shift(mine, "xh", 1).astype(f32)).astype(bf16)
    narrow_own = stack(narrow_rows, z_issue(narrow_rows), "stack_narrow")
    narrow_other = shift(narrow_own, "co", 1)

    rows = rows + shift(rows, "co", 1)
    near, far = shift(rows, "xl", 1), shift(rows, "xh", 1)
    cross = lax.ppermute(rows, ("xh", "xl"), [(0, 3), (1, 2), (2, 1), (3, 0)])
    rows = (rows + near) + (far + cross)
    rows = (rows + shift(rows, "z", 2)) + (shift(rows, "z", 1) + shift(rows, "z", 3))
    rows = (rows + shift(rows, "y", 2)) + (shift(rows, "y", 1) + shift(rows, "y", 3))
    mix_grad = jnp.sum(rows, axis=1).reshape(2, 4, 6)

    gate_up_grad, down_grad = call(
        finish_wide_kernel,
        [((2, 128, 8 * ff), f32, "hbm"), ((ff, width), f32, "hbm")],
        [places] + h(wide_own, wide_other),
        "finish_wide",
        4,
        [pltpu.VMEM((2, 8 * ff, 128), f32)],
        [mine],
    )
    qkv_grad, out_grad = call(
        finish_narrow_kernel,
        [((3, 128, width), f32, "hbm"), ((128, width), f32, "hbm")],
        [places] + h(narrow_own, narrow_other),
        "finish_narrow",
        3,
    )
    return (
        out_streams[None], streams_grad[None], qkv_grad, out_grad, gate_up_grad, down_grad, mix_grad,
    )


def solution(mesh):
    fine = Mesh(
        np.asarray(mesh.devices).reshape([n for _, n in AXES]), tuple(name for name, _ in AXES)
    )
    in_specs = (
        P(SHARD, None, CTX, None),
        P(SHARD, CTX),
        P(),
        P(None, SHARD, None),
        P(SHARD, None),
        P(None, SHARD, None),
        P(SHARD, None),
        P(SHARD, None, CTX, None),
    )
    out_specs = (
        P(SHARD, None, CTX, None),
        P(SHARD, None, CTX, None),
        P(None, SHARD, None),
        P(SHARD, None),
        P(None, SHARD, None),
        P(SHARD, None),
        P(),
    )
    return jax.shard_map(shards, mesh=fine, in_specs=in_specs, out_specs=out_specs, check_vma=False)
```

```python
import jax
import jax.numpy as jnp
import numpy as np
from jax import lax
from jax.experimental import pallas as pl
from jax.experimental.pallas import tpu as pltpu
from jax.sharding import Mesh
from jax.sharding import PartitionSpec as P

HD = 64
TILE = 256
VMEM = 24 * 1024 * 1024
COST = 1.1e9
PIECE = 44
PLACE = 48
SLICE = 8 * PLACE
eps = 1e-05
rope_base = 1000000.0
neg_big = -1e30
bf16 = jnp.bfloat16
f32 = jnp.float32
smem = pl.BlockSpec(memory_space=pltpu.SMEM)
vmem = pl.BlockSpec(memory_space=pltpu.VMEM)
anywhere = pl.BlockSpec(memory_space=pl.ANY)
hbm = pl.BlockSpec(memory_space=pltpu.HBM)

AXES = (("z", 4), ("xh", 2), ("co", 2), ("xl", 2), ("y", 4))
SIZE = dict(AXES)
CTX = ("z", "xh", "co")
SHARD = ("xl", "y")
TEAM = ("co", "z")
HEAD_OF = [8 * (c % 2) + 2 * (c // 4) + (c // 2) % 2 for c in range(16)]


def shift(values, axis, amount):
    count = SIZE[axis]
    return lax.ppermute(values, axis, [(i, (i + amount) % count) for i in range(count)])


def z_issue(values):
    return [shift(values, "z", k) for k in range(1, 4)]


class Late:
    def __init__(self, copy, ref):
        self.copy, self.ref = copy, ref

    def wait(self):
        self.copy.wait()
        return self.ref


def call(kernel, outs, ins, name, us, scratch=(), order=(), beside=()):
    known = (smem, vmem)
    extra_ins = len(order) + len(beside)
    ends = len(ins), len(ins) + extra_ins, len(ins) + extra_ins + len(outs)
    near = [k for k, (_, place) in enumerate(ins) if place not in known]
    far = [k for k, out in enumerate(outs) if len(out) > 2]

    def part(k):
        value, place = ins[k]
        if isinstance(place, tuple):
            return value.shape[:-1] + (place[2] - place[1],)
        return value.shape

    def body(*refs):
        given, results, rest = list(refs[: ends[0]]), list(refs[ends[1] : ends[2]]), refs[ends[2] :]
        rest, sems = (rest[:-1], rest[-1]) if near or far else (rest, None)
        loaded = rest[len(scratch) : len(scratch) + len(near)]
        staged = rest[len(scratch) + len(near) :]
        copies, waits = [], []
        for j, (k, ref) in enumerate(zip(near, loaded)):
            source, place = given[k], ins[k][1]
            if isinstance(place, tuple):
                source = source.at[..., place[1] : place[2]]
            copies.append(pltpu.make_async_copy(source, ref, sems.at[j]))
            if (place[0] if isinstance(place, tuple) else place) == "hbm":
                waits.append(copies[-1])
                given[k] = ref
            else:
                given[k] = Late(copies[-1], ref)
        for copy in copies:
            copy.start()
        for copy in waits:
            copy.wait()
        copies = []
        for j, (k, ref) in enumerate(zip(far, staged)):
            copies.append(pltpu.make_async_copy(ref, results[k], sems.at[len(near) + j]))
            results[k] = ref
        kernel(*given, *results, *rest[: len(scratch)])
        for copy in copies:
            copy.start()
        for copy in copies:
            copy.wait()

    extra = [pltpu.VMEM(part(k), ins[k][0].dtype) for k in near]
    extra += [pltpu.VMEM(outs[k][0], outs[k][1]) for k in far]
    if near or far:
        extra.append(pltpu.SemaphoreType.DMA((len(near) + len(far),)))

    def in_hbm(value):
        return pltpu.with_memory_space_constraint(value, pltpu.HBM)

    def out_type(out):
        if len(out) > 2:
            return pltpu.HBM(out[0], out[1])
        return jax.ShapeDtypeStruct(out[0], out[1])

    return pl.pallas_call(
        body,
        out_shape=tuple(out_type(out) for out in outs),
        in_specs=[place if place in known else hbm for _, place in ins]
        + [hbm] * len(order)
        + [anywhere] * len(beside),
        out_specs=tuple(
            hbm if len(out) > 2 else smem if out[1] == jnp.int32 else vmem for out in outs
        ),
        scratch_shapes=list(scratch) + extra,
        compiler_params=pltpu.CompilerParams(vmem_limit_bytes=VMEM),
        cost_estimate=pl.CostEstimate(
            flops=int(us * COST), bytes_accessed=0, transcendentals=0
        ),
        name=name,
    )(
        *[value if place in known else in_hbm(value) for value, place in ins],
        *[in_hbm(value) for value in order],
        *beside,
    )


def contract(left, right, dims):
    return lax.dot_general(left, right, (dims, ((), ())), preferred_element_type=f32)


def normalize(values):
    centered = values - jnp.mean(values, axis=-1, keepdims=True)
    inverse = lax.rsqrt(jnp.mean(centered * centered, axis=-1, keepdims=True) + eps)
    return (centered * inverse, inverse)


def norm_back(grad, normed, inverse):
    return inverse * (
        grad
        - jnp.mean(grad, axis=-1, keepdims=True)
        - normed * jnp.mean(grad * normed, axis=-1, keepdims=True)
    )


def weighted(terms):
    total = None
    for weight, values in terms:
        part = weight * values
        total = part if total is None else total + part
    return total


def live_column(segments):
    wide = jnp.broadcast_to((segments[...] > 0).astype(f32), (128, 128))
    return wide.T[:, 0:1]


class Mix:
    def __init__(self, ref):
        self.p = [[ref[m, s, 0] for s in range(4)] for m in range(2)]
        self.r = [[[ref[m, s, 1 + r] for r in range(4)] for s in range(4)] for m in range(2)]
        self.g = [[ref[m, s, 5] for s in range(4)] for m in range(2)]

    def second_of_streams(self, r):
        return sum(self.p[1][s] * self.r[0][s][r] for s in range(4))

    def second_of_branch(self):
        return sum(self.p[1][s] * self.g[0][s] for s in range(4))


def core_add_kernel(own, received, first, *rest):
    first[...] = own[0].astype(f32) + received[0].astype(f32)
    for k, target in enumerate(rest, 1):
        target[...] = (own[k].astype(f32) + received[k].astype(f32)).astype(bf16)


def first_norm_kernel(mix_ref, streams, segments, out):
    mix = Mix(mix_ref)
    for c in range(4):
        rows = slice(32 * c, 32 * c + 32)
        first = weighted([(mix.p[0][s], streams[s, rows].astype(f32)) for s in range(4)])
        out[rows] = normalize(first)[0].astype(bf16)
    out[128:144] = jnp.zeros((16, 1024), bf16)
    out[128:144, 0:128] = jnp.broadcast_to(segments[...].astype(f32), (16, 128)).astype(bf16)


def pick_heads_kernel(_, weights, out):
    for s in range(8):
        out[s] = weights[...]


def pick_heads(team, weights):
    return pl.pallas_call(
        pick_heads_kernel,
        grid_spec=pltpu.PrefetchScalarGridSpec(
            num_scalar_prefetch=1,
            grid=(1,),
            in_specs=[pl.BlockSpec((3, 128, 128), lambda _, team: (0, 0, team[0]))],
            out_specs=pl.BlockSpec((8, 3, 128, 128), lambda _, team: (0, 0, 0, 0)),
        ),
        out_shape=pltpu.HBM((8, 3, 128, 128), bf16),
        compiler_params=pltpu.CompilerParams(vmem_limit_bytes=VMEM),
        cost_estimate=pl.CostEstimate(flops=int(COST), bytes_accessed=0, transcendentals=0),
        name="pick_heads",
    )(team, pltpu.with_memory_space_constraint(weights, pltpu.HBM))


def pieces(d):
    start, place, result = PLACE * d, 0, []
    while place < PLACE:
        count = min(PLACE - place, 128 - start % 128)
        result.append((place, start // 128, start % 128, count))
        start, place = start + count, place + count
    return result


def pick_kernel(places, out_weight, down, gate_up, wide):
    team = places[4]
    wide[:, 0:1024] = out_weight.wait()[...]
    place = lax.broadcasted_iota(jnp.int32, (PLACE, 8 * PIECE), 0)
    unit = lax.broadcasted_iota(jnp.int32, (PLACE, 8 * PIECE), 1)
    picked = jnp.where((unit == team * PIECE + place) & (place < PIECE), 1.0, 0.0).astype(bf16)
    rows = contract(picked, down.wait()[...], ((1,), (0,))).astype(bf16)
    for d in range(8):
        for place, tile, start, count in pieces(d):
            lanes = slice(1024 + 128 * tile, 1024 + 128 * tile + 128)
            wide[start : start + count, lanes] = rows[
                place : place + count, 128 * d : 128 * d + 128
            ]
    gate_up = gate_up.wait()
    units = gate_up.shape[2]
    unit = lax.broadcasted_iota(jnp.int32, (units, SLICE), 0)
    place = lax.broadcasted_iota(jnp.int32, (units, SLICE), 1)
    piece = lax.rem(place, PLACE)
    wanted = (place // PLACE) * (8 * PIECE) + team * PIECE + piece
    picked = jnp.where((unit == wanted) & (piece < PIECE), 1.0, 0.0).astype(bf16)
    columns = contract(gate_up[...].reshape(256, units), picked, ((1,), (0,))).astype(bf16)
    for j in range(2):
        wide[:, 1408 + SLICE * j : 1408 + SLICE * j + SLICE] = columns[128 * j : 128 * j + 128]


def weight_row(places, s):
    return pl.multiple_of((s % 4) * 256 + lax.rem(s // 4 + places[3] // 4, 2) * 128, 128)


def pair_kernel(own, other, rows, columns):
    for k, source in enumerate((own, other)):
        rows[k] = source[:, 0:1408]
        columns[k] = source[:, 1408:]


def unpack_kernel(places, rows, columns, gate_up, down):
    for s in range(8):
        gate_up[128 * s : 128 * s + 128] = columns[pl.ds(weight_row(places, s), 128)]
        block = rows[pl.ds(weight_row(places, s), 128)]
        for d in range(8):
            for place, tile, start, count in pieces(d):
                down[
                    PLACE * s + place : PLACE * s + place + count, 128 * d : 128 * d + 128
                ] = block[start : start + count, 128 * tile : 128 * tile + 128]


def grad_branch2_kernel(mix_ref, cotangent, segments, out):
    mix = Mix(mix_ref)
    live = live_column(segments)
    for c in range(4):
        rows = slice(32 * c, 32 * c + 32)
        total = weighted([(mix.g[1][s], cotangent[s, rows].astype(f32)) for s in range(4)])
        out[rows] = (live[rows] * total).astype(bf16)


def turn(values, cosine, sine):
    one, two = values[:32], values[32:]
    return jnp.concatenate([one * cosine - two * sine, two * cosine + one * sine], axis=0)


def turn_back(grad, cosine, sine):
    one, two = grad[:32], grad[32:]
    return jnp.concatenate([one * cosine + two * sine, two * cosine - one * sine], axis=0)


def turn_heads_kernel(weights, out):
    for s in range(8):
        for j in range(3):
            out[128 * j : 128 * j + 128, 128 * s : 128 * s + 128] = weights[s, j].T


def stack_kernel(first, second, third, fourth, out):
    for k, part in enumerate((first, second, third, fourth)):
        out[k] = part[...]


def project_kernel(places, own, other, wide, cosine, sine, kept, sent):
    half = places[1]

    def rows(head):
        return [wide[pl.ds(pl.multiple_of(128 * j + HD * head, HD), HD), :] for j in range(3)]

    mine = jnp.concatenate(rows(half) + rows(1 - half), axis=0)
    for near, tokens in enumerate((own, other)):
        blocks = contract(mine, tokens[:, 0:128].reshape(512, 1024), ((1,), (1,)))
        for back in range(4):
            lanes = slice(back * TILE + near * 128, back * TILE + near * 128 + 128)
            block = blocks[:, 128 * back : 128 * back + 128]
            segs = tokens[back, 128:144, 0:128]
            cos, sin = cosine[0, :, lanes], sine[0, :, lanes]
            for target, base in ((kept, 0), (sent, 192)):
                query = turn(block[base : base + 64], cos, sin).astype(bf16)
                target[0:64, lanes] = (query.astype(f32) * 0.125).astype(bf16)
                target[64:128, lanes] = turn(block[base + 64 : base + 128], cos, sin).astype(bf16)
                target[128:192, lanes] = block[base + 128 : base + 192].astype(bf16)
                target[192:208, lanes] = segs


def tile_mask(core, edges, k_tile, q_tile):
    local_k = lax.broadcasted_iota(jnp.int32, (TILE, 1), 0)
    local_q = lax.broadcasted_iota(jnp.int32, (1, TILE), 1)
    k_pos = (local_k + core * 128) % TILE + k_tile * TILE
    q_pos = (local_q + core * 128) % TILE + q_tile * TILE
    start = jnp.zeros_like(q_pos)
    for edge in edges:
        start = jnp.where(q_pos >= edge, edge, start)
    return (k_pos >= start) & (k_pos <= q_pos)


def first_tile(edges, q_tile):
    place = q_tile * TILE
    start = jnp.int32(0)
    for edge in edges:
        start = jnp.where(place >= edge, edge, start)
    return start // TILE


def tile_place(places, tile):
    part = lax.rem(lax.rem(tile, 2) + places[1], 2)
    back = lax.rem(places[0] - tile // 2 + 4, 4)
    return part, pl.ds(pl.multiple_of(back * TILE, TILE), TILE)


def attend_kernel(places, kept, received, qkv, context, context_wide, logsum, edges_out):
    core = places[2]
    qkv[0] = kept[0:192]
    qkv[1] = received[0:192]
    seg_own = kept[192:208].astype(f32)
    seg_far = received[192:208].astype(f32)
    edges = []
    for d in range(1, 5):
        count = jnp.float32(0)
        for seg in (seg_own, seg_far):
            inside = (seg > 0.5) & (seg < d + 0.5)
            count = count + jnp.sum(jnp.where(inside, 0.0625, 0.0))
        edge = count.astype(jnp.int32)
        edges_out[d - 1] = edge
        edges.append(edge)

    @pl.loop(0, 8)
    def _(q_tile):
        q_part, q_lanes = tile_place(places, q_tile)
        query = qkv[q_part, 0:HD, q_lanes]

        def load(k_tile):
            k_part, k_lanes = tile_place(places, jnp.maximum(k_tile, 0))
            key = qkv[k_part, HD : 2 * HD, k_lanes]
            raw = contract(key, query, ((0,), (0,)))
            raw = jnp.where(tile_mask(core, edges, k_tile, q_tile), raw, neg_big)
            return raw, qkv[k_part, 2 * HD : 3 * HD, k_lanes]

        def step(pair, carry):
            top, total, mixed = carry
            raw1, value1 = load(q_tile - 2 * pair)
            raw2, value2 = load(q_tile - 2 * pair - 1)
            new_top = jnp.maximum(
                top,
                jnp.maximum(
                    jnp.max(raw1, axis=0, keepdims=True), jnp.max(raw2, axis=0, keepdims=True)
                ),
            )
            weights1, weights2 = jnp.exp(raw1 - new_top), jnp.exp(raw2 - new_top)
            fade = jnp.exp(top - new_top)
            total = total * fade + (
                jnp.sum(weights1, axis=0, keepdims=True) + jnp.sum(weights2, axis=0, keepdims=True)
            )
            mixed = mixed * fade + (
                contract(value1, weights1.astype(bf16), ((1,), (0,)))
                + contract(value2, weights2.astype(bf16), ((1,), (0,)))
            )
            return new_top, total, mixed

        init = (
            jnp.full((1, TILE), neg_big, f32),
            jnp.zeros((1, TILE), f32),
            jnp.zeros((HD, TILE), f32),
        )
        top, total, mixed = lax.fori_loop(0, (q_tile - first_tile(edges, q_tile)) // 2 + 1, step, init)
        mixed = mixed / total
        context_wide[q_part, :, q_lanes] = mixed
        logsum[q_part, :, q_lanes] = jnp.broadcast_to(top + jnp.log(total), (8, TILE))
        low = mixed.astype(bf16)
        context[q_tile * 2 + core] = low[:, :128]
        context[q_tile * 2 + 1 - core] = low[:, 128:]


def attend_back_kernel(
    places, edge_ref, qkv, context_wide, logsum, grad_context, cosine, sine, columns,
    grads_own, grads_far, columns_out, dk_acc, dv_acc, grads,
):
    core = places[2]
    columns_out[...] = columns[...]
    edges = [edge_ref[d] for d in range(4)]
    dk_acc[...] = jnp.zeros_like(dk_acc)
    dv_acc[...] = jnp.zeros_like(dv_acc)

    def put(tile, rows, values):
        part, lanes = tile_place(places, tile)
        grads[part, rows, lanes] = values.astype(bf16)

    @pl.loop(0, 8)
    def _(q_tile):
        q_part, q_lanes = tile_place(places, q_tile)
        query = qkv[q_part, 0:HD, q_lanes]
        grad = jnp.concatenate(
            [grad_context[q_tile * 2 + core], grad_context[q_tile * 2 + 1 - core]], axis=1
        )
        delta = jnp.sum(
            grad.astype(f32) * context_wide[q_part, :, q_lanes], axis=0, keepdims=True
        )
        norm = logsum[q_part, 0:1, q_lanes]

        def part(k_tile):
            place = jnp.maximum(k_tile, 0)
            k_part, k_lanes = tile_place(places, place)
            key = qkv[k_part, HD : 2 * HD, k_lanes]
            value = qkv[k_part, 2 * HD : 3 * HD, k_lanes]
            raw = contract(key, query, ((0,), (0,)))
            dprobs = contract(value, grad, ((0,), (0,)))
            raw = jnp.where(tile_mask(core, edges, k_tile, q_tile), raw, neg_big)
            probs = jnp.exp(raw - norm)
            draw = (probs * (dprobs - delta)).astype(bf16)
            return place, key, probs.astype(bf16), draw

        def step(pair, dq):
            for place, key, probs, draw in [
                part(q_tile - 2 * pair),
                part(q_tile - 2 * pair - 1),
            ]:
                dv_acc[place] += contract(grad, probs, ((1,), (1,)))
                dk_acc[place] += contract(query, draw, ((1,), (1,)))
                dq = dq + contract(key, draw, ((1,), (0,)))
            return dq

        dq = lax.fori_loop(
            0, (q_tile - first_tile(edges, q_tile)) // 2 + 1, step, jnp.zeros((HD, TILE), f32)
        )
        cos, sin = cosine[q_part, :, q_lanes], sine[q_part, :, q_lanes]
        put(q_tile, slice(0, HD), turn_back(dq * 0.125, cos, sin))

    @pl.loop(0, 8)
    def _(tile):
        part, lanes = tile_place(places, tile)
        cos, sin = cosine[part, :, lanes], sine[part, :, lanes]
        put(tile, slice(HD, 2 * HD), turn_back(dk_acc[tile], cos, sin))
        put(tile, slice(2 * HD, 3 * HD), dv_acc[tile])

    grads_own[...] = grads[0]
    grads_far[...] = grads[1]


def post_attend_kernel(
    places, mix_ref, blocks, out_weight, streams, segments, normed2, branch1, context, turned
):
    mix = Mix(mix_ref)
    live = live_column(segments)
    for c in range(16):
        context[HD * HEAD_OF[c] : HD * HEAD_OF[c] + HD] = blocks[c]
        row = weight_row(places, HEAD_OF[c] // 2) + HD * (HEAD_OF[c] % 2)
        turned[pl.ds(pl.multiple_of(row, HD), HD), :] = blocks[c]
    out_weight, streams = out_weight.wait(), streams.wait()
    branch1[...] = live * contract(turned[...], out_weight[...], ((0,), (0,)))
    of_streams = [mix.second_of_streams(r) for r in range(4)]
    of_branch = mix.second_of_branch()
    for c in range(4):
        rows = slice(32 * c, 32 * c + 32)
        second = weighted(
            [(of_streams[r], streams[r, rows].astype(f32)) for r in range(4)]
            + [(of_branch, branch1[rows])]
        )
        normed2[rows] = normalize(second)[0].astype(bf16)


def feed_forward_kernel(normed, grad_branch, weights, down, grad_normed, hidden, grad_gate, grad_up):
    for c in range(2):
        rows = slice(256 * c, 256 * c + 256)
        tokens = normed[2 * c : 2 * c + 2].reshape(256, 1024)
        grad = contract(grad_branch[2 * c : 2 * c + 2].reshape(256, 1024), down[...], ((1,), (1,)))
        gate = contract(tokens, weights[:, 0:SLICE], ((1,), (0,)))
        up = contract(tokens, weights[:, SLICE : 2 * SLICE], ((1,), (0,)))
        sigma = jax.nn.sigmoid(gate)
        silu = gate * sigma
        hidden[rows] = (silu * up).astype(bf16)
        grad_of_gate = (grad * up * sigma * (1.0 + gate * (1.0 - sigma))).astype(bf16)
        grad_of_up = (grad * silu).astype(bf16)
        grad_gate[rows] = grad_of_gate
        grad_up[rows] = grad_of_up
        total = contract(grad_of_gate, weights[:, 0:SLICE], ((1,), (1,)))
        total = total + contract(grad_of_up, weights[:, SLICE : 2 * SLICE], ((1,), (1,)))
        grad_normed[2 * c : 2 * c + 2] = total.astype(bf16).reshape(2, 128, 1024)


def branch2_kernel(hidden_own, hidden_other, down, context, own, other, context_out):
    context_out[...] = context[...]
    own[...] = contract(hidden_own[...], down[...], ((1,), (0,))).astype(bf16).reshape(4, 128, 1024)
    other[...] = (
        contract(hidden_other[...], down[...], ((1,), (0,))).astype(bf16).reshape(4, 128, 1024)
    )


def wide_tiles_kernel(
    places, gate_own, normed_own, gate_other, normed_other, up_own, up_other,
    hidden_own, grad_own, hidden_other, grad_other, out,
):
    def tile_of(left_own, right_own, left_other, right_other):
        tile = contract(left_own.wait()[...], right_own().reshape(512, 1024), ((0,), (0,)))
        return tile + contract(
            left_other.wait()[...], right_other().reshape(512, 1024), ((0,), (0,))
        )

    def slot(s):
        return 2 * (s % 4) + lax.rem(s // 4 + places[3] // 4, 2)

    first = tile_of(
        gate_own, lambda: normed_own.wait()[...], gate_other, lambda: normed_other.wait()[...]
    )
    second = tile_of(
        up_own, lambda: normed_own.ref[...], up_other, lambda: normed_other.ref[...]
    )
    for j, tile in enumerate((first, second)):
        for s in range(8):
            out[slot(s), SLICE * j : SLICE * j + SLICE] = tile[
                :, 128 * s : 128 * s + 128
            ].astype(bf16)
    tile = tile_of(
        hidden_own, lambda: grad_own.wait()[...], hidden_other, lambda: grad_other.wait()[...]
    ).astype(bf16)
    for s in range(8):
        rows = tile[PLACE * s : PLACE * s + PLACE]
        for d in range(8):
            start = 2 * SLICE + PLACE * d
            out[slot(s), start : start + PLACE] = rows[:, 128 * d : 128 * d + 128]


def second_back_kernel(
    places, mix_ref, t0, t1, t2, t3, streams, cotangent, branch1, segments, out_weight,
    grad_second, grad_columns, grad_context, low, turned,
):
    mix = Mix(mix_ref)
    live = live_column(segments)
    of_streams = [mix.second_of_streams(r) for r in range(4)]
    of_branch = mix.second_of_branch()
    of_grad = [sum(mix.g[0][s] * mix.r[1][q][s] for s in range(4)) for q in range(4)]
    for c in range(4):
        rows = slice(32 * c, 32 * c + 32)
        second = weighted(
            [(of_streams[r], streams[r, rows].astype(f32)) for r in range(4)]
            + [(of_branch, branch1[rows])]
        )
        normed, inverse = normalize(second)
        grad = (t0[rows] + t1[rows].astype(f32)) + (t2[rows].astype(f32) + t3[rows].astype(f32))
        back = norm_back(grad, normed, inverse)
        grad_second[rows] = back
        branch = weighted(
            [(of_grad[q], cotangent[q, rows].astype(f32)) for q in range(4)] + [(of_branch, back)]
        )
        low[rows] = (live[rows] * branch).astype(bf16)
    turned[...] = contract(out_weight.wait()[...], low[...], ((1,), (1,)))
    for c in range(16):
        row = weight_row(places, HEAD_OF[c] // 2) + HD * (HEAD_OF[c] % 2)
        grad_context[c] = turned[pl.ds(pl.multiple_of(row, HD), HD), :].astype(bf16)
    for i in range(8):
        grad_columns[2 * (i % 4) + i // 4] = low[:, 128 * i : 128 * i + 128]


def mix_sums_kernel(
    mix_ref, t0, t1, t2, t3, streams, cotangent, branch1, grad_second, segments,
    out, branch2, acc,
):
    mix = Mix(mix_ref)
    live = live_column(segments)
    for c in range(4):
        rows = slice(32 * c, 32 * c + 32)
        branch2[rows] = live[rows] * (
            (t0[rows] + t1[rows].astype(f32)) + (t2[rows].astype(f32) + t3[rows].astype(f32))
        )
    acc[...] = jnp.zeros_like(acc)

    def fold(values):
        return sum(values[:8, 128 * j : 128 * j + 128] for j in range(2)) + sum(
            values[8:, 128 * j : 128 * j + 128] for j in range(2)
        )

    @pl.loop(0, 8)
    def _(r):
        rows = pl.ds(pl.multiple_of(r * 16, 16), 16)

        @pl.loop(0, 4)
        def _(l):
            lanes = pl.ds(pl.multiple_of(l * 256, 256), 256)
            hin = [streams[s, rows, lanes].astype(f32) for s in range(4)]
            top = [cotangent[s, rows, lanes].astype(f32) for s in range(4)]
            branch, back = branch1[rows, lanes], grad_second[rows, lanes]
            last = branch2[rows, lanes]
            mid = [
                weighted([(mix.r[0][s][q], hin[q]) for q in range(4)] + [(mix.g[0][s], branch)])
                for s in range(4)
            ]
            grad = [
                weighted([(mix.r[1][q][s], top[q]) for q in range(4)] + [(mix.p[1][s], back)])
                for s in range(4)
            ]
            for s in range(4):
                for q in range(4):
                    acc[s * 6 + 1 + q] += fold(grad[s] * hin[q])
                    acc[24 + s * 6 + 1 + q] += fold(top[s] * mid[q])
                acc[s * 6 + 5] += fold(grad[s] * branch)
                acc[24 + s * 6] += fold(mid[s] * back)
                acc[24 + s * 6 + 5] += fold(top[s] * last)

    out[...] = jnp.sum(acc[...], axis=1)


def out_streams_kernel(mix_ref, streams, branch1, branch2, out):
    mix = Mix(mix_ref)
    of_streams = [
        [sum(mix.r[1][s][q] * mix.r[0][q][r] for q in range(4)) for r in range(4)]
        for s in range(4)
    ]
    of_branch = [sum(mix.r[1][s][q] * mix.g[0][q] for q in range(4)) for s in range(4)]
    for c in range(4):
        rows = slice(32 * c, 32 * c + 32)
        hin = [streams[s, rows].astype(f32) for s in range(4)]
        for s in range(4):
            total = weighted(
                [(of_streams[s][r], hin[r]) for r in range(4)]
                + [(of_branch[s], branch1[rows]), (mix.g[1][s], branch2[rows])]
            )
            out[s, rows] = total.astype(bf16)


def near_lanes(values, near):
    return jnp.concatenate(
        [values[:, TILE * k + 128 * near : TILE * k + 128 * near + 128] for k in range(4)], axis=1
    )


def pair_back_kernel(places, own, far, weights, grad_own, grad_other, pair):
    half = places[1]
    for j in range(3):
        rows = slice(HD * j, HD * j + HD)
        pair[pl.ds(pl.multiple_of(128 * j + HD * half, HD), HD), :] = own[rows]
        pair[pl.ds(pl.multiple_of(128 * j + HD * (1 - half), HD), HD), :] = far[rows]
    for near, target in ((1, grad_other), (0, grad_own)):
        total = contract(near_lanes(pair, near), weights[...], ((0,), (0,)))
        target[...] = total.astype(bf16).reshape(4, 128, 1024)


def narrow_tiles_kernel(
    places, pair, normed_own, normed_other, columns, context_own, context_other, out
):
    z, core = places[0], places[2]
    tile = jnp.zeros((384, 1024), f32)
    for near, tokens in enumerate((normed_own, normed_other)):
        tokens = tokens[:, 0:128].reshape(512, 1024)
        tile = tile + contract(near_lanes(pair, near), tokens, ((1,), (0,)))
    for s in range(8):
        out[s, 0:384] = tile[:, 128 * s : 128 * s + 128].astype(bf16)
    tile = jnp.zeros((128, 1024), f32)
    for back in range(4):
        for near in range(2):
            source = columns[2 * lax.rem(z - back + 4, 4) + lax.rem(core + near, 2)]
            context = (context_own if near == 0 else context_other)[back]
            tile = tile + contract(source, context, ((0,), (1,)))
    for s in range(8):
        out[s, 384:512] = tile[:, 128 * s : 128 * s + 128].astype(bf16)


def fold_kernel(blocks, *outs):
    start = 0
    for out in outs:
        rows = slice(start, start + out.shape[0])
        total = blocks[0, rows].astype(f32)
        for s in range(1, 8):
            total = total + blocks[s, rows].astype(f32)
        out[...] = total.astype(bf16)
        start += out.shape[0]


def fold_narrow_kernel(blocks, out):
    total = blocks[0].astype(f32)
    for s in range(1, 8):
        total = total + blocks[s].astype(f32)
    out[0:512] = total[0:512].astype(bf16)
    high, low = two_parts(total[512:513] + total[513:514])
    out[512:528] = jnp.concatenate([high, low, jnp.zeros((14, 128), bf16)], axis=0)


def add_narrow_kernel(own, far, out):
    total = own[...].astype(f32) + far[...].astype(f32)
    out[0:512] = total[0:512].astype(bf16)
    high, low = two_parts(total[512:513] + total[513:514])
    out[512:528] = jnp.concatenate([high, low, jnp.zeros((14, 128), bf16)], axis=0)


def member(places, own, other, index):
    back = lax.rem(places[0] - index % 4 + 4, 4)
    return jnp.where(places[2] == index // 4, own[back].astype(f32), other[back].astype(f32))


def finish_wide_kernel(places, own, other, gate_up, down, rows):
    for i in range(8):
        block = member(places, own, other, i)
        for s in range(8):
            for j in range(2):
                start = SLICE * j + PLACE * s
                unit = 8 * PIECE * s + PIECE * i
                rows[j, unit : unit + PIECE] = block[start : start + PIECE]
        for d in range(8):
            start = 2 * SLICE + PLACE * d
            down[PIECE * i : PIECE * i + PIECE, 128 * d : 128 * d + 128] = block[
                start : start + PIECE
            ]
    for j in range(2):
        for k in range(rows.shape[1] // 128):
            lanes = slice(128 * k, 128 * k + 128)
            gate_up[j, :, lanes] = rows[j, lanes].T


def finish_narrow_kernel(places, own, other, qkv, out, sums):
    total = jnp.zeros((1, 128), f32)
    for i in range(8):
        block = member(places, own, other, i)
        total = total + (block[512:513] + block[513:514])
        for j in range(3):
            qkv[j, :, 128 * i : 128 * i + 128] = block[128 * j : 128 * j + 128].T
        out[:, 128 * i : 128 * i + 128] = block[384:512].T
    sums[...] = jnp.broadcast_to(total, (8, 128))


def two_parts(values):
    high = values.astype(bf16)
    return high, (values - high.astype(f32)).astype(bf16)


def first_back_kernel(
    mix_ref, t0, t1, t2, t3, streams, cotangent, grad_second, sums, tiles, streams_grad, out, mix_rows
):
    mix = Mix(mix_ref)
    of_top = [
        [sum(mix.r[1][q][s] * mix.r[0][s][r] for s in range(4)) for q in range(4)]
        for r in range(4)
    ]
    of_back = [sum(mix.r[0][s][r] * mix.p[1][s] for s in range(4)) for r in range(4)]
    total = [jnp.zeros((1, 1024), f32) for _ in range(4)]
    for c in range(4):
        rows = slice(32 * c, 32 * c + 32)
        hin = [streams[s, rows].astype(f32) for s in range(4)]
        top = [cotangent[s, rows].astype(f32) for s in range(4)]
        normed, inverse = normalize(weighted([(mix.p[0][s], hin[s]) for s in range(4)]))
        grad = (t0[rows] + t1[rows].astype(f32)) + (t2[rows].astype(f32) + t3[rows].astype(f32))
        back1 = norm_back(grad, normed, inverse)
        back2 = grad_second[rows]
        for r in range(4):
            value = weighted(
                [(of_top[r][q], top[q]) for q in range(4)]
                + [(of_back[r], back2), (mix.p[0][r], back1)]
            )
            streams_grad[r, rows] = value.astype(bf16)
            total[r] = total[r] + jnp.sum(hin[r] * back1, axis=0, keepdims=True)
    mix_rows[0:48] = sums[...]
    mix_rows[48:] = jnp.zeros((80, 128), f32)
    for s in range(4):
        row = sum(total[s][:, 128 * k : 128 * k + 128] for k in range(8))
        mix_rows[s * 6 : s * 6 + 1] = row
    high, low = two_parts(jnp.sum(mix_rows[...].T, axis=0, keepdims=True))
    rows = jnp.concatenate([high, low, jnp.zeros((14, 128), bf16)], axis=0)
    tiles = tiles.wait()
    for s in range(8):
        out[s, 0:512] = tiles[s]
        out[s, 512:528] = rows


def split_kernel(source, own, other):
    own[...] = source[0]
    other[...] = source[1]


def copy_kernel(source, out):
    out[...] = source[...]


def add4_kernel(one, two, three, four, out):
    out[...] = (one[...] + two[...]) + (three[...] + four[...])


def add2_kernel(one, two, out):
    out[...] = (one[...].astype(f32) + two[...].astype(f32)).astype(out.dtype)


def shards(
    streams, segments, stream_mix, qkv_weight, out_weight, gate_up_weight, down_weight, cotangent
):
    z, half, core = lax.axis_index("z"), lax.axis_index("xh"), lax.axis_index("co")
    team, row = lax.axis_index(TEAM), lax.axis_index(SHARD)
    width = streams.shape[3]
    ff = down_weight.shape[0]
    places = (jnp.stack([z, half, core, row, team]).astype(jnp.int32), smem)
    mix = (stream_mix, smem)
    streams, cotangent, segments = streams[0], cotangent[0], (segments, vmem)
    token = ((128, width), bf16)
    token4 = ((4, 128, width), bf16)

    def v(*values):
        return [(value, vmem) for value in values]

    def h(*values):
        return [(value, "hbm") for value in values]

    def l(*values):
        return [(value, "late") for value in values]

    def stack(values, parts, name, us=1, order=(), beside=()):
        (result,) = call(
            stack_kernel,
            [((4,) + values.shape, bf16, "hbm")],
            v(values, *parts),
            name,
            us,
            order=order,
            beside=beside,
        )
        return result

    (weights,) = call(
        pick_kernel,
        [((128, 1408 + 2 * SLICE), bf16, "hbm")],
        [places] + l(out_weight, down_weight, gate_up_weight),
        "pick",
        4,
    )
    weights_far = shift(weights, "xl", 1)

    qkv_blocks = pick_heads(team.astype(jnp.int32)[None], qkv_weight)
    (normed1,) = call(
        first_norm_kernel,
        [((144, width), bf16)],
        [mix] + h(streams) + [segments],
        "first_norm",
        3,
        order=[qkv_blocks, weights],
    )
    qkv_blocks = lax.all_to_all(qkv_blocks, SHARD, 0, 0, tiled=True)
    normed1_z = z_issue(normed1)
    normed1_own = stack(normed1, normed1_z, "stack_normed1", beside=[qkv_blocks])
    normed1_other = shift(normed1_own, "co", 1)
    weights, gu_weights = call(
        pair_kernel,
        [((2, 128, 1408), bf16, "hbm"), ((2, 128, 2 * SLICE), bf16, "hbm")],
        h(weights) + v(weights_far),
        "pair_weights",
        2,
        order=[normed1_own],
    )
    weights = lax.all_gather(weights, "y", axis=0, tiled=True).reshape(1024, 1408)
    gu_weights = lax.all_gather(gu_weights, "y", axis=0, tiled=True).reshape(1024, 2 * SLICE)
    freq = rope_base ** (-(jnp.arange(32, dtype=f32) * 2.0) / HD)
    back, near, place = jnp.arange(4), jnp.arange(2), jnp.arange(128)
    positions = (
        512 * ((z - back[None, :, None, None] + 4) % 4)
        + 256 * ((half + near[:, None, None, None]) % 2)
        + 128 * ((core + near[None, None, :, None]) % 2)
        + place[None, None, None, :]
    ).reshape(2, 1, 1024)
    angle = positions.astype(f32) * freq[None, :, None]
    cosine, sine = jnp.cos(angle), jnp.sin(angle)

    (pair_weights,) = call(
        turn_heads_kernel, [((384, width), bf16, "hbm")], v(qkv_blocks), "turn_heads", 1
    )
    kept, sent = call(
        project_kernel,
        [((208, 1024), bf16, "hbm"), ((208, 1024), bf16, "hbm")],
        [places] + h(normed1_own) + v(normed1_other) + h(pair_weights) + v(cosine, sine),
        "project",
        4,
    )
    received = shift(sent, "xh", 1)
    (grad_branch2,) = call(
        grad_branch2_kernel,
        [token],
        [mix] + h(cotangent) + [segments],
        "grad_branch2",
        0,
        order=[kept],
    )
    grad2_z = z_issue(grad_branch2)

    qkv, context_blocks, context_wide, logsum, edges = call(
        attend_kernel,
        [
            ((2, 192, 1024), bf16, "hbm"),
            ((16, HD, 128), bf16, "hbm"),
            ((2, HD, 1024), f32, "hbm"),
            ((2, 8, 1024), f32, "hbm"),
            ((4,), jnp.int32),
        ],
        [places] + h(kept) + v(received),
        "attend",
        12,
        beside=[grad_branch2],
    )
    context_mine = lax.all_to_all(context_blocks, CTX, 0, 0, tiled=True)

    grad2_own = stack(grad_branch2, grad2_z, "stack_grad2", 1, [context_blocks])
    grad2_other = shift(grad2_own, "co", 1)
    normed2, branch1, context = call(
        post_attend_kernel,
        [token, ((128, width), f32, "hbm"), ((width, 128), bf16, "hbm")],
        [places, mix]
        + v(context_mine)
        + [(weights, ("late", 0, 1024))]
        + l(streams)
        + [segments],
        "post_attend",
        3,
        [pltpu.VMEM((width, 128), bf16)],
        [grad2_own],
    )
    normed2_z = z_issue(normed2)
    gu_all, down = call(
        unpack_kernel,
        [((width, 2 * SLICE), bf16, "hbm"), ((SLICE, width), bf16, "hbm")],
        [places, (weights, ("hbm", 1024, 1408))] + h(gu_weights),
        "unpack",
        4,
        beside=normed2_z[:1],
    )
    normed2_own = stack(normed2, normed2_z, "stack_normed2", order=[down])
    normed2_other = shift(normed2_own, "co", 1)
    acts = [token4] + [((512, SLICE), bf16, "hbm")] * 3
    grad_own, hidden_own, gate_own, up_own = call(
        feed_forward_kernel,
        acts,
        h(normed2_own, grad2_own, gu_all, down),
        "feed_forward_own",
        5,
    )
    grad_other, hidden_other, gate_other, up_other = call(
        feed_forward_kernel,
        acts,
        v(normed2_other, grad2_other) + h(gu_all, down),
        "feed_forward_other",
        5,
        order=[hidden_own],
    )

    def core_add(own, other, name, order, beside=(), own_in_hbm=False):
        return call(
            core_add_kernel,
            [((128, width), f32, "hbm")] + [token] * 3,
            (h(own) if own_in_hbm else v(own)) + v(shift(other, "co", 1)),
            name,
            1,
            order=order,
            beside=beside,
        )

    def z_terms(terms):
        return [terms[0]] + [shift(term, "z", -k) for k, term in enumerate(terms[1:], 1)]

    terms = core_add(grad_own, grad_other, "core_add_second", [hidden_other])
    grad_normed2 = z_terms(terms)
    half_own, half_other, context = call(
        branch2_kernel,
        [token4 + ("hbm",), token4 + ("hbm",), ((width, 128), bf16, "hbm")],
        h(hidden_own, hidden_other, down, context),
        "branch2",
        3,
        order=[terms[0]],
    )
    context_z = z_issue(context)

    grad_second, grad_columns, grad_context = call(
        second_back_kernel,
        [
            ((128, width), f32, "hbm"),
            ((8, 128, 128), bf16, "hbm"),
            ((16, HD, 128), bf16, "hbm"),
        ],
        [places, mix]
        + h(grad_normed2[0])
        + v(*grad_normed2[1:])
        + h(streams, cotangent, branch1)
        + [segments, (weights, ("late", 0, 1024))],
        "second_back",
        5,
        [pltpu.VMEM((128, width), bf16), pltpu.VMEM((width, 128), f32)],
    )
    grad_context = lax.all_to_all(grad_context, CTX, 0, 0, tiled=True)

    (wide_tiles,) = call(
        wide_tiles_kernel,
        [((8, 3 * SLICE, 128), bf16, "hbm")],
        [places] + l(
            gate_own, normed2_own, gate_other, normed2_other, up_own, up_other,
            hidden_own, grad2_own, hidden_other, grad2_other,
        ),
        "wide_tiles",
        7,
        order=[grad_second],
    )
    wide_mine = lax.psum_scatter(wide_tiles, "y", scatter_dimension=0, tiled=True)
    terms = core_add(half_own, half_other, "core_add_branch2", [wide_tiles], own_in_hbm=True)
    branch2 = z_terms(terms)

    grads_own, grads_far, columns = call(
        attend_back_kernel,
        [((192, 1024), bf16, "hbm"), ((192, 1024), bf16, "hbm"), ((8, 128, 128), bf16, "hbm")],
        [places, (edges, smem)]
        + h(qkv, context_wide, logsum)
        + v(grad_context, cosine, sine)
        + h(grad_columns),
        "attend_back",
        25,
        [
            pltpu.VMEM((8, HD, TILE), f32),
            pltpu.VMEM((8, HD, TILE), f32),
            pltpu.VMEM((2, 192, 1024), bf16),
        ],
        [terms[0]],
    )
    received = shift(grads_far, "xh", 1)
    columns = lax.all_to_all(columns, ("z", "co"), 0, 0, tiled=True)
    sums, branch2 = call(
        mix_sums_kernel,
        [((48, 128), f32, "hbm"), ((128, width), f32, "hbm")],
        [mix]
        + h(branch2[0])
        + v(*branch2[1:])
        + h(streams, cotangent, branch1, grad_second)
        + [segments],
        "mix_sums",
        7,
        [pltpu.VMEM((48, 8, 128), f32)],
        [grads_own],
        context_z,
    )
    grad_own, grad_other, pair = call(
        pair_back_kernel,
        [token4, token4 + ("hbm",), ((384, 1024), bf16, "hbm")],
        [places] + h(grads_own) + v(received) + h(pair_weights),
        "pair_back",
        4,
        order=[sums],
        beside=[columns],
    )
    wide_type = ((3 * SLICE, 128), bf16)
    wide_mine, wide_far = call(
        split_kernel, [wide_type, wide_type], v(wide_mine), "split_wide", 1, order=[pair]
    )
    wide_far = shift(wide_far, "xl", 1)
    terms = core_add(grad_own, grad_other, "core_add_first", [], [wide_mine])
    grad_normed1 = z_terms(terms)
    context_own = stack(context, context_z, "stack_context", 1, [terms[0]])
    context_other = shift(context_own, "co", 1)

    (wide_rows,) = call(
        add2_kernel, [wide_type], v(wide_mine, wide_far), "add_wide_xl", 1, beside=grad_normed1[1:2]
    )
    wide_far = shift(wide_rows, "xh", 1)
    (narrow_tiles,) = call(
        narrow_tiles_kernel,
        [((8, 512, 128), bf16, "hbm")],
        [places]
        + h(pair, normed1_own, normed1_other)
        + v(columns)
        + h(context_own, context_other),
        "narrow_tiles",
        6,
        order=[terms[0]],
        beside=[wide_rows],
    )
    narrow_order = narrow_tiles
    (wide_rows,) = call(
        add2_kernel, [wide_type], v(wide_rows, wide_far), "add_wide", 1, order=[narrow_order]
    )
    wide_z = z_issue(wide_rows)
    streams_grad, narrow_tiles = call(
        first_back_kernel,
        [token4 + ("hbm",), ((8, 528, 128), bf16, "hbm")],
        [mix]
        + h(grad_normed1[0])
        + v(*grad_normed1[1:])
        + h(streams, cotangent, grad_second, sums)
        + l(narrow_tiles),
        "first_back",
        6,
        [pltpu.VMEM((128, 128), f32)],
        beside=[wide_rows],
    )
    narrow_tiles = lax.all_to_all(narrow_tiles, SHARD, 0, 0, tiled=True)

    narrow_type = [((528, 128), bf16)]
    (mine,) = call(fold_narrow_kernel, narrow_type, v(narrow_tiles), "fold_narrow", 1)
    narrow_far = shift(mine, "xh", 1)
    wide_own = stack(wide_rows, wide_z, "stack_wide", 1, beside=[mine])
    wide_other = shift(wide_own, "co", 1)
    (out_streams,) = call(
        out_streams_kernel,
        [token4 + ("hbm",)],
        [mix] + h(streams, branch1, branch2),
        "out_streams",
        4,
        order=[wide_own],
    )
    (narrow_rows,) = call(
        add_narrow_kernel, narrow_type, v(mine, narrow_far), "add_narrow", 1, order=[out_streams]
    )
    narrow_z = z_issue(narrow_rows)
    gate_up_grad, down_grad = call(
        finish_wide_kernel,
        [((2, 128, 8 * ff), f32, "hbm"), ((ff, width), f32, "hbm")],
        [places] + h(wide_own) + v(wide_other),
        "finish_wide",
        5,
        [pltpu.VMEM((2, 8 * ff, 128), f32)],
        beside=[narrow_rows],
    )
    narrow_own = stack(narrow_rows, narrow_z, "stack_narrow", 1, [down_grad])
    narrow_other = shift(narrow_own, "co", 1)
    qkv_grad, out_grad, sums = call(
        finish_narrow_kernel,
        [((3, 128, width), f32, "hbm"), ((128, width), f32, "hbm"), ((8, 128), f32, "hbm")],
        [places] + h(narrow_own) + v(narrow_other),
        "finish_narrow",
        3,
    )
    mix_grad = sums[0, :48].reshape(2, 4, 6)
    return (
        out_streams[None], streams_grad[None], qkv_grad, out_grad, gate_up_grad, down_grad, mix_grad,
    )


def solution(mesh):
    fine = Mesh(
        np.asarray(mesh.devices).reshape([n for _, n in AXES]), tuple(name for name, _ in AXES)
    )
    in_specs = (
        P(SHARD, None, CTX, None),
        P(SHARD, CTX),
        P(),
        P(None, SHARD, None),
        P(SHARD, None),
        P(None, SHARD, None),
        P(SHARD, None),
        P(SHARD, None, CTX, None),
    )
    out_specs = (
        P(SHARD, None, CTX, None),
        P(SHARD, None, CTX, None),
        P(None, SHARD, None),
        P(SHARD, None),
        P(None, SHARD, None),
        P(SHARD, None),
        P(),
    )
    return jax.shard_map(shards, mesh=fine, in_specs=in_specs, out_specs=out_specs, check_vma=False)
```

```python
import jax
import jax.numpy as jnp
import numpy as np
from jax import lax
from jax.experimental import pallas as pl
from jax.experimental.pallas import tpu as pltpu
from jax.sharding import Mesh
from jax.sharding import PartitionSpec as P

HD = 64
TILE = 256
VMEM = 24 * 1024 * 1024
COST = 1.1e9
PIECE = 44
PLACE = 48
SLICE = 8 * PLACE
eps = 1e-05
rope_base = 1000000.0
neg_big = -1e30
bf16 = jnp.bfloat16
f32 = jnp.float32
smem = pl.BlockSpec(memory_space=pltpu.SMEM)
vmem = pl.BlockSpec(memory_space=pltpu.VMEM)
anywhere = pl.BlockSpec(memory_space=pl.ANY)
hbm = pl.BlockSpec(memory_space=pltpu.HBM)
raw = pl.BlockSpec(memory_space=pltpu.HBM)

AXES = (("z", 4), ("xh", 2), ("co", 2), ("xl", 2), ("y", 4))
SIZE = dict(AXES)
CTX = ("z", "xh", "co")
SHARD = ("xl", "y")
TEAM = ("co", "z")
HEAD_OF = [8 * (c % 2) + 2 * (c // 4) + (c // 2) % 2 for c in range(16)]


class Kept:
    def __init__(self):
        self.arrays = []

    def add(self, array):
        self.arrays.append(array)
        return array

    def __contains__(self, array):
        return any(array is other for other in self.arrays)


kept_arrays = Kept()


def shift(values, axis, amount):
    count = SIZE[axis]
    moved = lax.ppermute(values, axis, [(i, (i + amount) % count) for i in range(count)])
    if axis == "co" and values in kept_arrays:
        kept_arrays.add(moved)
    return moved


def z_issue(values):
    return [shift(values, "z", k) for k in range(1, 4)]


class Late:
    def __init__(self, copy, ref):
        self.copy, self.ref = copy, ref

    def wait(self):
        if self.copy is not None:
            self.copy.wait()
        return self.ref


def call(kernel, outs, ins, name, us, scratch=(), order=(), beside=()):
    known = (smem, vmem, raw)
    stays = [value in kept_arrays and place not in (smem, raw) for value, place in ins]
    extra_ins = len(order) + len(beside)
    ends = len(ins), len(ins) + extra_ins, len(ins) + extra_ins + len(outs)
    near = [k for k, (_, place) in enumerate(ins) if place not in known and not stays[k]]
    far = [k for k, out in enumerate(outs) if len(out) > 2 and out[2] == "hbm"]

    def part(k):
        value, place = ins[k]
        if isinstance(place, tuple):
            return value.shape[:-1] + (place[2] - place[1],)
        return value.shape

    def body(*refs):
        given, results, rest = list(refs[: ends[0]]), list(refs[ends[1] : ends[2]]), refs[ends[2] :]
        rest, sems = (rest[:-1], rest[-1]) if near or far else (rest, None)
        loaded = rest[len(scratch) : len(scratch) + len(near)]
        staged = rest[len(scratch) + len(near) :]
        for k, (_, place) in enumerate(ins):
            if stays[k] and place == "late":
                given[k] = Late(None, given[k])
        copies, waits = [], []
        for j, (k, ref) in enumerate(zip(near, loaded)):
            source, place = given[k], ins[k][1]
            if isinstance(place, tuple):
                source = source.at[..., place[1] : place[2]]
            copies.append(pltpu.make_async_copy(source, ref, sems.at[j]))
            if (place[0] if isinstance(place, tuple) else place) == "hbm":
                waits.append(copies[-1])
                given[k] = ref
            else:
                given[k] = Late(copies[-1], ref)
        for copy in copies:
            copy.start()
        for copy in waits:
            copy.wait()
        copies = []
        for j, (k, ref) in enumerate(zip(far, staged)):
            copies.append(pltpu.make_async_copy(ref, results[k], sems.at[len(near) + j]))
            results[k] = ref
        kernel(*given, *results, *rest[: len(scratch)])
        for copy in copies:
            copy.start()
        for copy in copies:
            copy.wait()

    extra = [pltpu.VMEM(part(k), ins[k][0].dtype) for k in near]
    extra += [pltpu.VMEM(outs[k][0], outs[k][1]) for k in far]
    if near or far:
        extra.append(pltpu.SemaphoreType.DMA((len(near) + len(far),)))

    def in_hbm(value):
        return pltpu.with_memory_space_constraint(value, pltpu.HBM)

    def out_type(out):
        if len(out) > 2 and out[2] == "vmem":
            return pltpu.VMEM(out[0], out[1])
        if len(out) > 2:
            return pltpu.HBM(out[0], out[1])
        return jax.ShapeDtypeStruct(out[0], out[1])

    def in_vmem(value):
        return pltpu.with_memory_space_constraint(value, pltpu.VMEM)

    def spec(k):
        return vmem if stays[k] else ins[k][1] if ins[k][1] in known else hbm

    def placed(k):
        value, place = ins[k]
        return in_vmem(value) if stays[k] else value if place in (smem, vmem) else in_hbm(value)

    results = pl.pallas_call(
        body,
        out_shape=tuple(out_type(out) for out in outs),
        in_specs=[spec(k) for k in range(len(ins))]
        + [anywhere if value in kept_arrays else hbm for value in order]
        + [anywhere] * len(beside),
        out_specs=tuple(
            hbm if k in far else smem if out[1] == jnp.int32 else vmem
            for k, out in enumerate(outs)
        ),
        scratch_shapes=list(scratch) + extra,
        compiler_params=pltpu.CompilerParams(vmem_limit_bytes=VMEM),
        cost_estimate=pl.CostEstimate(
            flops=int(us * COST), bytes_accessed=0, transcendentals=0
        ),
        name=name,
    )(
        *[placed(k) for k in range(len(ins))],
        *[value if value in kept_arrays else in_hbm(value) for value in order],
        *beside,
    )
    for out, result in zip(outs, results):
        if len(out) > 2 and out[2] == "vmem":
            kept_arrays.add(result)
    return results


def contract(left, right, dims):
    return lax.dot_general(left, right, (dims, ((), ())), preferred_element_type=f32)


def normalize(values):
    centered = values - jnp.mean(values, axis=-1, keepdims=True)
    inverse = lax.rsqrt(jnp.mean(centered * centered, axis=-1, keepdims=True) + eps)
    return (centered * inverse, inverse)


def norm_back(grad, normed, inverse):
    return inverse * (
        grad
        - jnp.mean(grad, axis=-1, keepdims=True)
        - normed * jnp.mean(grad * normed, axis=-1, keepdims=True)
    )


def weighted(terms):
    total = None
    for weight, values in terms:
        part = weight * values
        total = part if total is None else total + part
    return total


def live_column(segments):
    wide = jnp.broadcast_to((segments[...] > 0).astype(f32), (128, 128))
    return wide.T[:, 0:1]


class Mix:
    def __init__(self, ref):
        self.p = [[ref[m, s, 0] for s in range(4)] for m in range(2)]
        self.r = [[[ref[m, s, 1 + r] for r in range(4)] for s in range(4)] for m in range(2)]
        self.g = [[ref[m, s, 5] for s in range(4)] for m in range(2)]

    def second_of_streams(self, r):
        return sum(self.p[1][s] * self.r[0][s][r] for s in range(4))

    def second_of_branch(self):
        return sum(self.p[1][s] * self.g[0][s] for s in range(4))


def core_add_kernel(own, received, first, *rest):
    first[...] = own[0].astype(f32) + received[0].astype(f32)
    for k, target in enumerate(rest, 1):
        target[...] = (own[k].astype(f32) + received[k].astype(f32)).astype(bf16)


def first_norm_kernel(mix_ref, streams, segments, out):
    mix = Mix(mix_ref)
    for c in range(4):
        rows = slice(32 * c, 32 * c + 32)
        first = weighted([(mix.p[0][s], streams[s, rows].astype(f32)) for s in range(4)])
        out[rows] = normalize(first)[0].astype(bf16)
    out[128:144] = jnp.zeros((16, 1024), bf16)
    out[128:144, 0:128] = jnp.broadcast_to(segments[...].astype(f32), (16, 128)).astype(bf16)


def pick_heads_kernel(places, weights, out, block):
    pltpu.sync_copy(
        weights.at[:, :, pl.ds(pl.multiple_of(places[4] * 128, 128), 128)], block
    )
    for s in range(8):
        out[s] = block[...]


def pieces(d):
    start, place, result = PLACE * d, 0, []
    while place < PLACE:
        count = min(PLACE - place, 128 - start % 128)
        result.append((place, start // 128, start % 128, count))
        start, place = start + count, place + count
    return result


def pick_kernel(places, out_weight, down, gate_up, wide):
    team, core = places[4], places[2]
    own, _ = halves(core)
    wide[:, 0:512] = out_weight.wait()[:, own]
    place = lax.broadcasted_iota(jnp.int32, (PLACE, 8 * PIECE), 0)
    unit = lax.broadcasted_iota(jnp.int32, (PLACE, 8 * PIECE), 1)
    picked = jnp.where((unit == team * PIECE + place) & (place < PIECE), 1.0, 0.0).astype(bf16)
    rows = contract(picked, down.wait()[...], ((1,), (0,))).astype(bf16)
    for d in range(8):
        for place, tile, start, count in pieces(d):
            lanes = slice(512 + 128 * tile, 512 + 128 * tile + 128)
            wide[start : start + count, lanes] = rows[
                place : place + count, 128 * d : 128 * d + 128
            ]
    gate_up = gate_up.wait()
    units = gate_up.shape[2]
    unit = lax.broadcasted_iota(jnp.int32, (units, SLICE), 0)
    place = lax.broadcasted_iota(jnp.int32, (units, SLICE), 1)
    piece = lax.rem(place, PLACE)
    wanted = (place // PLACE) * (8 * PIECE) + team * PIECE + piece
    picked = jnp.where((unit == wanted) & (piece < PIECE), 1.0, 0.0).astype(bf16)
    columns = contract(gate_up[...].reshape(256, units), picked, ((1,), (0,))).astype(bf16)
    for j in range(2):
        wide[:, 896 + SLICE * j : 896 + SLICE * j + SLICE] = columns[128 * j : 128 * j + 128]


def halves(core):
    own = pl.ds(pl.multiple_of(core * 512, 512), 512)
    other = pl.ds(pl.multiple_of((1 - core) * 512, 512), 512)
    return own, other


def unpack_out_kernel(places, near, far, out):
    for part, source in enumerate((near, far)):
        source = source.wait()
        for y in range(4):
            s = 4 * lax.rem(places[3] // 4 + part, 2) + y
            out[pl.ds(pl.multiple_of(128 * s, 128), 128)] = source[128 * y : 128 * y + 128]


def unpack_kernel(places, near, far, gate_up, down):
    for part, source in enumerate((near, far)):
        source = source.wait()
        for y in range(4):
            s = 4 * lax.rem(places[3] // 4 + part, 2) + y
            block = source[128 * y : 128 * y + 128]
            gate_up[pl.ds(pl.multiple_of(128 * s, 128), 128)] = block[:, 384:]
            for d in range(8):
                for place, tile, start, count in pieces(d):
                    row = pl.multiple_of(PLACE * s + place, 16)
                    down[pl.ds(row, count), 128 * d : 128 * d + 128] = block[
                        start : start + count, 128 * tile : 128 * tile + 128
                    ]


def grad_branch2_kernel(mix_ref, cotangent, segments, out):
    mix = Mix(mix_ref)
    live = live_column(segments)
    for c in range(4):
        rows = slice(32 * c, 32 * c + 32)
        total = weighted([(mix.g[1][s], cotangent[s, rows].astype(f32)) for s in range(4)])
        out[rows] = (live[rows] * total).astype(bf16)


def turn(values, cosine, sine):
    one, two = values[:32], values[32:]
    return jnp.concatenate([one * cosine - two * sine, two * cosine + one * sine], axis=0)


def turn_back(grad, cosine, sine):
    one, two = grad[:32], grad[32:]
    return jnp.concatenate([one * cosine + two * sine, two * cosine - one * sine], axis=0)


def turn_heads_kernel(weights, out):
    for s in range(8):
        for j in range(3):
            out[128 * j : 128 * j + 128, 128 * s : 128 * s + 128] = weights[s, j].T


def stack_kernel(first, second, third, fourth, out):
    for k, part in enumerate((first, second, third, fourth)):
        out[k] = part[...]


def project_kernel(places, own, other, wide, cosine, sine, kept, sent):
    half = places[1]

    def rows(head):
        return [wide[pl.ds(pl.multiple_of(128 * j + HD * head, HD), HD), :] for j in range(3)]

    mine = jnp.concatenate(rows(half) + rows(1 - half), axis=0)
    for near, tokens in enumerate((own, other)):
        tokens = tokens.wait()
        blocks = contract(mine, tokens[:, 0:128].reshape(512, 1024), ((1,), (1,)))
        for back in range(4):
            lanes = slice(back * TILE + near * 128, back * TILE + near * 128 + 128)
            block = blocks[:, 128 * back : 128 * back + 128]
            segs = tokens[back, 128:144, 0:128]
            cos, sin = cosine[0, :, lanes], sine[0, :, lanes]
            for target, base in ((kept, 0), (sent, 192)):
                query = turn(block[base : base + 64], cos, sin).astype(bf16)
                target[0:64, lanes] = (query.astype(f32) * 0.125).astype(bf16)
                target[64:128, lanes] = turn(block[base + 64 : base + 128], cos, sin).astype(bf16)
                target[128:192, lanes] = block[base + 128 : base + 192].astype(bf16)
                target[192:208, lanes] = segs


def tile_mask(core, edges, k_tile, q_tile):
    local_k = lax.broadcasted_iota(jnp.int32, (TILE, 1), 0)
    local_q = lax.broadcasted_iota(jnp.int32, (1, TILE), 1)
    k_pos = (local_k + core * 128) % TILE + k_tile * TILE
    q_pos = (local_q + core * 128) % TILE + q_tile * TILE
    start = jnp.zeros_like(q_pos)
    for edge in edges:
        start = jnp.where(q_pos >= edge, edge, start)
    return (k_pos >= start) & (k_pos <= q_pos)


def first_tile(edges, q_tile):
    place = q_tile * TILE
    start = jnp.int32(0)
    for edge in edges:
        start = jnp.where(place >= edge, edge, start)
    return start // TILE


def tile_place(places, tile):
    part = lax.rem(lax.rem(tile, 2) + places[1], 2)
    back = lax.rem(places[0] - tile // 2 + 4, 4)
    return part, pl.ds(pl.multiple_of(back * TILE, TILE), TILE)


def attend_kernel(places, kept, received, qkv, context, context_wide, logsum, edges_out):
    core = places[2]
    qkv[0] = kept[0:192]
    qkv[1] = received[0:192]
    seg_own = kept[192:208].astype(f32)
    seg_far = received[192:208].astype(f32)
    edges = []
    for d in range(1, 5):
        count = jnp.float32(0)
        for seg in (seg_own, seg_far):
            inside = (seg > 0.5) & (seg < d + 0.5)
            count = count + jnp.sum(jnp.where(inside, 0.0625, 0.0))
        edge = count.astype(jnp.int32)
        edges_out[d - 1] = edge
        edges.append(edge)

    @pl.loop(0, 8)
    def _(q_tile):
        q_part, q_lanes = tile_place(places, q_tile)
        query = qkv[q_part, 0:HD, q_lanes]

        def load(k_tile):
            k_part, k_lanes = tile_place(places, jnp.maximum(k_tile, 0))
            key = qkv[k_part, HD : 2 * HD, k_lanes]
            raw = contract(key, query, ((0,), (0,)))
            raw = jnp.where(tile_mask(core, edges, k_tile, q_tile), raw, neg_big)
            return raw, qkv[k_part, 2 * HD : 3 * HD, k_lanes]

        def step(pair, carry):
            top, total, mixed = carry
            raw1, value1 = load(q_tile - 2 * pair)
            raw2, value2 = load(q_tile - 2 * pair - 1)
            new_top = jnp.maximum(
                top,
                jnp.maximum(
                    jnp.max(raw1, axis=0, keepdims=True), jnp.max(raw2, axis=0, keepdims=True)
                ),
            )
            weights1, weights2 = jnp.exp(raw1 - new_top), jnp.exp(raw2 - new_top)
            fade = jnp.exp(top - new_top)
            total = total * fade + (
                jnp.sum(weights1, axis=0, keepdims=True) + jnp.sum(weights2, axis=0, keepdims=True)
            )
            mixed = mixed * fade + (
                contract(value1, weights1.astype(bf16), ((1,), (0,)))
                + contract(value2, weights2.astype(bf16), ((1,), (0,)))
            )
            return new_top, total, mixed

        init = (
            jnp.full((1, TILE), neg_big, f32),
            jnp.zeros((1, TILE), f32),
            jnp.zeros((HD, TILE), f32),
        )
        top, total, mixed = lax.fori_loop(0, (q_tile - first_tile(edges, q_tile)) // 2 + 1, step, init)
        mixed = mixed / total
        context_wide[q_part, :, q_lanes] = mixed
        logsum[q_part, :, q_lanes] = jnp.broadcast_to(top + jnp.log(total), (8, TILE))
        low = mixed.astype(bf16)
        context[q_tile * 2 + core] = low[:, :128]
        context[q_tile * 2 + 1 - core] = low[:, 128:]


def attend_back_kernel(
    places, edge_ref, qkv, context_wide, logsum, grad_context, cosine, sine, columns,
    grads_own, grads_far, columns_out, dk_acc, dv_acc, grads,
):
    core = places[2]
    columns_out[...] = columns[...]
    edges = [edge_ref[d] for d in range(4)]
    dk_acc[...] = jnp.zeros_like(dk_acc)
    dv_acc[...] = jnp.zeros_like(dv_acc)

    def put(tile, rows, values):
        part, lanes = tile_place(places, tile)
        grads[part, rows, lanes] = values.astype(bf16)

    @pl.loop(0, 8)
    def _(q_tile):
        q_part, q_lanes = tile_place(places, q_tile)
        query = qkv[q_part, 0:HD, q_lanes]
        grad = jnp.concatenate(
            [grad_context[q_tile * 2 + core], grad_context[q_tile * 2 + 1 - core]], axis=1
        )
        delta = jnp.sum(
            grad.astype(f32) * context_wide[q_part, :, q_lanes], axis=0, keepdims=True
        )
        norm = logsum[q_part, 0:1, q_lanes]

        def part(k_tile):
            place = jnp.maximum(k_tile, 0)
            k_part, k_lanes = tile_place(places, place)
            key = qkv[k_part, HD : 2 * HD, k_lanes]
            value = qkv[k_part, 2 * HD : 3 * HD, k_lanes]
            raw = contract(key, query, ((0,), (0,)))
            dprobs = contract(value, grad, ((0,), (0,)))
            raw = jnp.where(tile_mask(core, edges, k_tile, q_tile), raw, neg_big)
            probs = jnp.exp(raw - norm)
            draw = (probs * (dprobs - delta)).astype(bf16)
            return place, key, probs.astype(bf16), draw

        def step(pair, dq):
            for place, key, probs, draw in [
                part(q_tile - 2 * pair),
                part(q_tile - 2 * pair - 1),
            ]:
                dv_acc[place] += contract(grad, probs, ((1,), (1,)))
                dk_acc[place] += contract(query, draw, ((1,), (1,)))
                dq = dq + contract(key, draw, ((1,), (0,)))
            return dq

        dq = lax.fori_loop(
            0, (q_tile - first_tile(edges, q_tile)) // 2 + 1, step, jnp.zeros((HD, TILE), f32)
        )
        cos, sin = cosine[q_part, :, q_lanes], sine[q_part, :, q_lanes]
        put(q_tile, slice(0, HD), turn_back(dq * 0.125, cos, sin))

    @pl.loop(0, 8)
    def _(tile):
        part, lanes = tile_place(places, tile)
        cos, sin = cosine[part, :, lanes], sine[part, :, lanes]
        put(tile, slice(HD, 2 * HD), turn_back(dk_acc[tile], cos, sin))
        put(tile, slice(2 * HD, 3 * HD), dv_acc[tile])

    grads_own[...] = grads[0]
    grads_far[...] = grads[1]


def post_attend_own_kernel(blocks, out_own, context, half):
    for c in range(16):
        context[HD * HEAD_OF[c] : HD * HEAD_OF[c] + HD] = blocks[c]
    half[...] = contract(context[...], out_own[...], ((0,), (0,)))


def post_attend_kernel(
    places, mix_ref, context, half, out_other, streams, segments, normed2, branch1
):
    mix = Mix(mix_ref)
    live = live_column(segments)
    own, other = halves(places[2])
    branch1[:, other] = live * contract(context[...], out_other.wait()[...], ((0,), (0,)))
    branch1[:, own] = live * half[...]
    streams = streams.wait()
    of_streams = [mix.second_of_streams(r) for r in range(4)]
    of_branch = mix.second_of_branch()
    for c in range(4):
        rows = slice(32 * c, 32 * c + 32)
        second = weighted(
            [(of_streams[r], streams[r, rows].astype(f32)) for r in range(4)]
            + [(of_branch, branch1[rows])]
        )
        normed2[rows] = normalize(second)[0].astype(bf16)


def ready(value):
    return value.wait() if isinstance(value, Late) else value


def feed_forward_kernel(normed, grad_branch, weights, down, grad_normed, hidden, grad_gate, grad_up):
    tokens = ready(normed)[...].reshape(512, 1024)
    weights = ready(weights)
    gate = contract(tokens, weights[:, 0:SLICE], ((1,), (0,)))
    up = contract(tokens, weights[:, SLICE : 2 * SLICE], ((1,), (0,)))
    sigma = jax.nn.sigmoid(gate)
    silu = gate * sigma
    hidden[...] = (silu * up).astype(bf16)
    grad = contract(
        ready(grad_branch)[...].reshape(512, 1024), ready(down)[...], ((1,), (1,))
    )
    grad_of_gate = (grad * up * sigma * (1.0 + gate * (1.0 - sigma))).astype(bf16)
    grad_of_up = (grad * silu).astype(bf16)
    grad_gate[...] = grad_of_gate
    grad_up[...] = grad_of_up
    total = contract(grad_of_gate, weights[:, 0:SLICE], ((1,), (1,)))
    total = total + contract(grad_of_up, weights[:, SLICE : 2 * SLICE], ((1,), (1,)))
    grad_normed[...] = total.astype(bf16).reshape(4, 128, 1024)


def branch2_kernel(hidden_own, hidden_other, down, context, own, other, context_out):
    context_out[...] = context[...]
    own[...] = contract(hidden_own[...], down[...], ((1,), (0,))).astype(bf16).reshape(4, 128, 1024)
    other[...] = (
        contract(hidden_other[...], down[...], ((1,), (0,))).astype(bf16).reshape(4, 128, 1024)
    )


def wide_tiles_kernel(
    places, gate_own, normed_own, gate_other, normed_other, up_own, up_other,
    hidden_own, grad_own, hidden_other, grad_other, out,
):
    def tile_of(left_own, right_own, left_other, right_other):
        tile = contract(left_own.wait()[...], right_own().reshape(512, 1024), ((0,), (0,)))
        return tile + contract(
            left_other.wait()[...], right_other().reshape(512, 1024), ((0,), (0,))
        )

    def slot(s):
        return 2 * (s % 4) + lax.rem(s // 4 + places[3] // 4, 2)

    first = tile_of(
        gate_own, lambda: normed_own.wait()[...], gate_other, lambda: normed_other.wait()[...]
    )
    second = tile_of(
        up_own, lambda: normed_own.ref[...], up_other, lambda: normed_other.ref[...]
    )
    for j, tile in enumerate((first, second)):
        for s in range(8):
            out[slot(s), SLICE * j : SLICE * j + SLICE] = tile[
                :, 128 * s : 128 * s + 128
            ].astype(bf16)
    tile = tile_of(
        hidden_own, lambda: grad_own.wait()[...], hidden_other, lambda: grad_other.wait()[...]
    ).astype(bf16)
    for s in range(8):
        rows = tile[PLACE * s : PLACE * s + PLACE]
        for d in range(8):
            start = 2 * SLICE + PLACE * d
            out[slot(s), start : start + PLACE] = rows[:, 128 * d : 128 * d + 128]


def second_back_kernel(
    places, mix_ref, t0, t1, t2, t3, streams, branch1, cotangent, segments, out_own, out_other,
    grad_second, grad_columns, grad_context, low, turned,
):
    mix = Mix(mix_ref)
    live = live_column(segments)
    of_streams = [mix.second_of_streams(r) for r in range(4)]
    of_branch = mix.second_of_branch()
    of_grad = [sum(mix.g[0][s] * mix.r[1][q][s] for s in range(4)) for q in range(4)]
    for c in range(4):
        rows = slice(32 * c, 32 * c + 32)
        second = weighted(
            [(of_streams[r], streams[r, rows].astype(f32)) for r in range(4)]
            + [(of_branch, branch1[rows])]
        )
        normed, inverse = normalize(second)
        grad = (t0[rows] + t1[rows].astype(f32)) + (t2[rows].astype(f32) + t3[rows].astype(f32))
        back = norm_back(grad, normed, inverse)
        grad_second[rows] = back
        if c == 0:
            cotangent = cotangent.wait()
        branch = weighted(
            [(of_grad[q], cotangent[q, rows].astype(f32)) for q in range(4)] + [(of_branch, back)]
        )
        low[rows] = (live[rows] * branch).astype(bf16)
    own, other = halves(places[2])
    turned[...] = contract(out_own.wait()[...], low[:, own], ((1,), (1,)))
    turned[...] += contract(out_other.wait()[...], low[:, other], ((1,), (1,)))
    for c in range(16):
        grad_context[c] = turned[HD * HEAD_OF[c] : HD * HEAD_OF[c] + HD].astype(bf16)
    for i in range(8):
        grad_columns[2 * (i % 4) + i // 4] = low[:, 128 * i : 128 * i + 128]


def mix_sums_kernel(
    mix_ref, t0, t1, t2, t3, streams, cotangent, branch1, grad_second, segments,
    out, branch2, acc,
):
    mix = Mix(mix_ref)
    live = live_column(segments)
    acc[...] = jnp.zeros_like(acc)
    for c in range(4):
        rows = slice(32 * c, 32 * c + 32)
        branch2[rows] = live[rows] * (
            (t0[rows] + t1[rows].astype(f32)) + (t2[rows].astype(f32) + t3[rows].astype(f32))
        )

    def fold(values):
        return sum(values[:8, 128 * j : 128 * j + 128] for j in range(4)) + sum(
            values[8:, 128 * j : 128 * j + 128] for j in range(4)
        )

    @pl.loop(0, 8)
    def _(r):
        rows = pl.ds(pl.multiple_of(r * 16, 16), 16)

        @pl.loop(0, 2)
        def _(l):
            lanes = pl.ds(pl.multiple_of(l * 512, 512), 512)
            hin = [streams[s, rows, lanes].astype(f32) for s in range(4)]
            branch, back = branch1[rows, lanes], grad_second[rows, lanes]
            last = branch2[rows, lanes]
            for q in range(4):
                top = cotangent[q, rows, lanes].astype(f32)
                for s in range(4):
                    acc[4 * q + s] += fold(top * hin[s])
                acc[16 + q] += fold(top * branch)
                acc[20 + q] += fold(top * last)
            for s in range(4):
                acc[24 + s] += fold(hin[s] * back)
            acc[28] += fold(branch * back)

    total = jnp.sum(acc[...], axis=1)

    def top_hin(q, s):
        return total[4 * q + s : 4 * q + s + 1]

    def top_branch(q):
        return total[16 + q : 17 + q]

    def back_hin(s):
        return total[24 + s : 25 + s]

    back_branch = total[28:29]
    for s in range(4):
        out[s * 6 : s * 6 + 1] = jnp.zeros((1, 128), f32)
        for r in range(4):
            row = s * 6 + 1 + r
            out[row : row + 1] = weighted(
                [(mix.r[1][q][s], top_hin(q, r)) for q in range(4)]
                + [(mix.p[1][s], back_hin(r))]
            )
            row = 24 + s * 6 + 1 + r
            out[row : row + 1] = weighted(
                [(mix.r[0][r][q], top_hin(s, q)) for q in range(4)]
                + [(mix.g[0][r], top_branch(s))]
            )
        row = s * 6 + 5
        out[row : row + 1] = weighted(
            [(mix.r[1][q][s], top_branch(q)) for q in range(4)] + [(mix.p[1][s], back_branch)]
        )
        row = 24 + s * 6
        out[row : row + 1] = weighted(
            [(mix.r[0][s][q], back_hin(q)) for q in range(4)] + [(mix.g[0][s], back_branch)]
        )
        row = 24 + s * 6 + 5
        out[row : row + 1] = total[20 + s : 21 + s]


def out_streams_kernel(mix_ref, streams, branch1, branch2, out):
    mix = Mix(mix_ref)
    of_streams = [
        [sum(mix.r[1][s][q] * mix.r[0][q][r] for q in range(4)) for r in range(4)]
        for s in range(4)
    ]
    of_branch = [sum(mix.r[1][s][q] * mix.g[0][q] for q in range(4)) for s in range(4)]
    for c in range(4):
        rows = slice(32 * c, 32 * c + 32)
        hin = [streams[s, rows].astype(f32) for s in range(4)]
        for s in range(4):
            total = weighted(
                [(of_streams[s][r], hin[r]) for r in range(4)]
                + [(of_branch[s], branch1[rows]), (mix.g[1][s], branch2[rows])]
            )
            out[s, rows] = total.astype(bf16)


def near_lanes(values, near):
    return jnp.concatenate(
        [values[:, TILE * k + 128 * near : TILE * k + 128 * near + 128] for k in range(4)], axis=1
    )


def pair_back_kernel(places, own, far, weights, grad, pair):
    half = places[1]
    own = own.wait()
    for j in range(3):
        rows = slice(HD * j, HD * j + HD)
        pair[pl.ds(pl.multiple_of(128 * j + HD * half, HD), HD), :] = own[rows]
        pair[pl.ds(pl.multiple_of(128 * j + HD * (1 - half), HD), HD), :] = far[rows]
    total = contract(near_lanes(pair, 1), weights.wait()[...], ((0,), (0,)))
    grad[...] = total.astype(bf16).reshape(4, 128, 1024)


def pair_back_own_kernel(pair, weights, grad):
    total = contract(near_lanes(pair, 0), weights[...], ((0,), (0,)))
    grad[...] = total.astype(bf16).reshape(4, 128, 1024)


def narrow_tiles_kernel(
    places, pair, normed_own, normed_other, columns, context_own, context_other, out
):
    z, core = places[0], places[2]
    pair = pair.wait()
    tile = jnp.zeros((384, 1024), f32)
    for near, tokens in enumerate((normed_own, normed_other)):
        tokens = tokens.wait()[:, 0:128].reshape(512, 1024)
        tile = tile + contract(near_lanes(pair, near), tokens, ((1,), (0,)))
    for s in range(8):
        out[s, 0:384] = tile[:, 128 * s : 128 * s + 128].astype(bf16)
    tile = jnp.zeros((128, 1024), f32)
    for near, contexts in enumerate((context_own, context_other)):
        contexts = ready(contexts)
        for back in range(4):
            source = columns[2 * lax.rem(z - back + 4, 4) + lax.rem(core + near, 2)]
            tile = tile + contract(source, contexts[back], ((0,), (1,)))
    for s in range(8):
        out[s, 384:512] = tile[:, 128 * s : 128 * s + 128].astype(bf16)


def fold_kernel(blocks, *outs):
    start = 0
    for out in outs:
        rows = slice(start, start + out.shape[0])
        total = blocks[0, rows].astype(f32)
        for s in range(1, 8):
            total = total + blocks[s, rows].astype(f32)
        out[...] = total.astype(bf16)
        start += out.shape[0]


def fold_narrow_kernel(blocks, out):
    total = blocks[0].astype(f32)
    for s in range(1, 8):
        total = total + blocks[s].astype(f32)
    out[0:512] = total[0:512].astype(bf16)
    high, low = two_parts(total[512:513] + total[513:514])
    out[512:528] = jnp.concatenate([high, low, jnp.zeros((14, 128), bf16)], axis=0)


def add_narrow_kernel(own, far, out):
    total = own[...].astype(f32) + far[...].astype(f32)
    out[0:512] = total[0:512].astype(bf16)
    high, low = two_parts(total[512:513] + total[513:514])
    out[512:528] = jnp.concatenate([high, low, jnp.zeros((14, 128), bf16)], axis=0)


def member(places, own, other, index):
    back = lax.rem(places[0] - index % 4 + 4, 4)
    return jnp.where(places[2] == index // 4, own[back].astype(f32), other[back].astype(f32))


def finish_wide_kernel(places, own, other, gate_up, down, rows):
    for i in range(8):
        block = member(places, own, other, i)
        for s in range(8):
            for j in range(2):
                start = SLICE * j + PLACE * s
                unit = 8 * PIECE * s + PIECE * i
                rows[j, unit : unit + PIECE] = block[start : start + PIECE]
        for d in range(8):
            start = 2 * SLICE + PLACE * d
            down[PIECE * i : PIECE * i + PIECE, 128 * d : 128 * d + 128] = block[
                start : start + PIECE
            ]
    for j in range(2):
        for k in range(rows.shape[1] // 128):
            lanes = slice(128 * k, 128 * k + 128)
            gate_up[j, :, lanes] = rows[j, lanes].T


def finish_narrow_kernel(places, own, other, qkv, out, mix_grad):
    total = jnp.zeros((1, 128), f32)
    for i in range(8):
        block = member(places, own, other, i)
        total = total + (block[512:513] + block[513:514])
        for j in range(3):
            qkv[j, :, 128 * i : 128 * i + 128] = block[128 * j : 128 * j + 128].T
        out[:, 128 * i : 128 * i + 128] = block[384:512].T
    for m in range(2):
        for s in range(4):
            lane = m * 24 + s * 6
            mix_grad[m, s : s + 1, :] = total[:, lane : lane + 6]


def two_parts(values):
    high = values.astype(bf16)
    return high, (values - high.astype(f32)).astype(bf16)


def first_back_kernel(
    mix_ref, t0, t1, t2, t3, streams, cotangent, grad_second, sums, tiles, streams_grad, out, mix_rows
):
    mix = Mix(mix_ref)
    of_top = [
        [sum(mix.r[1][q][s] * mix.r[0][s][r] for s in range(4)) for q in range(4)]
        for r in range(4)
    ]
    of_back = [sum(mix.r[0][s][r] * mix.p[1][s] for s in range(4)) for r in range(4)]
    total = [jnp.zeros((1, 1024), f32) for _ in range(4)]
    cotangent, grad_second = cotangent.wait(), grad_second.wait()
    for c in range(4):
        rows = slice(32 * c, 32 * c + 32)
        hin = [streams[s, rows].astype(f32) for s in range(4)]
        top = [cotangent[s, rows].astype(f32) for s in range(4)]
        normed, inverse = normalize(weighted([(mix.p[0][s], hin[s]) for s in range(4)]))
        grad = (t0[rows] + t1[rows].astype(f32)) + (t2[rows].astype(f32) + t3[rows].astype(f32))
        back1 = norm_back(grad, normed, inverse)
        back2 = grad_second[rows]
        for r in range(4):
            value = weighted(
                [(of_top[r][q], top[q]) for q in range(4)]
                + [(of_back[r], back2), (mix.p[0][r], back1)]
            )
            streams_grad[r, rows] = value.astype(bf16)
            total[r] = total[r] + jnp.sum(hin[r] * back1, axis=0, keepdims=True)
    mix_rows[0:48] = sums.wait()[...]
    mix_rows[48:] = jnp.zeros((80, 128), f32)
    for s in range(4):
        row = sum(total[s][:, 128 * k : 128 * k + 128] for k in range(8))
        mix_rows[s * 6 : s * 6 + 1] = row
    high, low = two_parts(jnp.sum(mix_rows[...].T, axis=0, keepdims=True))
    rows = jnp.concatenate([high, low, jnp.zeros((14, 128), bf16)], axis=0)
    tiles = tiles.wait()
    for s in range(8):
        out[s, 0:512] = tiles[s]
        out[s, 512:528] = rows


def split_kernel(source, own, other):
    own[...] = source[0]
    other[...] = source[1]


def copy_kernel(source, out):
    out[...] = source[...]


def add4_kernel(one, two, three, four, out):
    out[...] = (one[...] + two[...]) + (three[...] + four[...])


def add2_kernel(one, two, out):
    out[...] = (one[...].astype(f32) + two[...].astype(f32)).astype(out.dtype)


def shards(
    streams, segments, stream_mix, qkv_weight, out_weight, gate_up_weight, down_weight, cotangent
):
    kept_arrays.arrays.clear()
    z, half, core = lax.axis_index("z"), lax.axis_index("xh"), lax.axis_index("co")
    team, row = lax.axis_index(TEAM), lax.axis_index(SHARD)
    width = streams.shape[3]
    ff = down_weight.shape[0]
    places = (jnp.stack([z, half, core, row, team]).astype(jnp.int32), smem)
    mix = (stream_mix, smem)
    streams, cotangent, segments = streams[0], cotangent[0], (segments, vmem)
    token = ((128, width), bf16)
    token4 = ((4, 128, width), bf16)

    def v(*values):
        return [(value, vmem) for value in values]

    def h(*values):
        return [(value, "hbm") for value in values]

    def l(*values):
        return [(value, "late") for value in values]

    def stack(values, parts, name, us=1, order=(), beside=(), in_hbm=False, place="hbm"):
        (result,) = call(
            stack_kernel,
            [((4,) + values.shape, bf16, place)],
            (h(values) if in_hbm else v(values)) + v(*parts),
            name,
            us,
            order=order,
            beside=beside,
        )
        return result

    (weights,) = call(
        pick_kernel,
        [((128, 896 + 2 * SLICE), bf16, "hbm")],
        [places] + l(out_weight, down_weight, gate_up_weight),
        "pick",
        4,
    )
    near_weights = lax.all_gather(weights, "y", axis=0, tiled=True)
    far_weights = lax.all_gather(shift(weights, "xl", 1), "y", axis=0, tiled=True)

    (normed1,) = call(
        first_norm_kernel,
        [((144, width), bf16)],
        [mix] + h(streams) + [segments],
        "first_norm",
        3,
        order=[weights],
    )
    (qkv_blocks,) = call(
        pick_heads_kernel,
        [((8, 3, 128, 128), bf16, "hbm")],
        [places, (qkv_weight, raw)],
        "pick_heads",
        2,
        [pltpu.VMEM((3, 128, 128), bf16)],
        beside=[normed1],
    )
    qkv_blocks = lax.all_to_all(qkv_blocks, SHARD, 0, 0, tiled=True)
    normed1_z = z_issue(normed1)
    normed1_own = stack(normed1, normed1_z, "stack_normed1", 4)
    normed1_other = shift(normed1_own, "co", 1)
    freq = rope_base ** (-(jnp.arange(32, dtype=f32) * 2.0) / HD)
    back, near, place = jnp.arange(4), jnp.arange(2), jnp.arange(128)
    positions = (
        512 * ((z - back[None, :, None, None] + 4) % 4)
        + 256 * ((half + near[:, None, None, None]) % 2)
        + 128 * ((core + near[None, None, :, None]) % 2)
        + place[None, None, None, :]
    ).reshape(2, 1, 1024)
    angle = positions.astype(f32) * freq[None, :, None]
    cosine, sine = jnp.cos(angle), jnp.sin(angle)

    (pair_weights,) = call(
        turn_heads_kernel, [((384, width), bf16, "hbm")], v(qkv_blocks), "turn_heads", 1
    )
    kept, sent = call(
        project_kernel,
        [((208, 1024), bf16, "vmem"), ((208, 1024), bf16, "vmem")],
        [places] + l(normed1_own, normed1_other) + h(pair_weights) + v(cosine, sine),
        "project",
        4,
    )
    received = shift(sent, "xh", 1)
    (grad_branch2,) = call(
        grad_branch2_kernel,
        [token],
        [mix] + h(cotangent) + [segments],
        "grad_branch2",
        0,
        order=[kept],
    )
    grad2_z = z_issue(grad_branch2)

    qkv, context_blocks, context_wide, logsum, edges = call(
        attend_kernel,
        [
            ((2, 192, 1024), bf16, "hbm"),
            ((16, HD, 128), bf16, "hbm"),
            ((2, HD, 1024), f32, "hbm"),
            ((2, 8, 1024), f32, "hbm"),
            ((4,), jnp.int32),
        ],
        [places] + h(kept) + v(received),
        "attend",
        12,
        beside=[grad_branch2],
    )
    context_mine = lax.all_to_all(context_blocks, CTX, 0, 0, tiled=True)

    grad2_own = stack(grad_branch2, grad2_z, "stack_grad2", 1, [context_blocks])
    grad2_other = shift(grad2_own, "co", 1)
    (out_own,) = call(
        unpack_out_kernel,
        [((width, 512), bf16, "vmem")],
        [places, (near_weights, ("late", 0, 512)), (far_weights, ("late", 0, 512))],
        "unpack_out",
        3,
        order=[grad2_own],
    )
    out_other = shift(out_own, "co", 1)
    context, branch_half = call(
        post_attend_own_kernel,
        [((width, 128), bf16, "vmem"), ((128, 512), f32, "vmem")],
        v(context_mine) + h(out_own),
        "post_attend_own",
        15,
    )
    normed2, branch1 = call(
        post_attend_kernel,
        [token, ((128, width), f32, "hbm")],
        [places, mix]
        + h(context)
        + v(branch_half)
        + l(out_other, streams)
        + [segments],
        "post_attend",
        3,
    )
    normed2_z = z_issue(normed2)
    inner = ("late", 512, 896 + 2 * SLICE)
    gu_all, down = call(
        unpack_kernel,
        [((width, 2 * SLICE), bf16, "vmem"), ((SLICE, width), bf16, "vmem")],
        [places, (near_weights, inner), (far_weights, inner)],
        "unpack",
        4,
        order=[out_own],
    )
    normed2_own = stack(normed2, normed2_z, "stack_normed2", order=[down])
    normed2_other = shift(normed2_own, "co", 1)
    acts = [token4 + ("vmem",)] + [((512, SLICE), bf16, "hbm")] * 3
    grad_own, hidden_own, gate_own, up_own = call(
        feed_forward_kernel,
        acts,
        l(normed2_own, grad2_own, gu_all, down),
        "feed_forward_own",
        5,
    )
    grad_other, hidden_other, gate_other, up_other = call(
        feed_forward_kernel,
        acts,
        l(normed2_other, grad2_other, gu_all, down),
        "feed_forward_other",
        5,
        order=[hidden_own],
    )

    def core_add(own, other, name, order, beside=(), own_in_hbm=False):
        return call(
            core_add_kernel,
            [((128, width), f32, "vmem")] + [token] * 3,
            (h(own) if own_in_hbm else v(own)) + v(shift(other, "co", 1)),
            name,
            1,
            order=order,
            beside=beside,
        )

    def z_terms(terms):
        return [terms[0]] + [shift(term, "z", -k) for k, term in enumerate(terms[1:], 1)]

    half_own, half_other, context = call(
        branch2_kernel,
        [token4 + ("vmem",), token4 + ("vmem",), ((width, 128), bf16, "vmem")],
        h(hidden_own, hidden_other, down, context),
        "branch2",
        3,
        order=[hidden_other],
    )
    terms = core_add(grad_own, grad_other, "core_add_second", [half_own])
    grad_normed2 = z_terms(terms)
    context_z = z_issue(context)

    grad_second, grad_columns, grad_context = call(
        second_back_kernel,
        [
            ((128, width), f32, "hbm"),
            ((8, 128, 128), bf16, "hbm"),
            ((16, HD, 128), bf16, "hbm"),
        ],
        [places, mix]
        + h(grad_normed2[0])
        + v(*grad_normed2[1:])
        + h(streams, branch1)
        + l(cotangent)
        + [segments] + l(out_own, out_other),
        "second_back",
        5,
        [pltpu.VMEM((128, width), bf16), pltpu.VMEM((width, 128), f32)],
    )
    grad_context = lax.all_to_all(grad_context, CTX, 0, 0, tiled=True)

    (wide_tiles,) = call(
        wide_tiles_kernel,
        [((8, 3 * SLICE, 128), bf16, "hbm")],
        [places] + l(
            gate_own, normed2_own, gate_other, normed2_other, up_own, up_other,
            hidden_own, grad2_own, hidden_other, grad2_other,
        ),
        "wide_tiles",
        7,
        order=[grad_second],
    )
    wide_mine = lax.psum_scatter(wide_tiles, "y", scatter_dimension=0, tiled=True)

    terms = core_add(half_own, half_other, "core_add_branch2", [wide_tiles], own_in_hbm=True)
    branch2 = z_terms(terms)
    grads_own, grads_far, columns = call(
        attend_back_kernel,
        [((192, 1024), bf16, "hbm"), ((192, 1024), bf16, "vmem"), ((8, 128, 128), bf16, "hbm")],
        [places, (edges, smem)]
        + h(qkv, context_wide, logsum)
        + v(grad_context, cosine, sine)
        + h(grad_columns),
        "attend_back",
        40,
        [
            pltpu.VMEM((8, HD, TILE), f32),
            pltpu.VMEM((8, HD, TILE), f32),
            pltpu.VMEM((2, 192, 1024), bf16),
        ],
        [terms[0]],
    )
    received = shift(grads_far, "xh", 1)
    columns = lax.all_to_all(columns, ("z", "co"), 0, 0, tiled=True)
    sums, branch2 = call(
        mix_sums_kernel,
        [((48, 128), f32, "vmem"), ((128, width), f32, "hbm")],
        [mix]
        + h(branch2[0])
        + v(*branch2[1:])
        + h(streams, cotangent, branch1, grad_second)
        + [segments],
        "mix_sums",
        7,
        [pltpu.VMEM((32, 8, 128), f32)],
        [grads_own],
        context_z,
    )
    context_own = stack(context, context_z, "stack_context", 1, [sums], in_hbm=True, place="vmem")
    context_other = shift(context_own, "co", 1)
    wide_type = ((3 * SLICE, 128), bf16)
    wide_mine, wide_far = call(
        split_kernel, [wide_type, wide_type], h(wide_mine), "split_wide", 1, order=[context_own]
    )
    wide_far = shift(wide_far, "xl", 1)
    grad_other, pair = call(
        pair_back_kernel,
        [token4 + ("vmem",), ((384, 1024), bf16, "vmem")],
        [places] + l(grads_own) + v(received) + l(pair_weights),
        "pair_back",
        4,
        order=[context_own],
        beside=[columns, wide_mine],
    )
    (grad_own,) = call(
        pair_back_own_kernel, [token4 + ("vmem",)], h(pair, pair_weights), "pair_back_own", 3
    )
    terms = core_add(grad_own, grad_other, "core_add_first", [])
    grad_normed1 = z_terms(terms)

    (narrow_tiles,) = call(
        narrow_tiles_kernel,
        [((8, 512, 128), bf16, "vmem")],
        [places]
        + l(pair, normed1_own, normed1_other)
        + v(columns)
        + l(context_own)
        + v(context_other),
        "narrow_tiles",
        6,
        order=[terms[0]],
    )
    narrow_order = narrow_tiles
    (wide_rows,) = call(
        add2_kernel, [wide_type], v(wide_mine, wide_far), "add_wide_xl", 1, order=[narrow_order], beside=grad_normed1[1:]
    )
    wide_far = shift(wide_rows, "xh", 1)
    streams_grad, narrow_tiles = call(
        first_back_kernel,
        [token4 + ("hbm",), ((8, 528, 128), bf16, "hbm")],
        [mix]
        + h(grad_normed1[0])
        + v(*grad_normed1[1:])
        + h(streams)
        + l(cotangent, grad_second, sums, narrow_tiles),
        "first_back",
        6,
        [pltpu.VMEM((128, 128), f32)],
    )
    narrow_tiles = lax.all_to_all(narrow_tiles, SHARD, 0, 0, tiled=True)

    (wide_rows,) = call(
        add2_kernel, [wide_type], v(wide_rows, wide_far), "add_wide", 1, order=[streams_grad]
    )
    wide_z = z_issue(wide_rows)
    (out_streams,) = call(
        out_streams_kernel,
        [token4 + ("hbm",)],
        [mix] + h(streams, branch1, branch2),
        "out_streams",
        8,
        beside=[wide_rows],
    )
    narrow_type = [((528, 128), bf16)]
    (mine,) = call(fold_narrow_kernel, narrow_type, v(narrow_tiles), "fold_narrow", 1, order=[out_streams])
    narrow_far = shift(mine, "xh", 1)
    wide_own = stack(wide_rows, wide_z, "stack_wide", 1, beside=[mine])
    wide_other = shift(wide_own, "co", 1)
    (narrow_rows,) = call(
        add_narrow_kernel, narrow_type, v(mine, narrow_far), "add_narrow", 1, order=[wide_own]
    )
    narrow_z = z_issue(narrow_rows)
    gate_up_grad, down_grad = call(
        finish_wide_kernel,
        [((2, 128, 8 * ff), f32, "hbm"), ((ff, width), f32, "hbm")],
        [places] + h(wide_own) + v(wide_other),
        "finish_wide",
        5,
        [pltpu.VMEM((2, 8 * ff, 128), f32)],
        beside=[narrow_rows],
    )
    narrow_own = stack(narrow_rows, narrow_z, "stack_narrow", 1, [down_grad])
    narrow_other = shift(narrow_own, "co", 1)
    qkv_grad, out_grad, mix_grad = call(
        finish_narrow_kernel,
        [((3, 128, width), f32, "hbm"), ((128, width), f32, "hbm"), ((2, 4, 6), f32)],
        [places] + h(narrow_own) + v(narrow_other),
        "finish_narrow",
        3,
    )
    return (
        out_streams[None], streams_grad[None], qkv_grad, out_grad, gate_up_grad, down_grad, mix_grad,
    )


def solution(mesh):
    fine = Mesh(
        np.asarray(mesh.devices).reshape([n for _, n in AXES]), tuple(name for name, _ in AXES)
    )
    in_specs = (
        P(SHARD, None, CTX, None),
        P(SHARD, CTX),
        P(),
        P(None, SHARD, None),
        P(SHARD, None),
        P(None, SHARD, None),
        P(SHARD, None),
        P(SHARD, None, CTX, None),
    )
    out_specs = (
        P(SHARD, None, CTX, None),
        P(SHARD, None, CTX, None),
        P(None, SHARD, None),
        P(SHARD, None),
        P(None, SHARD, None),
        P(SHARD, None),
        P(),
    )
    return jax.shard_map(shards, mesh=fine, in_specs=in_specs, out_specs=out_specs, check_vma=False)
```

```python
import jax
import jax.numpy as jnp
import numpy as np
from jax import lax
from jax.experimental import pallas as pl
from jax.experimental.pallas import tpu as pltpu
from jax.sharding import Mesh
from jax.sharding import PartitionSpec as P

HD = 64
TILE = 256
VMEM = 24 * 1024 * 1024
COST = 1.1e9
PIECE = 44
PLACE = 48
SLICE = 8 * PLACE
eps = 1e-05
rope_base = 1000000.0
neg_big = -1e30
bf16 = jnp.bfloat16
f32 = jnp.float32
smem = pl.BlockSpec(memory_space=pltpu.SMEM)
vmem = pl.BlockSpec(memory_space=pltpu.VMEM)
anywhere = pl.BlockSpec(memory_space=pl.ANY)
hbm = pl.BlockSpec(memory_space=pltpu.HBM)
raw = pl.BlockSpec(memory_space=pltpu.HBM)

AXES = (("z", 4), ("xh", 2), ("co", 2), ("xl", 2), ("y", 4))
SIZE = dict(AXES)
CTX = ("z", "xh", "co")
SHARD = ("xl", "y")
TEAM = ("co", "z")
HEAD_OF = [8 * (c % 2) + 2 * (c // 4) + (c // 2) % 2 for c in range(16)]


class Kept:
    def __init__(self):
        self.arrays = []

    def add(self, array):
        self.arrays.append(array)
        return array

    def __contains__(self, array):
        return any(array is other for other in self.arrays)


kept_arrays = Kept()


def shift(values, axis, amount):
    count = SIZE[axis]
    moved = lax.ppermute(values, axis, [(i, (i + amount) % count) for i in range(count)])
    if axis == "co" and values in kept_arrays:
        kept_arrays.add(moved)
    return moved


def z_issue(values):
    return [shift(values, "z", k) for k in range(1, 4)]


class Late:
    def __init__(self, copy, ref):
        self.copy, self.ref = copy, ref

    def wait(self):
        if self.copy is not None:
            self.copy.wait()
        return self.ref


def call(kernel, outs, ins, name, us, scratch=(), order=(), beside=()):
    known = (smem, vmem, raw)
    stays = [value in kept_arrays and place not in (smem, raw) for value, place in ins]
    extra_ins = len(order) + len(beside)
    ends = len(ins), len(ins) + extra_ins, len(ins) + extra_ins + len(outs)
    near = [k for k, (_, place) in enumerate(ins) if place not in known and not stays[k]]
    far = [k for k, out in enumerate(outs) if len(out) > 2 and out[2] == "hbm"]

    def part(k):
        value, place = ins[k]
        if isinstance(place, tuple):
            return value.shape[:-1] + (place[2] - place[1],)
        return value.shape

    def body(*refs):
        given, results, rest = list(refs[: ends[0]]), list(refs[ends[1] : ends[2]]), refs[ends[2] :]
        rest, sems = (rest[:-1], rest[-1]) if near or far else (rest, None)
        loaded = rest[len(scratch) : len(scratch) + len(near)]
        staged = rest[len(scratch) + len(near) :]
        for k, (_, place) in enumerate(ins):
            if stays[k] and place == "late":
                given[k] = Late(None, given[k])
        copies, waits = [], []
        for j, (k, ref) in enumerate(zip(near, loaded)):
            source, place = given[k], ins[k][1]
            if isinstance(place, tuple):
                source = source.at[..., place[1] : place[2]]
            copies.append(pltpu.make_async_copy(source, ref, sems.at[j]))
            if (place[0] if isinstance(place, tuple) else place) == "hbm":
                waits.append(copies[-1])
                given[k] = ref
            else:
                given[k] = Late(copies[-1], ref)
        for copy in copies:
            copy.start()
        for copy in waits:
            copy.wait()
        copies = []
        for j, (k, ref) in enumerate(zip(far, staged)):
            copies.append(pltpu.make_async_copy(ref, results[k], sems.at[len(near) + j]))
            results[k] = ref
        kernel(*given, *results, *rest[: len(scratch)])
        for copy in copies:
            copy.start()
        for copy in copies:
            copy.wait()

    extra = [pltpu.VMEM(part(k), ins[k][0].dtype) for k in near]
    extra += [pltpu.VMEM(outs[k][0], outs[k][1]) for k in far]
    if near or far:
        extra.append(pltpu.SemaphoreType.DMA((len(near) + len(far),)))

    def in_hbm(value):
        return pltpu.with_memory_space_constraint(value, pltpu.HBM)

    def out_type(out):
        if len(out) > 2 and out[2] == "vmem":
            return pltpu.VMEM(out[0], out[1])
        if len(out) > 2:
            return pltpu.HBM(out[0], out[1])
        return jax.ShapeDtypeStruct(out[0], out[1])

    def in_vmem(value):
        return pltpu.with_memory_space_constraint(value, pltpu.VMEM)

    def spec(k):
        return vmem if stays[k] else ins[k][1] if ins[k][1] in known else hbm

    def placed(k):
        value, place = ins[k]
        return in_vmem(value) if stays[k] else value if place in (smem, vmem) else in_hbm(value)

    results = pl.pallas_call(
        body,
        out_shape=tuple(out_type(out) for out in outs),
        in_specs=[spec(k) for k in range(len(ins))]
        + [anywhere if value in kept_arrays else hbm for value in order]
        + [anywhere] * len(beside),
        out_specs=tuple(
            hbm if k in far else smem if out[1] == jnp.int32 else vmem
            for k, out in enumerate(outs)
        ),
        scratch_shapes=list(scratch) + extra,
        compiler_params=pltpu.CompilerParams(vmem_limit_bytes=VMEM),
        cost_estimate=pl.CostEstimate(
            flops=int(us * COST), bytes_accessed=0, transcendentals=0
        ),
        name=name,
    )(
        *[placed(k) for k in range(len(ins))],
        *[value if value in kept_arrays else in_hbm(value) for value in order],
        *beside,
    )
    for out, result in zip(outs, results):
        if len(out) > 2 and out[2] == "vmem":
            kept_arrays.add(result)
    return results


def contract(left, right, dims):
    return lax.dot_general(left, right, (dims, ((), ())), preferred_element_type=f32)


def normalize(values):
    centered = values - jnp.mean(values, axis=-1, keepdims=True)
    inverse = lax.rsqrt(jnp.mean(centered * centered, axis=-1, keepdims=True) + eps)
    return (centered * inverse, inverse)


def norm_back(grad, normed, inverse):
    return inverse * (
        grad
        - jnp.mean(grad, axis=-1, keepdims=True)
        - normed * jnp.mean(grad * normed, axis=-1, keepdims=True)
    )


def weighted(terms):
    total = None
    for weight, values in terms:
        part = weight * values
        total = part if total is None else total + part
    return total


def live_column(segments):
    wide = jnp.broadcast_to((segments[...] > 0).astype(f32), (128, 128))
    return wide.T[:, 0:1]


class Mix:
    def __init__(self, ref):
        self.p = [[ref[m, s, 0] for s in range(4)] for m in range(2)]
        self.r = [[[ref[m, s, 1 + r] for r in range(4)] for s in range(4)] for m in range(2)]
        self.g = [[ref[m, s, 5] for s in range(4)] for m in range(2)]

    def second_of_streams(self, r):
        return sum(self.p[1][s] * self.r[0][s][r] for s in range(4))

    def second_of_branch(self):
        return sum(self.p[1][s] * self.g[0][s] for s in range(4))


def core_add_kernel(own, received, first, *rest):
    first[...] = own[0].astype(f32) + received[0].astype(f32)
    for k, target in enumerate(rest, 1):
        target[...] = (own[k].astype(f32) + received[k].astype(f32)).astype(bf16)


def first_norm_kernel(mix_ref, streams, segments, out):
    mix = Mix(mix_ref)
    for c in range(4):
        rows = slice(32 * c, 32 * c + 32)
        first = weighted([(mix.p[0][s], streams[s, rows].astype(f32)) for s in range(4)])
        out[rows] = normalize(first)[0].astype(bf16)
    out[128:144] = jnp.zeros((16, 1024), bf16)
    out[128:144, 0:128] = jnp.broadcast_to(segments[...].astype(f32), (16, 128)).astype(bf16)


def pick_heads_kernel(places, weights, out, block):
    pltpu.sync_copy(
        weights.at[:, :, pl.ds(pl.multiple_of(places[4] * 128, 128), 128)], block
    )
    for s in range(8):
        out[s] = block[...]


def pieces(d):
    start, place, result = PLACE * d, 0, []
    while place < PLACE:
        count = min(PLACE - place, 128 - start % 128)
        result.append((place, start // 128, start % 128, count))
        start, place = start + count, place + count
    return result


def pick_kernel(places, out_weight, down, gate_up, wide):
    team, core = places[4], places[2]
    own, _ = halves(core)
    wide[:, 0:512] = out_weight.wait()[:, own]
    start = jnp.minimum(team * PIECE // 16 * 16, 8 * PIECE - 64)
    place = lax.broadcasted_iota(jnp.int32, (PLACE, 1), 0)
    wanted = jnp.where(place < PIECE, place + (team * PIECE - start), -1)
    unit = lax.broadcasted_iota(jnp.int32, (1, 64), 1)
    picked = jnp.where(unit == wanted, 1.0, 0.0).astype(bf16)
    down = down.wait()[pl.ds(pl.multiple_of(start, 16), 64)]
    rows = contract(picked, down, ((1,), (0,))).astype(bf16)
    for d in range(8):
        for place, tile, start, count in pieces(d):
            lanes = slice(512 + 128 * tile, 512 + 128 * tile + 128)
            wide[start : start + count, lanes] = rows[
                place : place + count, 128 * d : 128 * d + 128
            ]
    units = gate_up.ref.shape[2] // 2
    unit = lax.broadcasted_iota(jnp.int32, (units, 1), 0)
    place = lax.broadcasted_iota(jnp.int32, (1, SLICE // 2), 1)
    piece = lax.rem(place, PLACE)
    wanted = (place // PLACE) * (8 * PIECE) + team * PIECE + piece
    wanted = jnp.where(piece < PIECE, wanted, -1)
    picked = jnp.where(unit == wanted, 1.0, 0.0).astype(bf16)
    gate_up = gate_up.wait()
    for j in range(2):
        columns = [
            contract(gate_up[j, :, units * k : units * k + units], picked, ((1,), (0,))).astype(bf16)
            for k in range(2)
        ]
        wide[:, 896 + SLICE * j : 896 + SLICE * j + SLICE] = jnp.concatenate(columns, axis=1)


def halves(core):
    own = pl.ds(pl.multiple_of(core * 512, 512), 512)
    other = pl.ds(pl.multiple_of((1 - core) * 512, 512), 512)
    return own, other


def pair_weights_kernel(near, far, out):
    out[0] = near[...]
    out[1] = far[...]


def unpack_out_kernel(places, weights, out):
    weights = weights.wait()
    for part in range(2):
        for y in range(4):
            s = 4 * lax.rem(places[3] // 4 + part, 2) + y
            out[pl.ds(pl.multiple_of(128 * s, 128), 128)] = weights[2 * y + part]


def unpack_kernel(places, weights, gate_up, down):
    weights = weights.wait()
    for part in range(2):
        for y in range(4):
            s = 4 * lax.rem(places[3] // 4 + part, 2) + y
            block = weights[2 * y + part]
            gate_up[pl.ds(pl.multiple_of(128 * s, 128), 128)] = block[:, 384:]
            for d in range(8):
                for place, tile, start, count in pieces(d):
                    row = pl.multiple_of(PLACE * s + place, 16)
                    down[pl.ds(row, count), 128 * d : 128 * d + 128] = block[
                        start : start + count, 128 * tile : 128 * tile + 128
                    ]


def grad_branch2_kernel(mix_ref, cotangent, segments, out):
    mix = Mix(mix_ref)
    live = live_column(segments)
    for c in range(4):
        rows = slice(32 * c, 32 * c + 32)
        total = weighted([(mix.g[1][s], cotangent[s, rows].astype(f32)) for s in range(4)])
        out[rows] = (live[rows] * total).astype(bf16)


def turn(values, cosine, sine):
    one, two = values[:32], values[32:]
    return jnp.concatenate([one * cosine - two * sine, two * cosine + one * sine], axis=0)


def turn_back(grad, cosine, sine):
    one, two = grad[:32], grad[32:]
    return jnp.concatenate([one * cosine + two * sine, two * cosine - one * sine], axis=0)


def turn_heads_kernel(weights, out):
    for s in range(8):
        for j in range(3):
            out[128 * j : 128 * j + 128, 128 * s : 128 * s + 128] = weights[s, j].T


def stack_kernel(first, second, third, fourth, out):
    for k, part in enumerate((first, second, third, fourth)):
        out[k] = part[...]


def project_kernel(places, own, other, wide, cosine, sine, kept, sent):
    half = places[1]

    def rows(head):
        return [wide[pl.ds(pl.multiple_of(128 * j + HD * head, HD), HD), :] for j in range(3)]

    mine = jnp.concatenate(rows(half) + rows(1 - half), axis=0)
    for near, tokens in enumerate((own, other)):
        tokens = tokens.wait()
        blocks = contract(mine, tokens[:, 0:128].reshape(512, 1024), ((1,), (1,)))
        for back in range(4):
            lanes = slice(back * TILE + near * 128, back * TILE + near * 128 + 128)
            block = blocks[:, 128 * back : 128 * back + 128]
            segs = tokens[back, 128:144, 0:128]
            cos, sin = cosine[0, :, lanes], sine[0, :, lanes]
            for target, base in ((kept, 0), (sent, 192)):
                query = turn(block[base : base + 64], cos, sin).astype(bf16)
                target[0:64, lanes] = (query.astype(f32) * 0.125).astype(bf16)
                target[64:128, lanes] = turn(block[base + 64 : base + 128], cos, sin).astype(bf16)
                target[128:192, lanes] = block[base + 128 : base + 192].astype(bf16)
                target[192:208, lanes] = segs


def pair_lanes(places, pair):
    back = lax.rem(places[0] - pair + 4, 4)
    return pl.ds(pl.multiple_of(back * TILE, TILE), TILE)


def in_order(places):
    return places[1], 1 - places[1]


def both(places, ref, rows, lanes):
    return jnp.concatenate([ref[part, rows, lanes] for part in in_order(places)], axis=1)


def pair_positions(places, pair, axis):
    local = lax.broadcasted_iota(jnp.int32, (TILE, 1) if axis == 0 else (1, TILE), axis)
    first = (local + places[2] * 128) % TILE + 2 * TILE * pair
    return jnp.concatenate([first, first + TILE], axis=axis)


def document_start(edges, place):
    start = jnp.zeros_like(place)
    for edge in edges:
        start = jnp.where(place >= edge, edge, start)
    return start


def pairs_of(edges, pair):
    return pair - document_start(edges, 2 * TILE * pair) // (2 * TILE) + 1


def attend_kernel(places, kept, received, qkv, context, context_wide, logsum, edges_out):
    core = places[2]
    qkv[0] = kept[0:192]
    qkv[1] = received[0:192]
    seg_own = kept[192:208].astype(f32)
    seg_far = received[192:208].astype(f32)
    edges = []
    for d in range(1, 5):
        count = jnp.float32(0)
        for seg in (seg_own, seg_far):
            inside = (seg > 0.5) & (seg < d + 0.5)
            count = count + jnp.sum(jnp.where(inside, 0.0625, 0.0))
        edge = count.astype(jnp.int32)
        edges_out[d - 1] = edge
        edges.append(edge)

    @pl.loop(0, 4)
    def _(q_pair):
        q_lanes = pair_lanes(places, q_pair)
        query = both(places, qkv, slice(0, HD), q_lanes)
        q_pos = pair_positions(places, q_pair, 1)
        start = document_start(edges, q_pos)

        def scores(key, pos, lanes):
            return jnp.where(pos >= start[:, lanes], contract(key, query[:, lanes], ((0,), (0,))), neg_big)

        def mix_values(value, weights):
            return contract(value, weights.astype(bf16), ((1,), (0,)))

        def step(back, carry):
            top, total, mixed = carry
            k_lanes = pair_lanes(places, q_pair - back)
            key = both(places, qkv, slice(HD, 2 * HD), k_lanes)
            raw = scores(key, pair_positions(places, q_pair - back, 0), slice(0, 2 * TILE))
            new_top = jnp.maximum(top, jnp.max(raw, axis=0, keepdims=True))
            weights = jnp.exp(raw - new_top)
            fade = jnp.exp(top - new_top)
            total = total * fade + jnp.sum(weights, axis=0, keepdims=True)
            value = both(places, qkv, slice(2 * HD, 3 * HD), k_lanes)
            return new_top, total, mixed * fade + mix_values(value, weights)

        late = slice(TILE, 2 * TILE)
        k_pos = pair_positions(places, q_pair, 0)
        seen = []
        for k, (part, lanes) in enumerate(zip(in_order(places), (slice(0, 2 * TILE), late))):
            pos = k_pos[k * TILE : k * TILE + TILE]
            raw = scores(qkv[part, HD : 2 * HD, q_lanes], pos, lanes)
            seen.append(jnp.where(pos <= q_pos[:, lanes], raw, neg_big))
        top = jnp.max(seen[0], axis=0, keepdims=True)
        top_late = jnp.maximum(top[:, late], jnp.max(seen[1], axis=0, keepdims=True))
        top = jnp.concatenate([top[:, :TILE], top_late], axis=1)
        weights = [jnp.exp(seen[0] - top), jnp.exp(seen[1] - top_late)]
        total, total_late = [jnp.sum(part, axis=0, keepdims=True) for part in weights]
        mixed, mixed_late = [
            mix_values(qkv[part, 2 * HD : 3 * HD, q_lanes], weights[k])
            for k, part in enumerate(in_order(places))
        ]
        total = jnp.concatenate([total[:, :TILE], total[:, late] + total_late], axis=1)
        mixed = jnp.concatenate([mixed[:, :TILE], mixed[:, late] + mixed_late], axis=1)
        top, total, mixed = lax.fori_loop(1, pairs_of(edges, q_pair), step, (top, total, mixed))
        mixed = mixed / total
        lasting = jnp.broadcast_to(top + jnp.log(total), (8, 2 * TILE))
        low = mixed.astype(bf16)
        for k, part in enumerate(in_order(places)):
            lanes = slice(k * TILE, k * TILE + TILE)
            context_wide[part, :, q_lanes] = mixed[:, lanes]
            logsum[part, :, q_lanes] = lasting[:, lanes]
            for near in range(2):
                place = 4 * q_pair + 2 * k + (core if near == 0 else 1 - core)
                context[place] = low[:, k * TILE + 128 * near : k * TILE + 128 * near + 128]


def attend_back_kernel(
    places, edge_ref, qkv, context_wide, logsum, grad_context, cosine, sine, columns,
    grads_own, grads_far, columns_out, dk_acc, dv_acc, grads,
):
    core = places[2]
    columns_out[...] = columns[...]
    edges = [edge_ref[d] for d in range(4)]

    @pl.loop(0, 4)
    def _(q_pair):
        q_lanes = pair_lanes(places, q_pair)
        query = both(places, qkv, slice(0, HD), q_lanes)
        q_pos = pair_positions(places, q_pair, 1)
        start = document_start(edges, q_pos)
        norm = both(places, logsum, slice(0, 1), q_lanes)
        blocks = []
        for place in (core, 1 - core, 2 + core, 3 - core):
            blocks.append(grad_context[4 * q_pair + place])
        grad = jnp.concatenate(blocks, axis=1)
        delta = jnp.sum(
            grad.astype(f32) * both(places, context_wide, slice(0, HD), q_lanes),
            axis=0, keepdims=True,
        )

        def back_tile(part, k_lanes, k_pos, lanes, own):
            key = qkv[part, HD : 2 * HD, k_lanes]
            value = qkv[part, 2 * HD : 3 * HD, k_lanes]
            raw = contract(key, query[:, lanes], ((0,), (0,)))
            dprobs = contract(value, grad[:, lanes], ((0,), (0,)))
            seen = k_pos >= start[:, lanes]
            if own:
                seen = seen & (k_pos <= q_pos[:, lanes])
            probs = jnp.exp(jnp.where(seen, raw, neg_big) - norm[:, lanes])
            draw = (probs * (dprobs - delta[:, lanes])).astype(bf16)
            dv = contract(grad[:, lanes], probs.astype(bf16), ((1,), (1,)))
            dk = contract(query[:, lanes], draw, ((1,), (1,)))
            dv_acc[part, :, k_lanes] = dv if own else dv_acc[part, :, k_lanes] + dv
            dk_acc[part, :, k_lanes] = dk if own else dk_acc[part, :, k_lanes] + dk
            return contract(key, draw, ((1,), (0,)))

        def step(back, dq):
            k_lanes = pair_lanes(places, q_pair - back)
            k_pos = pair_positions(places, q_pair - back, 0)
            for k, part in enumerate(in_order(places)):
                pos = k_pos[k * TILE : k * TILE + TILE]
                dq = dq + back_tile(part, k_lanes, pos, slice(0, 2 * TILE), False)
            return dq

        early, late = in_order(places)
        k_pos = pair_positions(places, q_pair, 0)
        dq = back_tile(early, q_lanes, k_pos[:TILE], slice(0, 2 * TILE), True)
        dq_late = back_tile(late, q_lanes, k_pos[TILE:], slice(TILE, 2 * TILE), True)
        dq = jnp.concatenate([dq[:, :TILE], dq[:, TILE:] + dq_late], axis=1)
        dq = lax.fori_loop(1, pairs_of(edges, q_pair), step, dq) * 0.125
        for k, part in enumerate(in_order(places)):
            cos, sin = cosine[part, :, q_lanes], sine[part, :, q_lanes]
            lanes = slice(k * TILE, k * TILE + TILE)
            grads[part, 0:HD, q_lanes] = turn_back(dq[:, lanes], cos, sin).astype(bf16)

    for part in range(2):
        dk = turn_back(dk_acc[part], cosine[part], sine[part])
        grads[part, HD : 2 * HD] = dk.astype(bf16)
        grads[part, 2 * HD : 3 * HD] = dv_acc[part].astype(bf16)
    grads_own[...] = grads[0]
    grads_far[...] = grads[1]


def post_attend_own_kernel(blocks, out_own, context, half):
    for c in range(16):
        context[HD * HEAD_OF[c] : HD * HEAD_OF[c] + HD] = blocks[c]
    half[...] = contract(context[...], out_own[...], ((0,), (0,)))


def post_attend_kernel(
    places, mix_ref, context, half, out_other, streams, segments, normed2, branch1
):
    mix = Mix(mix_ref)
    live = live_column(segments)
    own, other = halves(places[2])
    branch1[:, other] = live * contract(context[...], out_other.wait()[...], ((0,), (0,)))
    branch1[:, own] = live * half[...]
    streams = streams.wait()
    of_streams = [mix.second_of_streams(r) for r in range(4)]
    of_branch = mix.second_of_branch()
    for c in range(4):
        rows = slice(32 * c, 32 * c + 32)
        second = weighted(
            [(of_streams[r], streams[r, rows].astype(f32)) for r in range(4)]
            + [(of_branch, branch1[rows])]
        )
        normed2[rows] = normalize(second)[0].astype(bf16)


def ready(value):
    return value.wait() if isinstance(value, Late) else value


def feed_forward_kernel(normed, grad_branch, weights, down, grad_normed, hidden, grad_gate, grad_up):
    tokens = ready(normed)[...].reshape(512, 1024)
    weights = ready(weights)
    gate = contract(tokens, weights[:, 0:SLICE], ((1,), (0,)))
    up = contract(tokens, weights[:, SLICE : 2 * SLICE], ((1,), (0,)))
    sigma = jax.nn.sigmoid(gate)
    silu = gate * sigma
    hidden[...] = (silu * up).astype(bf16)
    grad = contract(
        ready(grad_branch)[...].reshape(512, 1024), ready(down)[...], ((1,), (1,))
    )
    grad_of_gate = (grad * up * sigma * (1.0 + gate * (1.0 - sigma))).astype(bf16)
    grad_of_up = (grad * silu).astype(bf16)
    grad_gate[...] = grad_of_gate
    grad_up[...] = grad_of_up
    total = contract(grad_of_gate, weights[:, 0:SLICE], ((1,), (1,)))
    total = total + contract(grad_of_up, weights[:, SLICE : 2 * SLICE], ((1,), (1,)))
    grad_normed[...] = total.astype(bf16).reshape(4, 128, 1024)


def branch2_kernel(hidden_own, hidden_other, down, context, own, other, context_out):
    context_out[...] = context[...]
    own[...] = contract(hidden_own[...], down[...], ((1,), (0,))).astype(bf16).reshape(4, 128, 1024)
    other[...] = (
        contract(hidden_other[...], down[...], ((1,), (0,))).astype(bf16).reshape(4, 128, 1024)
    )


def wide_tiles_kernel(
    places, gate_own, normed_own, gate_other, normed_other, up_own, up_other,
    hidden_own, grad_own, hidden_other, grad_other, out,
):
    def tile_of(left_own, right_own, left_other, right_other):
        tile = contract(left_own.wait()[...], right_own().reshape(512, 1024), ((0,), (0,)))
        return tile + contract(
            left_other.wait()[...], right_other().reshape(512, 1024), ((0,), (0,))
        )

    def slot(s):
        return 2 * (s % 4) + lax.rem(s // 4 + places[3] // 4, 2)

    first = tile_of(
        gate_own, lambda: normed_own.wait()[...], gate_other, lambda: normed_other.wait()[...]
    )
    second = tile_of(
        up_own, lambda: normed_own.ref[...], up_other, lambda: normed_other.ref[...]
    )
    for j, tile in enumerate((first, second)):
        for s in range(8):
            out[slot(s), SLICE * j : SLICE * j + SLICE] = tile[
                :, 128 * s : 128 * s + 128
            ].astype(bf16)
    tile = tile_of(
        hidden_own, lambda: grad_own.wait()[...], hidden_other, lambda: grad_other.wait()[...]
    ).astype(bf16)
    for s in range(8):
        rows = tile[PLACE * s : PLACE * s + PLACE]
        for d in range(8):
            start = 2 * SLICE + PLACE * d
            out[slot(s), start : start + PLACE] = rows[:, 128 * d : 128 * d + 128]


def second_back_kernel(
    places, mix_ref, t0, t1, t2, t3, streams, branch1, cotangent, segments, out_own, out_other,
    grad_second, grad_columns, grad_context, low, turned,
):
    mix = Mix(mix_ref)
    live = live_column(segments)
    of_streams = [mix.second_of_streams(r) for r in range(4)]
    of_branch = mix.second_of_branch()
    of_grad = [sum(mix.g[0][s] * mix.r[1][q][s] for s in range(4)) for q in range(4)]
    for c in range(4):
        rows = slice(32 * c, 32 * c + 32)
        second = weighted(
            [(of_streams[r], streams[r, rows].astype(f32)) for r in range(4)]
            + [(of_branch, branch1[rows])]
        )
        normed, inverse = normalize(second)
        grad = (t0[rows] + t1[rows].astype(f32)) + (t2[rows].astype(f32) + t3[rows].astype(f32))
        back = norm_back(grad, normed, inverse)
        grad_second[rows] = back
        if c == 0:
            cotangent = cotangent.wait()
        branch = weighted(
            [(of_grad[q], cotangent[q, rows].astype(f32)) for q in range(4)] + [(of_branch, back)]
        )
        low[rows] = (live[rows] * branch).astype(bf16)
    own, other = halves(places[2])
    turned[...] = contract(out_own.wait()[...], low[:, own], ((1,), (1,)))
    turned[...] += contract(out_other.wait()[...], low[:, other], ((1,), (1,)))
    for c in range(16):
        grad_context[c] = turned[HD * HEAD_OF[c] : HD * HEAD_OF[c] + HD].astype(bf16)
    for i in range(8):
        grad_columns[2 * (i % 4) + i // 4] = low[:, 128 * i : 128 * i + 128]


def mix_sums_kernel(
    mix_ref, t0, t1, t2, t3, streams, cotangent, branch1, grad_second, segments,
    out, branch2, acc,
):
    mix = Mix(mix_ref)
    live = live_column(segments)
    acc[...] = jnp.zeros_like(acc)
    for c in range(4):
        rows = slice(32 * c, 32 * c + 32)
        branch2[rows] = live[rows] * (
            (t0[rows] + t1[rows].astype(f32)) + (t2[rows].astype(f32) + t3[rows].astype(f32))
        )

    def fold(values):
        return sum(values[:8, 128 * j : 128 * j + 128] for j in range(4)) + sum(
            values[8:, 128 * j : 128 * j + 128] for j in range(4)
        )

    @pl.loop(0, 8)
    def _(r):
        rows = pl.ds(pl.multiple_of(r * 16, 16), 16)

        @pl.loop(0, 2)
        def _(l):
            lanes = pl.ds(pl.multiple_of(l * 512, 512), 512)
            hin = [streams[s, rows, lanes].astype(f32) for s in range(4)]
            branch, back = branch1[rows, lanes], grad_second[rows, lanes]
            last = branch2[rows, lanes]
            for q in range(4):
                top = cotangent[q, rows, lanes].astype(f32)
                for s in range(4):
                    acc[4 * q + s] += fold(top * hin[s])
                acc[16 + q] += fold(top * branch)
                acc[20 + q] += fold(top * last)
            for s in range(4):
                acc[24 + s] += fold(hin[s] * back)
            acc[28] += fold(branch * back)

    total = jnp.sum(acc[...], axis=1)

    def top_hin(q, s):
        return total[4 * q + s : 4 * q + s + 1]

    def top_branch(q):
        return total[16 + q : 17 + q]

    def back_hin(s):
        return total[24 + s : 25 + s]

    back_branch = total[28:29]
    for s in range(4):
        out[s * 6 : s * 6 + 1] = jnp.zeros((1, 128), f32)
        for r in range(4):
            row = s * 6 + 1 + r
            out[row : row + 1] = weighted(
                [(mix.r[1][q][s], top_hin(q, r)) for q in range(4)]
                + [(mix.p[1][s], back_hin(r))]
            )
            row = 24 + s * 6 + 1 + r
            out[row : row + 1] = weighted(
                [(mix.r[0][r][q], top_hin(s, q)) for q in range(4)]
                + [(mix.g[0][r], top_branch(s))]
            )
        row = s * 6 + 5
        out[row : row + 1] = weighted(
            [(mix.r[1][q][s], top_branch(q)) for q in range(4)] + [(mix.p[1][s], back_branch)]
        )
        row = 24 + s * 6
        out[row : row + 1] = weighted(
            [(mix.r[0][s][q], back_hin(q)) for q in range(4)] + [(mix.g[0][s], back_branch)]
        )
        row = 24 + s * 6 + 5
        out[row : row + 1] = total[20 + s : 21 + s]


def out_streams_kernel(mix_ref, streams, branch1, branch2, out):
    mix = Mix(mix_ref)
    of_streams = [
        [sum(mix.r[1][s][q] * mix.r[0][q][r] for q in range(4)) for r in range(4)]
        for s in range(4)
    ]
    of_branch = [sum(mix.r[1][s][q] * mix.g[0][q] for q in range(4)) for s in range(4)]
    for c in range(4):
        rows = slice(32 * c, 32 * c + 32)
        hin = [streams[s, rows].astype(f32) for s in range(4)]
        for s in range(4):
            total = weighted(
                [(of_streams[s][r], hin[r]) for r in range(4)]
                + [(of_branch[s], branch1[rows]), (mix.g[1][s], branch2[rows])]
            )
            out[s, rows] = total.astype(bf16)


def near_lanes(values, near):
    return jnp.concatenate(
        [values[:, TILE * k + 128 * near : TILE * k + 128 * near + 128] for k in range(4)], axis=1
    )


def pair_back_kernel(places, own, far, weights, grad, pair):
    half = places[1]
    own = own.wait()
    for j in range(3):
        rows = slice(HD * j, HD * j + HD)
        pair[pl.ds(pl.multiple_of(128 * j + HD * half, HD), HD), :] = own[rows]
        pair[pl.ds(pl.multiple_of(128 * j + HD * (1 - half), HD), HD), :] = far[rows]
    total = contract(near_lanes(pair, 1), weights.wait()[...], ((0,), (0,)))
    grad[...] = total.astype(bf16).reshape(4, 128, 1024)


def pair_back_own_kernel(pair, weights, grad):
    total = contract(near_lanes(pair, 0), weights[...], ((0,), (0,)))
    grad[...] = total.astype(bf16).reshape(4, 128, 1024)


def narrow_tiles_kernel(
    places, pair, normed_own, normed_other, columns, context_own, context_other, out
):
    z, core = places[0], places[2]
    pair = pair.wait()
    tile = jnp.zeros((384, 1024), f32)
    for near, tokens in enumerate((normed_own, normed_other)):
        tokens = tokens.wait()[:, 0:128].reshape(512, 1024)
        tile = tile + contract(near_lanes(pair, near), tokens, ((1,), (0,)))
    for s in range(8):
        out[s, 0:384] = tile[:, 128 * s : 128 * s + 128].astype(bf16)
    tile = jnp.zeros((128, 1024), f32)
    for near, contexts in enumerate((context_own, context_other)):
        contexts = ready(contexts)
        for back in range(4):
            source = columns[2 * lax.rem(z - back + 4, 4) + lax.rem(core + near, 2)]
            tile = tile + contract(source, contexts[back], ((0,), (1,)))
    for s in range(8):
        out[s, 384:512] = tile[:, 128 * s : 128 * s + 128].astype(bf16)


def fold_kernel(blocks, *outs):
    start = 0
    for out in outs:
        rows = slice(start, start + out.shape[0])
        total = blocks[0, rows].astype(f32)
        for s in range(1, 8):
            total = total + blocks[s, rows].astype(f32)
        out[...] = total.astype(bf16)
        start += out.shape[0]


def fold_narrow_kernel(blocks, out):
    total = blocks[0].astype(f32)
    for s in range(1, 8):
        total = total + blocks[s].astype(f32)
    out[0:512] = total[0:512].astype(bf16)
    high, low = two_parts(total[512:513] + total[513:514])
    out[512:528] = jnp.concatenate([high, low, jnp.zeros((14, 128), bf16)], axis=0)


def add_narrow_kernel(own, far, out):
    total = own[...].astype(f32) + far[...].astype(f32)
    out[0:512] = total[0:512].astype(bf16)
    high, low = two_parts(total[512:513] + total[513:514])
    out[512:528] = jnp.concatenate([high, low, jnp.zeros((14, 128), bf16)], axis=0)


def member(places, own, other, index):
    back = lax.rem(places[0] - index % 4 + 4, 4)
    return jnp.where(places[2] == index // 4, own[back].astype(f32), other[back].astype(f32))


def finish_wide_kernel(places, own, other, gate_up, down, rows):
    for i in range(8):
        block = member(places, own, other, i)
        for s in range(8):
            for j in range(2):
                start = SLICE * j + PLACE * s
                unit = 8 * PIECE * s + PIECE * i
                rows[j, unit : unit + PIECE] = block[start : start + PIECE]
        for d in range(8):
            start = 2 * SLICE + PLACE * d
            down[PIECE * i : PIECE * i + PIECE, 128 * d : 128 * d + 128] = block[
                start : start + PIECE
            ]
    for j in range(2):
        for k in range(rows.shape[1] // 128):
            lanes = slice(128 * k, 128 * k + 128)
            gate_up[j, :, lanes] = rows[j, lanes].T


def finish_narrow_kernel(places, own, other, qkv, out, mix_grad):
    total = jnp.zeros((1, 128), f32)
    for i in range(8):
        block = member(places, own, other, i)
        total = total + (block[512:513] + block[513:514])
        for j in range(3):
            qkv[j, :, 128 * i : 128 * i + 128] = block[128 * j : 128 * j + 128].T
        out[:, 128 * i : 128 * i + 128] = block[384:512].T
    for m in range(2):
        for s in range(4):
            lane = m * 24 + s * 6
            mix_grad[m, s : s + 1, :] = total[:, lane : lane + 6]


def two_parts(values):
    high = values.astype(bf16)
    return high, (values - high.astype(f32)).astype(bf16)


def first_back_kernel(
    mix_ref, t0, t1, t2, t3, streams, cotangent, grad_second, sums, tiles, streams_grad, out, mix_rows
):
    mix = Mix(mix_ref)
    of_top = [
        [sum(mix.r[1][q][s] * mix.r[0][s][r] for s in range(4)) for q in range(4)]
        for r in range(4)
    ]
    of_back = [sum(mix.r[0][s][r] * mix.p[1][s] for s in range(4)) for r in range(4)]
    total = [jnp.zeros((1, 1024), f32) for _ in range(4)]
    cotangent, grad_second = cotangent.wait(), grad_second.wait()
    for c in range(4):
        rows = slice(32 * c, 32 * c + 32)
        hin = [streams[s, rows].astype(f32) for s in range(4)]
        top = [cotangent[s, rows].astype(f32) for s in range(4)]
        normed, inverse = normalize(weighted([(mix.p[0][s], hin[s]) for s in range(4)]))
        grad = (t0[rows] + t1[rows].astype(f32)) + (t2[rows].astype(f32) + t3[rows].astype(f32))
        back1 = norm_back(grad, normed, inverse)
        back2 = grad_second[rows]
        for r in range(4):
            value = weighted(
                [(of_top[r][q], top[q]) for q in range(4)]
                + [(of_back[r], back2), (mix.p[0][r], back1)]
            )
            streams_grad[r, rows] = value.astype(bf16)
            total[r] = total[r] + jnp.sum(hin[r] * back1, axis=0, keepdims=True)
    mix_rows[0:48] = sums.wait()[...]
    mix_rows[48:] = jnp.zeros((80, 128), f32)
    for s in range(4):
        row = sum(total[s][:, 128 * k : 128 * k + 128] for k in range(8))
        mix_rows[s * 6 : s * 6 + 1] = row
    high, low = two_parts(jnp.sum(mix_rows[...].T, axis=0, keepdims=True))
    rows = jnp.concatenate([high, low, jnp.zeros((14, 128), bf16)], axis=0)
    tiles = tiles.wait()
    for s in range(8):
        out[s, 0:512] = tiles[s]
        out[s, 512:528] = rows


def split_kernel(source, own, other):
    own[...] = source[0]
    other[...] = source[1]


def copy_kernel(source, out):
    out[...] = source[...]


def add4_kernel(one, two, three, four, out):
    out[...] = (one[...] + two[...]) + (three[...] + four[...])


def add2_kernel(one, two, out):
    out[...] = (one[...].astype(f32) + two[...].astype(f32)).astype(out.dtype)


def shards(
    streams, segments, stream_mix, qkv_weight, out_weight, gate_up_weight, down_weight, cotangent
):
    kept_arrays.arrays.clear()
    z, half, core = lax.axis_index("z"), lax.axis_index("xh"), lax.axis_index("co")
    team, row = lax.axis_index(TEAM), lax.axis_index(SHARD)
    width = streams.shape[3]
    ff = down_weight.shape[0]
    places = (jnp.stack([z, half, core, row, team]).astype(jnp.int32), smem)
    mix = (stream_mix, smem)
    streams, cotangent, segments = streams[0], cotangent[0], (segments, vmem)
    token = ((128, width), bf16)
    token4 = ((4, 128, width), bf16)

    def v(*values):
        return [(value, vmem) for value in values]

    def h(*values):
        return [(value, "hbm") for value in values]

    def l(*values):
        return [(value, "late") for value in values]

    def stack(values, parts, name, us=1, order=(), beside=(), in_hbm=False, place="hbm"):
        (result,) = call(
            stack_kernel,
            [((4,) + values.shape, bf16, place)],
            (h(values) if in_hbm else v(values)) + v(*parts),
            name,
            us,
            order=order,
            beside=beside,
        )
        return result

    (weights,) = call(
        pick_kernel,
        [((128, 896 + 2 * SLICE), bf16, "hbm")],
        [places] + l(out_weight, down_weight, gate_up_weight),
        "pick",
        4,
    )
    far_weights = shift(weights, "xl", 1)

    (normed1,) = call(
        first_norm_kernel,
        [((144, width), bf16)],
        [mix] + h(streams) + [segments],
        "first_norm",
        3,
        order=[weights],
    )
    (qkv_blocks,) = call(
        pick_heads_kernel,
        [((8, 3, 128, 128), bf16, "hbm")],
        [places, (qkv_weight, raw)],
        "pick_heads",
        2,
        [pltpu.VMEM((3, 128, 128), bf16)],
        beside=[normed1],
    )
    qkv_blocks = lax.all_to_all(qkv_blocks, SHARD, 0, 0, tiled=True)
    normed1_z = z_issue(normed1)
    (weights,) = call(
        pair_weights_kernel,
        [((2, 128, 896 + 2 * SLICE), bf16, "hbm")],
        h(weights) + v(far_weights),
        "pair_weights",
        1,
        beside=[normed1],
    )
    weights = lax.all_gather(weights, "y", axis=0, tiled=True)
    normed1_own = stack(normed1, normed1_z, "stack_normed1", 4)
    normed1_other = shift(normed1_own, "co", 1)
    freq = rope_base ** (-(jnp.arange(32, dtype=f32) * 2.0) / HD)
    back, near, place = jnp.arange(4), jnp.arange(2), jnp.arange(128)
    positions = (
        512 * ((z - back[None, :, None, None] + 4) % 4)
        + 256 * ((half + near[:, None, None, None]) % 2)
        + 128 * ((core + near[None, None, :, None]) % 2)
        + place[None, None, None, :]
    ).reshape(2, 1, 1024)
    angle = positions.astype(f32) * freq[None, :, None]
    cosine, sine = jnp.cos(angle), jnp.sin(angle)

    (pair_weights,) = call(
        turn_heads_kernel, [((384, width), bf16, "hbm")], v(qkv_blocks), "turn_heads", 1
    )
    kept, sent = call(
        project_kernel,
        [((208, 1024), bf16, "vmem"), ((208, 1024), bf16, "vmem")],
        [places] + l(normed1_own, normed1_other) + h(pair_weights) + v(cosine, sine),
        "project",
        16,
    )
    received = shift(sent, "xh", 1)
    (grad_branch2,) = call(
        grad_branch2_kernel,
        [token],
        [mix] + h(cotangent) + [segments],
        "grad_branch2",
        0,
        order=[kept],
    )
    grad2_z = z_issue(grad_branch2)

    qkv, context_blocks, context_wide, logsum, edges = call(
        attend_kernel,
        [
            ((2, 192, 1024), bf16, "hbm"),
            ((16, HD, 128), bf16, "hbm"),
            ((2, HD, 1024), f32, "hbm"),
            ((2, 8, 1024), f32, "hbm"),
            ((4,), jnp.int32),
        ],
        [places] + h(kept) + v(received),
        "attend",
        12,
        beside=[grad_branch2],
    )
    context_mine = lax.all_to_all(context_blocks, CTX, 0, 0, tiled=True)

    grad2_own = stack(grad_branch2, grad2_z, "stack_grad2", 1, [context_blocks])
    grad2_other = shift(grad2_own, "co", 1)
    (out_own,) = call(
        unpack_out_kernel,
        [((width, 512), bf16, "vmem")],
        [places, (weights, ("late", 0, 512))],
        "unpack_out",
        3,
        order=[grad2_own],
    )
    out_other = shift(out_own, "co", 1)
    context, branch_half = call(
        post_attend_own_kernel,
        [((width, 128), bf16, "vmem"), ((128, 512), f32, "vmem")],
        v(context_mine) + h(out_own),
        "post_attend_own",
        15,
    )
    normed2, branch1 = call(
        post_attend_kernel,
        [token, ((128, width), f32, "hbm")],
        [places, mix]
        + h(context)
        + v(branch_half)
        + l(out_other, streams)
        + [segments],
        "post_attend",
        3,
    )
    normed2_z = z_issue(normed2)
    inner = ("late", 512, 896 + 2 * SLICE)
    gu_all, down = call(
        unpack_kernel,
        [((width, 2 * SLICE), bf16, "vmem"), ((SLICE, width), bf16, "vmem")],
        [places, (weights, inner)],
        "unpack",
        4,
        order=[out_own],
    )
    normed2_own = stack(normed2, normed2_z, "stack_normed2", order=[down])
    normed2_other = shift(normed2_own, "co", 1)
    acts = [token4 + ("vmem",)] + [((512, SLICE), bf16, "hbm")] * 3
    grad_own, hidden_own, gate_own, up_own = call(
        feed_forward_kernel,
        acts,
        l(normed2_own, grad2_own, gu_all, down),
        "feed_forward_own",
        5,
    )
    grad_other, hidden_other, gate_other, up_other = call(
        feed_forward_kernel,
        acts,
        l(normed2_other, grad2_other, gu_all, down),
        "feed_forward_other",
        5,
        order=[hidden_own],
    )

    def core_add(own, other, name, order, beside=(), own_in_hbm=False):
        return call(
            core_add_kernel,
            [((128, width), f32, "vmem")] + [token] * 3,
            (h(own) if own_in_hbm else v(own)) + v(shift(other, "co", 1)),
            name,
            1,
            order=order,
            beside=beside,
        )

    def z_terms(terms):
        return [terms[0]] + [shift(term, "z", -k) for k, term in enumerate(terms[1:], 1)]

    half_own, half_other, context = call(
        branch2_kernel,
        [token4 + ("vmem",), token4 + ("vmem",), ((width, 128), bf16, "vmem")],
        h(hidden_own, hidden_other, down, context),
        "branch2",
        3,
        order=[hidden_other],
    )
    terms = core_add(grad_own, grad_other, "core_add_second", [half_own])
    grad_normed2 = z_terms(terms)
    context_z = z_issue(context)

    grad_second, grad_columns, grad_context = call(
        second_back_kernel,
        [
            ((128, width), f32, "hbm"),
            ((8, 128, 128), bf16, "hbm"),
            ((16, HD, 128), bf16, "hbm"),
        ],
        [places, mix]
        + h(grad_normed2[0])
        + v(*grad_normed2[1:])
        + h(streams, branch1)
        + l(cotangent)
        + [segments] + l(out_own, out_other),
        "second_back",
        5,
        [pltpu.VMEM((128, width), bf16), pltpu.VMEM((width, 128), f32)],
    )
    grad_context = lax.all_to_all(grad_context, CTX, 0, 0, tiled=True)

    (wide_tiles,) = call(
        wide_tiles_kernel,
        [((8, 3 * SLICE, 128), bf16, "hbm")],
        [places] + l(
            gate_own, normed2_own, gate_other, normed2_other, up_own, up_other,
            hidden_own, grad2_own, hidden_other, grad2_other,
        ),
        "wide_tiles",
        7,
        order=[grad_second],
    )
    wide_mine = lax.psum_scatter(wide_tiles, "y", scatter_dimension=0, tiled=True)

    terms = core_add(half_own, half_other, "core_add_branch2", [wide_tiles], own_in_hbm=True)
    branch2 = z_terms(terms)
    grads_own, grads_far, columns = call(
        attend_back_kernel,
        [((192, 1024), bf16, "hbm"), ((192, 1024), bf16, "vmem"), ((8, 128, 128), bf16, "hbm")],
        [places, (edges, smem)]
        + h(qkv, context_wide, logsum)
        + v(grad_context, cosine, sine)
        + h(grad_columns),
        "attend_back",
        40,
        [
            pltpu.VMEM((2, HD, 1024), f32),
            pltpu.VMEM((2, HD, 1024), f32),
            pltpu.VMEM((2, 192, 1024), bf16),
        ],
        [terms[0]],
    )
    received = shift(grads_far, "xh", 1)
    columns = lax.all_to_all(columns, ("z", "co"), 0, 0, tiled=True)
    sums, branch2 = call(
        mix_sums_kernel,
        [((48, 128), f32, "vmem"), ((128, width), f32, "hbm")],
        [mix]
        + h(branch2[0])
        + v(*branch2[1:])
        + h(streams, cotangent, branch1, grad_second)
        + [segments],
        "mix_sums",
        7,
        [pltpu.VMEM((32, 8, 128), f32)],
        [grads_own],
        context_z,
    )
    context_own = stack(context, context_z, "stack_context", 1, [sums], in_hbm=True, place="vmem")
    context_other = shift(context_own, "co", 1)
    wide_type = ((3 * SLICE, 128), bf16)
    wide_mine, wide_far = call(
        split_kernel, [wide_type, wide_type], h(wide_mine), "split_wide", 1, order=[context_own]
    )
    wide_far = shift(wide_far, "xl", 1)
    grad_other, pair = call(
        pair_back_kernel,
        [token4 + ("vmem",), ((384, 1024), bf16, "vmem")],
        [places] + l(grads_own) + v(received) + l(pair_weights),
        "pair_back",
        4,
        order=[context_own],
        beside=[columns, wide_mine],
    )
    (grad_own,) = call(
        pair_back_own_kernel, [token4 + ("vmem",)], h(pair, pair_weights), "pair_back_own", 3
    )
    terms = core_add(grad_own, grad_other, "core_add_first", [])
    grad_normed1 = z_terms(terms)

    (narrow_tiles,) = call(
        narrow_tiles_kernel,
        [((8, 512, 128), bf16, "vmem")],
        [places]
        + l(pair, normed1_own, normed1_other)
        + v(columns)
        + l(context_own)
        + v(context_other),
        "narrow_tiles",
        6,
        order=[terms[0]],
    )
    narrow_order = narrow_tiles
    (wide_rows,) = call(
        add2_kernel, [wide_type], v(wide_mine, wide_far), "add_wide_xl", 1, order=[narrow_order], beside=grad_normed1[1:]
    )
    wide_far = shift(wide_rows, "xh", 1)
    streams_grad, narrow_tiles = call(
        first_back_kernel,
        [token4 + ("hbm",), ((8, 528, 128), bf16, "hbm")],
        [mix]
        + h(grad_normed1[0])
        + v(*grad_normed1[1:])
        + h(streams)
        + l(cotangent, grad_second, sums, narrow_tiles),
        "first_back",
        6,
        [pltpu.VMEM((128, 128), f32)],
    )
    narrow_tiles = lax.all_to_all(narrow_tiles, SHARD, 0, 0, tiled=True)

    (wide_rows,) = call(
        add2_kernel, [wide_type], v(wide_rows, wide_far), "add_wide", 1, order=[streams_grad]
    )
    wide_z = z_issue(wide_rows)
    (out_streams,) = call(
        out_streams_kernel,
        [token4 + ("hbm",)],
        [mix] + h(streams, branch1, branch2),
        "out_streams",
        8,
        beside=[wide_rows],
    )
    narrow_type = [((528, 128), bf16)]
    (mine,) = call(fold_narrow_kernel, narrow_type, v(narrow_tiles), "fold_narrow", 1, order=[out_streams])
    narrow_far = shift(mine, "xh", 1)
    wide_own = stack(wide_rows, wide_z, "stack_wide", 1, beside=[mine])
    wide_other = shift(wide_own, "co", 1)
    (narrow_rows,) = call(
        add_narrow_kernel, narrow_type, v(mine, narrow_far), "add_narrow", 1, order=[wide_own]
    )
    narrow_z = z_issue(narrow_rows)
    gate_up_grad, down_grad = call(
        finish_wide_kernel,
        [((2, 128, 8 * ff), f32, "hbm"), ((ff, width), f32, "hbm")],
        [places] + h(wide_own) + v(wide_other),
        "finish_wide",
        5,
        [pltpu.VMEM((2, 8 * ff, 128), f32)],
        beside=[narrow_rows],
    )
    narrow_own = stack(narrow_rows, narrow_z, "stack_narrow", 1, [down_grad])
    narrow_other = shift(narrow_own, "co", 1)
    qkv_grad, out_grad, mix_grad = call(
        finish_narrow_kernel,
        [((3, 128, width), f32, "hbm"), ((128, width), f32, "hbm"), ((2, 4, 6), f32)],
        [places] + h(narrow_own) + v(narrow_other),
        "finish_narrow",
        3,
    )
    return (
        out_streams[None], streams_grad[None], qkv_grad, out_grad, gate_up_grad, down_grad, mix_grad,
    )


def solution(mesh):
    fine = Mesh(
        np.asarray(mesh.devices).reshape([n for _, n in AXES]), tuple(name for name, _ in AXES)
    )
    in_specs = (
        P(SHARD, None, CTX, None),
        P(SHARD, CTX),
        P(),
        P(None, SHARD, None),
        P(SHARD, None),
        P(None, SHARD, None),
        P(SHARD, None),
        P(SHARD, None, CTX, None),
    )
    out_specs = (
        P(SHARD, None, CTX, None),
        P(SHARD, None, CTX, None),
        P(None, SHARD, None),
        P(SHARD, None),
        P(None, SHARD, None),
        P(SHARD, None),
        P(),
    )
    return jax.shard_map(shards, mesh=fine, in_specs=in_specs, out_specs=out_specs, check_vma=False)
```

```python
import jax
import jax.numpy as jnp
import numpy as np
from jax import lax
from jax.experimental import pallas as pl
from jax.experimental.pallas import tpu as pltpu
from jax.sharding import Mesh
from jax.sharding import PartitionSpec as P

HD = 64
TILE = 256
VMEM = 24 * 1024 * 1024
COST = 1.1e9
PIECE = 44
PLACE = 48
SLICE = 8 * PLACE
eps = 1e-05
rope_base = 1000000.0
neg_big = -1e30
bf16 = jnp.bfloat16
f32 = jnp.float32
smem = pl.BlockSpec(memory_space=pltpu.SMEM)
vmem = pl.BlockSpec(memory_space=pltpu.VMEM)
anywhere = pl.BlockSpec(memory_space=pl.ANY)
hbm = pl.BlockSpec(memory_space=pltpu.HBM)
raw = pl.BlockSpec(memory_space=pltpu.HBM)

AXES = (("z", 4), ("xh", 2), ("co", 2), ("xl", 2), ("y", 4))
SIZE = dict(AXES)
CTX = ("z", "xh", "co")
SHARD = ("xl", "y")
TEAM = ("co", "z")
HEAD_OF = [8 * (c % 2) + 2 * (c // 4) + (c // 2) % 2 for c in range(16)]


class Kept:
    def __init__(self):
        self.arrays = []

    def add(self, array):
        self.arrays.append(array)
        return array

    def __contains__(self, array):
        return any(array is other for other in self.arrays)


kept_arrays = Kept()


def shift(values, axis, amount):
    count = SIZE[axis]
    moved = lax.ppermute(values, axis, [(i, (i + amount) % count) for i in range(count)])
    if axis == "co" and values in kept_arrays:
        kept_arrays.add(moved)
    return moved


def z_issue(values):
    return [shift(values, "z", k) for k in range(1, 4)]


class Late:
    def __init__(self, copy, ref):
        self.copy, self.ref = copy, ref

    def wait(self):
        if self.copy is not None:
            self.copy.wait()
        return self.ref


class Early:
    def __init__(self, ref, target, sem):
        self.ref, self.target, self.sem = ref, target, sem

    def __getitem__(self, where):
        return self.ref[where]

    def __setitem__(self, where, value):
        self.ref[where] = value

    def send(self, *where):
        self.send_from(self.ref.at[where] if where else self.ref, *where)

    def send_from(self, source, *where):
        target = self.target.at[where] if where else self.target
        pltpu.make_async_copy(source, target, self.sem).start()


def call(kernel, outs, ins, name, us, scratch=(), order=(), beside=()):
    known = (smem, vmem, raw)
    stays = [value in kept_arrays and place not in (smem, raw) for value, place in ins]
    extra_ins = len(order) + len(beside)
    ends = len(ins), len(ins) + extra_ins, len(ins) + extra_ins + len(outs)
    near = [k for k, (_, place) in enumerate(ins) if place not in known and not stays[k]]
    far = [k for k, out in enumerate(outs) if len(out) > 2 and out[2] != "vmem"]

    def part(k):
        value, place = ins[k]
        if isinstance(place, tuple):
            return value.shape[:-1] + (place[2] - place[1],)
        return value.shape

    def body(*refs):
        given, results, rest = list(refs[: ends[0]]), list(refs[ends[1] : ends[2]]), refs[ends[2] :]
        rest, sems = (rest[:-1], rest[-1]) if near or far else (rest, None)
        loaded = rest[len(scratch) : len(scratch) + len(near)]
        staged = rest[len(scratch) + len(near) :]
        for k, (_, place) in enumerate(ins):
            if stays[k] and place == "late":
                given[k] = Late(None, given[k])
        copies, waits = [], []
        for j, (k, ref) in enumerate(zip(near, loaded)):
            source, place = given[k], ins[k][1]
            if isinstance(place, tuple):
                source = source.at[..., place[1] : place[2]]
            copies.append(pltpu.make_async_copy(source, ref, sems.at[j]))
            if (place[0] if isinstance(place, tuple) else place) == "hbm":
                waits.append(copies[-1])
                given[k] = ref
            else:
                given[k] = Late(copies[-1], ref)
        for copy in copies:
            copy.start()
        for copy in waits:
            copy.wait()
        copies = []
        for j, (k, ref) in enumerate(zip(far, staged)):
            sem = sems.at[len(near) + j]
            copies.append(pltpu.make_async_copy(ref, results[k], sem))
            results[k] = Early(ref, results[k], sem) if outs[k][2] == "early" else ref
        kernel(*given, *results, *rest[: len(scratch)])
        for copy, k in zip(copies, far):
            if outs[k][2] != "early":
                copy.start()
        for copy in copies:
            copy.wait()

    extra = [pltpu.VMEM(part(k), ins[k][0].dtype) for k in near]
    extra += [pltpu.VMEM(outs[k][0], outs[k][1]) for k in far]
    if near or far:
        extra.append(pltpu.SemaphoreType.DMA((len(near) + len(far),)))

    def in_hbm(value):
        return pltpu.with_memory_space_constraint(value, pltpu.HBM)

    def out_type(out):
        if len(out) > 2 and out[2] == "vmem":
            return pltpu.VMEM(out[0], out[1])
        if len(out) > 2:
            return pltpu.HBM(out[0], out[1])
        return jax.ShapeDtypeStruct(out[0], out[1])

    def in_vmem(value):
        return pltpu.with_memory_space_constraint(value, pltpu.VMEM)

    def spec(k):
        return vmem if stays[k] else ins[k][1] if ins[k][1] in known else hbm

    def placed(k):
        value, place = ins[k]
        return in_vmem(value) if stays[k] else value if place in (smem, vmem) else in_hbm(value)

    results = pl.pallas_call(
        body,
        out_shape=tuple(out_type(out) for out in outs),
        in_specs=[spec(k) for k in range(len(ins))]
        + [anywhere if value in kept_arrays else hbm for value in order]
        + [anywhere] * len(beside),
        out_specs=tuple(
            hbm if k in far else smem if out[1] == jnp.int32 else vmem
            for k, out in enumerate(outs)
        ),
        scratch_shapes=list(scratch) + extra,
        compiler_params=pltpu.CompilerParams(vmem_limit_bytes=VMEM),
        cost_estimate=pl.CostEstimate(
            flops=int(us * COST), bytes_accessed=0, transcendentals=0
        ),
        name=name,
    )(
        *[placed(k) for k in range(len(ins))],
        *[value if value in kept_arrays else in_hbm(value) for value in order],
        *beside,
    )
    for out, result in zip(outs, results):
        if len(out) > 2 and out[2] == "vmem":
            kept_arrays.add(result)
    return results


def contract(left, right, dims):
    return lax.dot_general(left, right, (dims, ((), ())), preferred_element_type=f32)


def normalize(values):
    centered = values - jnp.mean(values, axis=-1, keepdims=True)
    inverse = lax.rsqrt(jnp.mean(centered * centered, axis=-1, keepdims=True) + eps)
    return (centered * inverse, inverse)


def norm_back(grad, normed, inverse):
    return inverse * (
        grad
        - jnp.mean(grad, axis=-1, keepdims=True)
        - normed * jnp.mean(grad * normed, axis=-1, keepdims=True)
    )


def weighted(terms):
    total = None
    for weight, values in terms:
        part = weight * values
        total = part if total is None else total + part
    return total


def live_column(segments):
    wide = jnp.broadcast_to((segments[...] > 0).astype(f32), (128, 128))
    return wide.T[:, 0:1]


class Mix:
    def __init__(self, ref):
        self.p = [[ref[m, s, 0] for s in range(4)] for m in range(2)]
        self.r = [[[ref[m, s, 1 + r] for r in range(4)] for s in range(4)] for m in range(2)]
        self.g = [[ref[m, s, 5] for s in range(4)] for m in range(2)]

    def second_of_streams(self, r):
        return sum(self.p[1][s] * self.r[0][s][r] for s in range(4))

    def second_of_branch(self):
        return sum(self.p[1][s] * self.g[0][s] for s in range(4))


def core_add_kernel(own, received, first, *rest):
    first[...] = own[0].astype(f32) + received[0].astype(f32)
    for k, target in enumerate(rest, 1):
        target[...] = (own[k].astype(f32) + received[k].astype(f32)).astype(bf16)


def first_norm_kernel(mix_ref, streams, segments, out):
    mix = Mix(mix_ref)
    for c in range(4):
        rows = slice(32 * c, 32 * c + 32)
        first = weighted([(mix.p[0][s], streams[s, rows].astype(f32)) for s in range(4)])
        out[rows] = normalize(first)[0].astype(bf16)
    out[128:144] = jnp.zeros((16, 1024), bf16)
    out[128:144, 0:128] = jnp.broadcast_to(segments[...].astype(f32), (16, 128)).astype(bf16)


def pick_heads_kernel(places, weights, out, block):
    pltpu.sync_copy(
        weights.at[:, :, pl.ds(pl.multiple_of(places[4] * 128, 128), 128)], block
    )
    for s in range(8):
        out.send_from(block, s)


def pieces(d):
    start, place, result = PLACE * d, 0, []
    while place < PLACE:
        count = min(PLACE - place, 128 - start % 128)
        result.append((place, start // 128, start % 128, count))
        start, place = start + count, place + count
    return result


def pick_kernel(places, out_weight, down, gate_up, wide):
    team, core = places[4], places[2]
    own, _ = halves(core)
    wide[:, 0:512] = out_weight.wait()[:, own]
    start = jnp.minimum(team * PIECE // 16 * 16, 8 * PIECE - 64)
    place = lax.broadcasted_iota(jnp.int32, (PLACE, 1), 0)
    wanted = jnp.where(place < PIECE, place + (team * PIECE - start), -1)
    unit = lax.broadcasted_iota(jnp.int32, (1, 64), 1)
    picked = jnp.where(unit == wanted, 1.0, 0.0).astype(bf16)
    down = down.wait()[pl.ds(pl.multiple_of(start, 16), 64)]
    rows = contract(picked, down, ((1,), (0,))).astype(bf16)
    for d in range(8):
        for place, tile, start, count in pieces(d):
            lanes = slice(512 + 128 * tile, 512 + 128 * tile + 128)
            wide[start : start + count, lanes] = rows[
                place : place + count, 128 * d : 128 * d + 128
            ]
    wide.send(slice(None), slice(0, 896))
    units = gate_up.ref.shape[2] // 2
    unit = lax.broadcasted_iota(jnp.int32, (units, 1), 0)
    place = lax.broadcasted_iota(jnp.int32, (1, SLICE // 2), 1)
    piece = lax.rem(place, PLACE)
    wanted = (place // PLACE) * (8 * PIECE) + team * PIECE + piece
    wanted = jnp.where(piece < PIECE, wanted, -1)
    picked = jnp.where(unit == wanted, 1.0, 0.0).astype(bf16)
    gate_up = gate_up.wait()
    for j in range(2):
        columns = [
            contract(gate_up[j, :, units * k : units * k + units], picked, ((1,), (0,))).astype(bf16)
            for k in range(2)
        ]
        lanes = slice(896 + SLICE * j, 896 + SLICE * j + SLICE)
        wide[:, lanes] = jnp.concatenate(columns, axis=1)
        wide.send(slice(None), lanes)


def halves(core):
    own = pl.ds(pl.multiple_of(core * 512, 512), 512)
    other = pl.ds(pl.multiple_of((1 - core) * 512, 512), 512)
    return own, other


def pair_weights_kernel(near, far, out):
    out[0] = near[...]
    out[1] = far[...]


def unpack_out_kernel(places, weights, out):
    weights = weights.wait()
    for part in range(2):
        for y in range(4):
            s = 4 * lax.rem(places[3] // 4 + part, 2) + y
            out[pl.ds(pl.multiple_of(128 * s, 128), 128)] = weights[2 * y + part]


def unpack_kernel(places, weights, gate_up, down):
    weights = weights.wait()
    for part in range(2):
        for y in range(4):
            s = 4 * lax.rem(places[3] // 4 + part, 2) + y
            block = weights[2 * y + part]
            gate_up[pl.ds(pl.multiple_of(128 * s, 128), 128)] = block[:, 384:]
            for d in range(8):
                for place, tile, start, count in pieces(d):
                    row = pl.multiple_of(PLACE * s + place, 16)
                    down[pl.ds(row, count), 128 * d : 128 * d + 128] = block[
                        start : start + count, 128 * tile : 128 * tile + 128
                    ]


def grad_branch2_kernel(mix_ref, cotangent, segments, out):
    mix = Mix(mix_ref)
    live = live_column(segments)
    for c in range(4):
        rows = slice(32 * c, 32 * c + 32)
        total = weighted([(mix.g[1][s], cotangent[s, rows].astype(f32)) for s in range(4)])
        out[rows] = (live[rows] * total).astype(bf16)


def turn(values, cosine, sine):
    one, two = values[:32], values[32:]
    return jnp.concatenate([one * cosine - two * sine, two * cosine + one * sine], axis=0)


def turn_back(grad, cosine, sine):
    one, two = grad[:32], grad[32:]
    return jnp.concatenate([one * cosine + two * sine, two * cosine - one * sine], axis=0)


def turn_heads_kernel(weights, out):
    for j in range(3):
        rows = slice(128 * j, 128 * j + 128)
        for s in range(8):
            out[rows, 128 * s : 128 * s + 128] = weights[s, j].T
        out.send(rows)


def stack_kernel(first, second, third, fourth, out):
    for k, part in enumerate((first, second, third, fourth)):
        out[k] = part[...]


def project_kernel(places, own, other, wide, cosine, sine, kept, sent):
    half = places[1]

    def rows(head):
        return [wide[pl.ds(pl.multiple_of(128 * j + HD * head, HD), HD), :] for j in range(3)]

    mine = jnp.concatenate(rows(half) + rows(1 - half), axis=0)
    for near, tokens in enumerate((own, other)):
        tokens = ready(tokens)
        blocks = contract(mine, tokens[:, 0:128].reshape(512, 1024), ((1,), (1,)))
        for back in range(4):
            lanes = slice(back * TILE + near * 128, back * TILE + near * 128 + 128)
            block = blocks[:, 128 * back : 128 * back + 128]
            segs = tokens[back, 128:144, 0:128]
            cos, sin = cosine[0, :, lanes], sine[0, :, lanes]
            for target, base in ((kept, 0), (sent, 192)):
                query = turn(block[base : base + 64], cos, sin).astype(bf16)
                target[0:64, lanes] = (query.astype(f32) * 0.125).astype(bf16)
                target[64:128, lanes] = turn(block[base + 64 : base + 128], cos, sin).astype(bf16)
                target[128:192, lanes] = block[base + 128 : base + 192].astype(bf16)
                target[192:208, lanes] = segs


def pair_lanes(places, pair):
    back = lax.rem(places[0] - pair + 4, 4)
    return pl.ds(pl.multiple_of(back * TILE, TILE), TILE)


def in_order(places):
    return places[1], 1 - places[1]


def both(places, ref, rows, lanes):
    return jnp.concatenate([ref[part, rows, lanes] for part in in_order(places)], axis=1)


def pair_positions(places, pair, axis):
    local = lax.broadcasted_iota(jnp.int32, (TILE, 1) if axis == 0 else (1, TILE), axis)
    first = (local + places[2] * 128) % TILE + 2 * TILE * pair
    return jnp.concatenate([first, first + TILE], axis=axis)


def document_start(edges, place):
    start = jnp.zeros_like(place)
    for edge in edges:
        start = jnp.where(place >= edge, edge, start)
    return start


def pairs_of(edges, pair):
    return pair - document_start(edges, 2 * TILE * pair) // (2 * TILE) + 1


def attend_kernel(places, kept, received, qkv, context, context_wide, logsum, edges_out):
    core = places[2]
    qkv[0] = kept[0:192]
    qkv[1] = received[0:192]
    qkv.send()
    seg_own = kept[192:208].astype(f32)
    seg_far = received[192:208].astype(f32)
    edges = []
    for d in range(1, 5):
        count = jnp.float32(0)
        for seg in (seg_own, seg_far):
            inside = (seg > 0.5) & (seg < d + 0.5)
            count = count + jnp.sum(jnp.where(inside, 0.0625, 0.0))
        edge = count.astype(jnp.int32)
        edges_out[d - 1] = edge
        edges.append(edge)

    @pl.loop(0, 4)
    def _(q_pair):
        q_lanes = pair_lanes(places, q_pair)
        query = both(places, qkv, slice(0, HD), q_lanes)
        q_pos = pair_positions(places, q_pair, 1)
        start = document_start(edges, q_pos)

        def scores(key, pos, lanes):
            return jnp.where(pos >= start[:, lanes], contract(key, query[:, lanes], ((0,), (0,))), neg_big)

        def mix_values(value, weights):
            return contract(value, weights.astype(bf16), ((1,), (0,)))

        def step(back, carry):
            top, total, mixed = carry
            k_lanes = pair_lanes(places, q_pair - back)
            key = both(places, qkv, slice(HD, 2 * HD), k_lanes)
            raw = scores(key, pair_positions(places, q_pair - back, 0), slice(0, 2 * TILE))
            new_top = jnp.maximum(top, jnp.max(raw, axis=0, keepdims=True))
            weights = jnp.exp(raw - new_top)
            fade = jnp.exp(top - new_top)
            total = total * fade + jnp.sum(weights, axis=0, keepdims=True)
            value = both(places, qkv, slice(2 * HD, 3 * HD), k_lanes)
            return new_top, total, mixed * fade + mix_values(value, weights)

        late = slice(TILE, 2 * TILE)
        k_pos = pair_positions(places, q_pair, 0)
        seen = []
        for k, (part, lanes) in enumerate(zip(in_order(places), (slice(0, 2 * TILE), late))):
            pos = k_pos[k * TILE : k * TILE + TILE]
            raw = scores(qkv[part, HD : 2 * HD, q_lanes], pos, lanes)
            seen.append(jnp.where(pos <= q_pos[:, lanes], raw, neg_big))
        top = jnp.max(seen[0], axis=0, keepdims=True)
        top_late = jnp.maximum(top[:, late], jnp.max(seen[1], axis=0, keepdims=True))
        top = jnp.concatenate([top[:, :TILE], top_late], axis=1)
        weights = [jnp.exp(seen[0] - top), jnp.exp(seen[1] - top_late)]
        total, total_late = [jnp.sum(part, axis=0, keepdims=True) for part in weights]
        mixed, mixed_late = [
            mix_values(qkv[part, 2 * HD : 3 * HD, q_lanes], weights[k])
            for k, part in enumerate(in_order(places))
        ]
        total = jnp.concatenate([total[:, :TILE], total[:, late] + total_late], axis=1)
        mixed = jnp.concatenate([mixed[:, :TILE], mixed[:, late] + mixed_late], axis=1)
        top, total, mixed = lax.fori_loop(1, pairs_of(edges, q_pair), step, (top, total, mixed))
        mixed = mixed / total
        lasting = jnp.broadcast_to(top + jnp.log(total), (8, 2 * TILE))
        low = mixed.astype(bf16)
        for k, part in enumerate(in_order(places)):
            lanes = slice(k * TILE, k * TILE + TILE)
            context_wide[part, :, q_lanes] = mixed[:, lanes]
            logsum[part, :, q_lanes] = lasting[:, lanes]
            for near in range(2):
                place = 4 * q_pair + 2 * k + (core if near == 0 else 1 - core)
                context[place] = low[:, k * TILE + 128 * near : k * TILE + 128 * near + 128]
        context.send(pl.ds(4 * q_pair, 4))
        for result in (context_wide, logsum):
            result.send(slice(None), slice(None), q_lanes)


def attend_back_kernel(
    places, edge_ref, qkv, context_wide, logsum, grad_context, cosine, sine, columns,
    grads_own, grads_far, columns_out, dk_acc, dv_acc, grads,
):
    core = places[2]
    columns_out[...] = columns[...]
    columns_out.send()
    edges = [edge_ref[d] for d in range(4)]

    @pl.loop(0, 4)
    def _(q_pair):
        q_lanes = pair_lanes(places, q_pair)
        query = both(places, qkv, slice(0, HD), q_lanes)
        q_pos = pair_positions(places, q_pair, 1)
        start = document_start(edges, q_pos)
        norm = both(places, logsum, slice(0, 1), q_lanes)
        blocks = []
        for place in (core, 1 - core, 2 + core, 3 - core):
            blocks.append(grad_context[4 * q_pair + place])
        grad = jnp.concatenate(blocks, axis=1)
        delta = jnp.sum(
            grad.astype(f32) * both(places, context_wide, slice(0, HD), q_lanes),
            axis=0, keepdims=True,
        )

        def back_tile(part, k_lanes, k_pos, lanes, own):
            key = qkv[part, HD : 2 * HD, k_lanes]
            value = qkv[part, 2 * HD : 3 * HD, k_lanes]
            raw = contract(key, query[:, lanes], ((0,), (0,)))
            dprobs = contract(value, grad[:, lanes], ((0,), (0,)))
            seen = k_pos >= start[:, lanes]
            if own:
                seen = seen & (k_pos <= q_pos[:, lanes])
            probs = jnp.exp(jnp.where(seen, raw, neg_big) - norm[:, lanes])
            draw = (probs * (dprobs - delta[:, lanes])).astype(bf16)
            dv = contract(grad[:, lanes], probs.astype(bf16), ((1,), (1,)))
            dk = contract(query[:, lanes], draw, ((1,), (1,)))
            dv_acc[part, :, k_lanes] = dv if own else dv_acc[part, :, k_lanes] + dv
            dk_acc[part, :, k_lanes] = dk if own else dk_acc[part, :, k_lanes] + dk
            return contract(key, draw, ((1,), (0,)))

        def step(back, dq):
            k_lanes = pair_lanes(places, q_pair - back)
            k_pos = pair_positions(places, q_pair - back, 0)
            for k, part in enumerate(in_order(places)):
                pos = k_pos[k * TILE : k * TILE + TILE]
                dq = dq + back_tile(part, k_lanes, pos, slice(0, 2 * TILE), False)
            return dq

        early, late = in_order(places)
        k_pos = pair_positions(places, q_pair, 0)
        dq = back_tile(early, q_lanes, k_pos[:TILE], slice(0, 2 * TILE), True)
        dq_late = back_tile(late, q_lanes, k_pos[TILE:], slice(TILE, 2 * TILE), True)
        dq = jnp.concatenate([dq[:, :TILE], dq[:, TILE:] + dq_late], axis=1)
        dq = lax.fori_loop(1, pairs_of(edges, q_pair), step, dq) * 0.125
        for k, part in enumerate(in_order(places)):
            cos, sin = cosine[part, :, q_lanes], sine[part, :, q_lanes]
            lanes = slice(k * TILE, k * TILE + TILE)
            grads[part, :, q_lanes] = turn_back(dq[:, lanes], cos, sin).astype(bf16)

    for part, target in enumerate((grads_own, grads_far)):
        target[0:HD] = grads[part]
        dk = turn_back(dk_acc[part], cosine[part], sine[part])
        target[HD : 2 * HD] = dk.astype(bf16)
        target[2 * HD : 3 * HD] = dv_acc[part].astype(bf16)
        if part == 0:
            grads_own.send()


def post_attend_own_kernel(blocks, out_own, context, half):
    for c in range(16):
        context[HD * HEAD_OF[c] : HD * HEAD_OF[c] + HD] = blocks[c]
    half[...] = contract(context[...], out_own[...], ((0,), (0,)))


def post_attend_kernel(
    places, mix_ref, context, half, out_other, streams, segments, normed2, branch1
):
    mix = Mix(mix_ref)
    live = live_column(segments)
    own, other = halves(places[2])
    branch1[:, other] = live * contract(context[...], out_other.wait()[...], ((0,), (0,)))
    branch1[:, own] = live * half[...]
    branch1.send()
    streams = streams.wait()
    of_streams = [mix.second_of_streams(r) for r in range(4)]
    of_branch = mix.second_of_branch()
    for c in range(4):
        rows = slice(32 * c, 32 * c + 32)
        second = weighted(
            [(of_streams[r], streams[r, rows].astype(f32)) for r in range(4)]
            + [(of_branch, branch1[rows])]
        )
        normed2[rows] = normalize(second)[0].astype(bf16)


def ready(value):
    return value.wait() if isinstance(value, Late) else value


def feed_forward_kernel(normed, grad_branch, weights, down, grad_normed, hidden, grad_gate, grad_up):
    tokens = ready(normed)[...].reshape(512, 1024)
    weights = ready(weights)
    gate = contract(tokens, weights[:, 0:SLICE], ((1,), (0,)))
    up = contract(tokens, weights[:, SLICE : 2 * SLICE], ((1,), (0,)))
    sigma = jax.nn.sigmoid(gate)
    silu = gate * sigma
    hidden[...] = (silu * up).astype(bf16)
    hidden.send()
    grad = contract(
        ready(grad_branch)[...].reshape(512, 1024), ready(down)[...], ((1,), (1,))
    )
    grad_of_gate = (grad * up * sigma * (1.0 + gate * (1.0 - sigma))).astype(bf16)
    grad_of_up = (grad * silu).astype(bf16)
    grad_gate[...] = grad_of_gate
    grad_up[...] = grad_of_up
    grad_gate.send()
    grad_up.send()
    total = contract(grad_of_gate, weights[:, 0:SLICE], ((1,), (1,)))
    total = total + contract(grad_of_up, weights[:, SLICE : 2 * SLICE], ((1,), (1,)))
    grad_normed[...] = total.astype(bf16).reshape(4, 128, 1024)


def branch2_kernel(hidden_own, hidden_other, down, context, own, other, context_out):
    context_out[...] = context[...]
    own[...] = contract(hidden_own[...], down[...], ((1,), (0,))).astype(bf16).reshape(4, 128, 1024)
    other[...] = (
        contract(hidden_other[...], down[...], ((1,), (0,))).astype(bf16).reshape(4, 128, 1024)
    )


def wide_tiles_kernel(
    places, gate_own, normed_own, gate_other, normed_other, up_own, up_other,
    hidden_own, grad_own, hidden_other, grad_other, out,
):
    def tile_of(left_own, right_own, left_other, right_other):
        tile = contract(left_own.wait()[...], right_own().reshape(512, 1024), ((0,), (0,)))
        return tile + contract(
            left_other.wait()[...], right_other().reshape(512, 1024), ((0,), (0,))
        )

    def slot(s):
        return 2 * (s % 4) + lax.rem(s // 4 + places[3] // 4, 2)

    def columns(j, tile):
        rows = slice(SLICE * j, SLICE * j + SLICE)
        for s in range(8):
            out[slot(s), rows] = tile[:, 128 * s : 128 * s + 128].astype(bf16)
        out.send(slice(None), rows)

    first = tile_of(
        gate_own, lambda: normed_own.wait()[...], gate_other, lambda: normed_other.wait()[...]
    )
    columns(0, first)
    second = tile_of(
        up_own, lambda: normed_own.ref[...], up_other, lambda: normed_other.ref[...]
    )
    columns(1, second)
    tile = tile_of(
        hidden_own, lambda: grad_own.wait()[...], hidden_other, lambda: grad_other.wait()[...]
    ).astype(bf16)
    for s in range(8):
        rows = tile[PLACE * s : PLACE * s + PLACE]
        for d in range(8):
            start = 2 * SLICE + PLACE * d
            out[slot(s), start : start + PLACE] = rows[:, 128 * d : 128 * d + 128]
    out.send(slice(None), slice(2 * SLICE, 3 * SLICE))


def second_back_kernel(
    places, mix_ref, t0, t1, t2, t3, streams, branch1, cotangent, segments, out_own, out_other,
    grad_second, grad_columns, grad_context, low, turned,
):
    mix = Mix(mix_ref)
    live = live_column(segments)
    of_streams = [mix.second_of_streams(r) for r in range(4)]
    of_branch = mix.second_of_branch()
    of_grad = [sum(mix.g[0][s] * mix.r[1][q][s] for s in range(4)) for q in range(4)]
    for c in range(4):
        rows = slice(32 * c, 32 * c + 32)
        second = weighted(
            [(of_streams[r], streams[r, rows].astype(f32)) for r in range(4)]
            + [(of_branch, branch1[rows])]
        )
        normed, inverse = normalize(second)
        grad = (t0[rows] + t1[rows].astype(f32)) + (t2[rows].astype(f32) + t3[rows].astype(f32))
        back = norm_back(grad, normed, inverse)
        grad_second[rows] = back
        grad_second.send(rows)
        if c == 0:
            cotangent = cotangent.wait()
        branch = weighted(
            [(of_grad[q], cotangent[q, rows].astype(f32)) for q in range(4)] + [(of_branch, back)]
        )
        low[rows] = (live[rows] * branch).astype(bf16)
    for i in range(8):
        grad_columns[2 * (i % 4) + i // 4] = low[:, 128 * i : 128 * i + 128]
    grad_columns.send()
    own, other = halves(places[2])
    turned[...] = contract(out_own.wait()[...], low[:, own], ((1,), (1,)))
    turned[...] += contract(out_other.wait()[...], low[:, other], ((1,), (1,)))
    for c in range(16):
        grad_context[c] = turned[HD * HEAD_OF[c] : HD * HEAD_OF[c] + HD].astype(bf16)
        if c % 4 == 3:
            grad_context.send(pl.ds(c - 3, 4))


def mix_sums_kernel(
    mix_ref, t0, t1, t2, t3, streams, cotangent, branch1, grad_second, segments,
    out, branch2, acc,
):
    mix = Mix(mix_ref)
    live = live_column(segments)
    acc[...] = jnp.zeros_like(acc)
    for c in range(4):
        rows = slice(32 * c, 32 * c + 32)
        branch2[rows] = live[rows] * (
            (t0[rows] + t1[rows].astype(f32)) + (t2[rows].astype(f32) + t3[rows].astype(f32))
        )
    branch2.send()

    def fold(values):
        return sum(values[:8, 128 * j : 128 * j + 128] for j in range(4)) + sum(
            values[8:, 128 * j : 128 * j + 128] for j in range(4)
        )

    @pl.loop(0, 8)
    def _(r):
        rows = pl.ds(pl.multiple_of(r * 16, 16), 16)

        @pl.loop(0, 2)
        def _(l):
            lanes = pl.ds(pl.multiple_of(l * 512, 512), 512)
            hin = [streams[s, rows, lanes].astype(f32) for s in range(4)]
            branch, back = branch1[rows, lanes], grad_second[rows, lanes]
            last = branch2[rows, lanes]
            for q in range(4):
                top = cotangent[q, rows, lanes].astype(f32)
                for s in range(4):
                    acc[4 * q + s] += fold(top * hin[s])
                acc[16 + q] += fold(top * branch)
                acc[20 + q] += fold(top * last)
            for s in range(4):
                acc[24 + s] += fold(hin[s] * back)
            acc[28] += fold(branch * back)

    total = jnp.sum(acc[...], axis=1)

    def top_hin(q, s):
        return total[4 * q + s : 4 * q + s + 1]

    def top_branch(q):
        return total[16 + q : 17 + q]

    def back_hin(s):
        return total[24 + s : 25 + s]

    back_branch = total[28:29]
    for s in range(4):
        out[s * 6 : s * 6 + 1] = jnp.zeros((1, 128), f32)
        for r in range(4):
            row = s * 6 + 1 + r
            out[row : row + 1] = weighted(
                [(mix.r[1][q][s], top_hin(q, r)) for q in range(4)]
                + [(mix.p[1][s], back_hin(r))]
            )
            row = 24 + s * 6 + 1 + r
            out[row : row + 1] = weighted(
                [(mix.r[0][r][q], top_hin(s, q)) for q in range(4)]
                + [(mix.g[0][r], top_branch(s))]
            )
        row = s * 6 + 5
        out[row : row + 1] = weighted(
            [(mix.r[1][q][s], top_branch(q)) for q in range(4)] + [(mix.p[1][s], back_branch)]
        )
        row = 24 + s * 6
        out[row : row + 1] = weighted(
            [(mix.r[0][s][q], back_hin(q)) for q in range(4)] + [(mix.g[0][s], back_branch)]
        )
        row = 24 + s * 6 + 5
        out[row : row + 1] = total[20 + s : 21 + s]


def out_streams_kernel(mix_ref, streams, branch1, branch2, out):
    mix = Mix(mix_ref)
    of_streams = [
        [sum(mix.r[1][s][q] * mix.r[0][q][r] for q in range(4)) for r in range(4)]
        for s in range(4)
    ]
    of_branch = [sum(mix.r[1][s][q] * mix.g[0][q] for q in range(4)) for s in range(4)]
    for c in range(4):
        rows = slice(32 * c, 32 * c + 32)
        hin = [streams[s, rows].astype(f32) for s in range(4)]
        for s in range(4):
            total = weighted(
                [(of_streams[s][r], hin[r]) for r in range(4)]
                + [(of_branch[s], branch1[rows]), (mix.g[1][s], branch2[rows])]
            )
            out[s, rows] = total.astype(bf16)


def near_lanes(values, near):
    return jnp.concatenate(
        [values[:, TILE * k + 128 * near : TILE * k + 128 * near + 128] for k in range(4)], axis=1
    )


def pair_back_kernel(places, own, far, weights, grad, pair):
    half = places[1]
    own = own.wait()
    for j in range(3):
        rows = slice(HD * j, HD * j + HD)
        pair[pl.ds(pl.multiple_of(128 * j + HD * half, HD), HD), :] = own[rows]
        pair[pl.ds(pl.multiple_of(128 * j + HD * (1 - half), HD), HD), :] = far[rows]
    total = contract(near_lanes(pair, 1), weights.wait()[...], ((0,), (0,)))
    grad[...] = total.astype(bf16).reshape(4, 128, 1024)


def pair_back_own_kernel(pair, weights, grad):
    total = contract(near_lanes(pair, 0), weights[...], ((0,), (0,)))
    grad[...] = total.astype(bf16).reshape(4, 128, 1024)


def narrow_tiles_kernel(
    places, pair, normed_own, normed_other, columns, context_own, context_other, out
):
    z, core = places[0], places[2]
    pair = pair.wait()
    tile = jnp.zeros((384, 1024), f32)
    for near, tokens in enumerate((normed_own, normed_other)):
        tokens = tokens.wait()[:, 0:128].reshape(512, 1024)
        tile = tile + contract(near_lanes(pair, near), tokens, ((1,), (0,)))
    for s in range(8):
        out[s, 0:384] = tile[:, 128 * s : 128 * s + 128].astype(bf16)
    tile = jnp.zeros((128, 1024), f32)
    for near, contexts in enumerate((context_own, context_other)):
        contexts = ready(contexts)
        for back in range(4):
            source = columns[2 * lax.rem(z - back + 4, 4) + lax.rem(core + near, 2)]
            tile = tile + contract(source, contexts[back], ((0,), (1,)))
    for s in range(8):
        out[s, 384:512] = tile[:, 128 * s : 128 * s + 128].astype(bf16)


def fold_kernel(blocks, *outs):
    start = 0
    for out in outs:
        rows = slice(start, start + out.shape[0])
        total = blocks[0, rows].astype(f32)
        for s in range(1, 8):
            total = total + blocks[s, rows].astype(f32)
        out[...] = total.astype(bf16)
        start += out.shape[0]


def fold_narrow_kernel(blocks, out):
    total = blocks[0].astype(f32)
    for s in range(1, 8):
        total = total + blocks[s].astype(f32)
    out[0:512] = total[0:512].astype(bf16)
    high, low = two_parts(total[512:513] + total[513:514])
    out[512:528] = jnp.concatenate([high, low, jnp.zeros((14, 128), bf16)], axis=0)


def add_narrow_kernel(own, far, out):
    total = own[...].astype(f32) + far[...].astype(f32)
    out[0:512] = total[0:512].astype(bf16)
    high, low = two_parts(total[512:513] + total[513:514])
    out[512:528] = jnp.concatenate([high, low, jnp.zeros((14, 128), bf16)], axis=0)


def member(places, own, other, index):
    back = lax.rem(places[0] - index % 4 + 4, 4)
    return jnp.where(places[2] == index // 4, own[back].astype(f32), other[back].astype(f32))


def finish_wide_kernel(places, own, other, gate_up, down, rows):
    for i in range(8):
        block = member(places, own, other, i)
        for s in range(8):
            for j in range(2):
                start = SLICE * j + PLACE * s
                unit = 8 * PIECE * s + PIECE * i
                rows[j, unit : unit + PIECE] = block[start : start + PIECE]
        for d in range(8):
            start = 2 * SLICE + PLACE * d
            down[PIECE * i : PIECE * i + PIECE, 128 * d : 128 * d + 128] = block[
                start : start + PIECE
            ]
    down.send()
    for j in range(2):
        for k in range(rows.shape[1] // 128):
            lanes = slice(128 * k, 128 * k + 128)
            gate_up[j, :, lanes] = rows[j, lanes].T
        gate_up.send(j)


def finish_narrow_kernel(places, own, other, qkv, out, mix_grad):
    total = jnp.zeros((1, 128), f32)
    for i in range(8):
        block = member(places, own, other, i)
        total = total + (block[512:513] + block[513:514])
        for j in range(3):
            qkv[j, :, 128 * i : 128 * i + 128] = block[128 * j : 128 * j + 128].T
        out[:, 128 * i : 128 * i + 128] = block[384:512].T
        if i % 2:
            lanes = slice(128 * i - 128, 128 * i + 128)
            qkv.send(slice(None), slice(None), lanes)
            out.send(slice(None), lanes)
    for m in range(2):
        for s in range(4):
            lane = m * 24 + s * 6
            mix_grad[m, s : s + 1, :] = total[:, lane : lane + 6]


def two_parts(values):
    high = values.astype(bf16)
    return high, (values - high.astype(f32)).astype(bf16)


def first_back_kernel(
    mix_ref, t0, t1, t2, t3, streams, cotangent, grad_second, sums, tiles, streams_grad, out, mix_rows
):
    mix = Mix(mix_ref)
    of_top = [
        [sum(mix.r[1][q][s] * mix.r[0][s][r] for s in range(4)) for q in range(4)]
        for r in range(4)
    ]
    of_back = [sum(mix.r[0][s][r] * mix.p[1][s] for s in range(4)) for r in range(4)]
    total = [jnp.zeros((1, 1024), f32) for _ in range(4)]
    out.send_from(tiles.wait(), slice(None), slice(0, 512))
    cotangent, grad_second = cotangent.wait(), grad_second.wait()
    for c in range(4):
        rows = slice(32 * c, 32 * c + 32)
        hin = [streams[s, rows].astype(f32) for s in range(4)]
        top = [cotangent[s, rows].astype(f32) for s in range(4)]
        normed, inverse = normalize(weighted([(mix.p[0][s], hin[s]) for s in range(4)]))
        grad = (t0[rows] + t1[rows].astype(f32)) + (t2[rows].astype(f32) + t3[rows].astype(f32))
        back1 = norm_back(grad, normed, inverse)
        back2 = grad_second[rows]
        for r in range(4):
            value = weighted(
                [(of_top[r][q], top[q]) for q in range(4)]
                + [(of_back[r], back2), (mix.p[0][r], back1)]
            )
            streams_grad[r, rows] = value.astype(bf16)
            total[r] = total[r] + jnp.sum(hin[r] * back1, axis=0, keepdims=True)
        streams_grad.send(slice(None), rows)
    mix_rows[0:48] = sums.wait()[...]
    mix_rows[48:] = jnp.zeros((80, 128), f32)
    for s in range(4):
        row = sum(total[s][:, 128 * k : 128 * k + 128] for k in range(8))
        mix_rows[s * 6 : s * 6 + 1] = row
    high, low = two_parts(jnp.sum(mix_rows[...].T, axis=0, keepdims=True))
    rows = jnp.concatenate([high, low, jnp.zeros((14, 128), bf16)], axis=0)
    for s in range(8):
        out[s, 512:528] = rows
    out.send(slice(None), slice(512, 528))


def split_kernel(source, own, other):
    own[...] = source[0]
    other[...] = source[1]


def copy_kernel(source, out):
    out[...] = source[...]


def add4_kernel(one, two, three, four, out):
    out[...] = (one[...] + two[...]) + (three[...] + four[...])


def add2_kernel(one, two, out):
    out[...] = (one[...].astype(f32) + two[...].astype(f32)).astype(out.dtype)


def shards(
    streams, segments, stream_mix, qkv_weight, out_weight, gate_up_weight, down_weight, cotangent
):
    kept_arrays.arrays.clear()
    z, half, core = lax.axis_index("z"), lax.axis_index("xh"), lax.axis_index("co")
    team, row = lax.axis_index(TEAM), lax.axis_index(SHARD)
    width = streams.shape[3]
    ff = down_weight.shape[0]
    places = (jnp.stack([z, half, core, row, team]).astype(jnp.int32), smem)
    mix = (stream_mix, smem)
    streams, cotangent, segments = streams[0], cotangent[0], (segments, vmem)
    token = ((128, width), bf16)
    token4 = ((4, 128, width), bf16)

    def v(*values):
        return [(value, vmem) for value in values]

    def h(*values):
        return [(value, "hbm") for value in values]

    def l(*values):
        return [(value, "late") for value in values]

    def stack(values, parts, name, us=1, order=(), beside=(), in_hbm=False, place="hbm"):
        (result,) = call(
            stack_kernel,
            [((4,) + values.shape, bf16, place)],
            (h(values) if in_hbm else v(values)) + v(*parts),
            name,
            us,
            order=order,
            beside=beside,
        )
        return result

    (weights,) = call(
        pick_kernel,
        [((128, 896 + 2 * SLICE), bf16, "early")],
        [places] + l(out_weight, down_weight, gate_up_weight),
        "pick",
        4,
    )
    far_weights = shift(weights, "xl", 1)

    (normed1,) = call(
        first_norm_kernel,
        [((144, width), bf16)],
        [mix] + h(streams) + [segments],
        "first_norm",
        3,
        order=[weights],
    )
    (qkv_blocks,) = call(
        pick_heads_kernel,
        [((8, 3, 128, 128), bf16, "early")],
        [places, (qkv_weight, raw)],
        "pick_heads",
        2,
        [pltpu.VMEM((3, 128, 128), bf16)],
        beside=[normed1],
    )
    qkv_blocks = lax.all_to_all(qkv_blocks, SHARD, 0, 0, tiled=True)
    normed1_z = z_issue(normed1)
    (weights,) = call(
        pair_weights_kernel,
        [((2, 128, 896 + 2 * SLICE), bf16, "hbm")],
        h(weights) + v(far_weights),
        "pair_weights",
        1,
        beside=[normed1],
    )
    weights = lax.all_gather(weights, "y", axis=0, tiled=True)
    normed1_own = stack(normed1, normed1_z, "stack_normed1", 4)
    normed1_other = shift(normed1_own, "co", 1)
    freq = rope_base ** (-(jnp.arange(32, dtype=f32) * 2.0) / HD)
    back, near, place = jnp.arange(4), jnp.arange(2), jnp.arange(128)
    positions = (
        512 * ((z - back[None, :, None, None] + 4) % 4)
        + 256 * ((half + near[:, None, None, None]) % 2)
        + 128 * ((core + near[None, None, :, None]) % 2)
        + place[None, None, None, :]
    ).reshape(2, 1, 1024)
    angle = positions.astype(f32) * freq[None, :, None]
    cosine, sine = jnp.cos(angle), jnp.sin(angle)

    (pair_weights,) = call(
        turn_heads_kernel, [((384, width), bf16, "early")], v(qkv_blocks), "turn_heads", 1
    )
    kept, sent = call(
        project_kernel,
        [((208, 1024), bf16, "vmem"), ((208, 1024), bf16, "vmem")],
        [places] + l(normed1_own) + v(normed1_other) + h(pair_weights) + v(cosine, sine),
        "project",
        16,
    )
    received = shift(sent, "xh", 1)
    (grad_branch2,) = call(
        grad_branch2_kernel,
        [token],
        [mix] + h(cotangent) + [segments],
        "grad_branch2",
        0,
        order=[kept],
    )
    grad2_z = z_issue(grad_branch2)

    qkv, context_blocks, context_wide, logsum, edges = call(
        attend_kernel,
        [
            ((2, 192, 1024), bf16, "early"),
            ((16, HD, 128), bf16, "early"),
            ((2, HD, 1024), f32, "early"),
            ((2, 8, 1024), f32, "early"),
            ((4,), jnp.int32),
        ],
        [places] + h(kept) + v(received),
        "attend",
        12,
        beside=[grad_branch2],
    )
    context_mine = lax.all_to_all(context_blocks, CTX, 0, 0, tiled=True)

    grad2_own = stack(grad_branch2, grad2_z, "stack_grad2", 1, [context_blocks])
    grad2_other = shift(grad2_own, "co", 1)
    (out_own,) = call(
        unpack_out_kernel,
        [((width, 512), bf16, "vmem")],
        [places, (weights, ("late", 0, 512))],
        "unpack_out",
        3,
        order=[grad2_own],
    )
    out_other = shift(out_own, "co", 1)
    context, branch_half = call(
        post_attend_own_kernel,
        [((width, 128), bf16, "vmem"), ((128, 512), f32, "vmem")],
        v(context_mine) + h(out_own),
        "post_attend_own",
        15,
    )
    normed2, branch1 = call(
        post_attend_kernel,
        [token, ((128, width), f32, "early")],
        [places, mix]
        + h(context)
        + v(branch_half)
        + l(out_other, streams)
        + [segments],
        "post_attend",
        3,
    )
    normed2_z = z_issue(normed2)
    inner = ("late", 512, 896 + 2 * SLICE)
    gu_all, down = call(
        unpack_kernel,
        [((width, 2 * SLICE), bf16, "vmem"), ((SLICE, width), bf16, "vmem")],
        [places, (weights, inner)],
        "unpack",
        4,
        order=[out_own],
    )
    normed2_own = stack(normed2, normed2_z, "stack_normed2", order=[down])
    normed2_other = shift(normed2_own, "co", 1)
    acts = [token4 + ("vmem",)] + [((512, SLICE), bf16, "early")] * 3
    grad_own, hidden_own, gate_own, up_own = call(
        feed_forward_kernel,
        acts,
        l(normed2_own, grad2_own, gu_all, down),
        "feed_forward_own",
        5,
    )
    grad_other, hidden_other, gate_other, up_other = call(
        feed_forward_kernel,
        acts,
        v(normed2_other) + l(grad2_other, gu_all, down),
        "feed_forward_other",
        5,
        order=[hidden_own],
    )

    def core_add(own, other, name, order, beside=(), own_in_hbm=False):
        return call(
            core_add_kernel,
            [((128, width), f32, "vmem")] + [token] * 3,
            (h(own) if own_in_hbm else v(own)) + v(shift(other, "co", 1)),
            name,
            1,
            order=order,
            beside=beside,
        )

    def z_terms(terms):
        return [terms[0]] + [shift(term, "z", -k) for k, term in enumerate(terms[1:], 1)]

    half_own, half_other, context = call(
        branch2_kernel,
        [token4 + ("vmem",), token4 + ("vmem",), ((width, 128), bf16, "vmem")],
        h(hidden_own, hidden_other, down, context),
        "branch2",
        3,
        order=[hidden_other],
    )
    terms = core_add(grad_own, grad_other, "core_add_second", [half_own])
    grad_normed2 = z_terms(terms)
    context_z = z_issue(context)

    grad_second, grad_columns, grad_context = call(
        second_back_kernel,
        [
            ((128, width), f32, "early"),
            ((8, 128, 128), bf16, "early"),
            ((16, HD, 128), bf16, "early"),
        ],
        [places, mix]
        + h(grad_normed2[0])
        + v(*grad_normed2[1:])
        + h(streams, branch1)
        + l(cotangent)
        + [segments] + l(out_own, out_other),
        "second_back",
        5,
        [pltpu.VMEM((128, width), bf16), pltpu.VMEM((width, 128), f32)],
    )
    grad_context = lax.all_to_all(grad_context, CTX, 0, 0, tiled=True)

    (wide_tiles,) = call(
        wide_tiles_kernel,
        [((8, 3 * SLICE, 128), bf16, "early")],
        [places] + l(
            gate_own, normed2_own, gate_other, normed2_other, up_own, up_other,
            hidden_own, grad2_own, hidden_other, grad2_other,
        ),
        "wide_tiles",
        7,
        order=[grad_second],
    )
    wide_mine = lax.psum_scatter(wide_tiles, "y", scatter_dimension=0, tiled=True)

    terms = core_add(half_own, half_other, "core_add_branch2", [wide_tiles], own_in_hbm=True)
    branch2 = z_terms(terms)
    grads_own, grads_far, columns = call(
        attend_back_kernel,
        [((192, 1024), bf16, "early"), ((192, 1024), bf16, "vmem"), ((8, 128, 128), bf16, "early")],
        [places, (edges, smem)]
        + h(qkv, context_wide, logsum)
        + v(grad_context, cosine, sine)
        + h(grad_columns),
        "attend_back",
        40,
        [
            pltpu.VMEM((2, HD, 1024), f32),
            pltpu.VMEM((2, HD, 1024), f32),
            pltpu.VMEM((2, HD, 1024), bf16),
        ],
        [terms[0]],
    )
    received = shift(grads_far, "xh", 1)
    columns = lax.all_to_all(columns, ("z", "co"), 0, 0, tiled=True)
    sums, branch2 = call(
        mix_sums_kernel,
        [((48, 128), f32, "vmem"), ((128, width), f32, "early")],
        [mix]
        + h(branch2[0])
        + v(*branch2[1:])
        + h(streams, cotangent, branch1, grad_second)
        + [segments],
        "mix_sums",
        7,
        [pltpu.VMEM((32, 8, 128), f32)],
        [grads_own],
        context_z,
    )
    context_own = stack(context, context_z, "stack_context", 1, [sums], in_hbm=True, place="vmem")
    context_other = shift(context_own, "co", 1)
    wide_type = ((3 * SLICE, 128), bf16)
    wide_mine, wide_far = call(
        split_kernel, [wide_type, wide_type], h(wide_mine), "split_wide", 1, order=[context_own]
    )
    wide_far = shift(wide_far, "xl", 1)
    grad_other, pair = call(
        pair_back_kernel,
        [token4 + ("vmem",), ((384, 1024), bf16, "vmem")],
        [places] + l(grads_own) + v(received) + l(pair_weights),
        "pair_back",
        4,
        order=[context_own],
        beside=[columns, wide_mine],
    )
    (grad_own,) = call(
        pair_back_own_kernel, [token4 + ("vmem",)], h(pair, pair_weights), "pair_back_own", 3
    )
    terms = core_add(grad_own, grad_other, "core_add_first", [])
    grad_normed1 = z_terms(terms)

    (narrow_tiles,) = call(
        narrow_tiles_kernel,
        [((8, 512, 128), bf16, "vmem")],
        [places]
        + l(pair, normed1_own, normed1_other)
        + v(columns)
        + l(context_own)
        + v(context_other),
        "narrow_tiles",
        6,
        order=[terms[0]],
    )
    narrow_order = narrow_tiles
    (wide_rows,) = call(
        add2_kernel, [wide_type], v(wide_mine, wide_far), "add_wide_xl", 1, order=[narrow_order], beside=grad_normed1[1:]
    )
    wide_far = shift(wide_rows, "xh", 1)
    streams_grad, narrow_tiles = call(
        first_back_kernel,
        [token4 + ("early",), ((8, 528, 128), bf16, "early")],
        [mix]
        + h(grad_normed1[0])
        + v(*grad_normed1[1:])
        + h(streams)
        + l(cotangent, grad_second, sums, narrow_tiles),
        "first_back",
        6,
        [pltpu.VMEM((128, 128), f32)],
    )
    narrow_tiles = lax.all_to_all(narrow_tiles, SHARD, 0, 0, tiled=True)

    (wide_rows,) = call(
        add2_kernel, [wide_type], v(wide_rows, wide_far), "add_wide", 1, order=[streams_grad]
    )
    wide_z = z_issue(wide_rows)
    (out_streams,) = call(
        out_streams_kernel,
        [token4 + ("hbm",)],
        [mix] + h(streams, branch1, branch2),
        "out_streams",
        8,
        beside=[wide_rows],
    )
    narrow_type = [((528, 128), bf16)]
    (mine,) = call(fold_narrow_kernel, narrow_type, v(narrow_tiles), "fold_narrow", 1, order=[out_streams])
    narrow_far = shift(mine, "xh", 1)
    wide_own = stack(wide_rows, wide_z, "stack_wide", 1, beside=[mine])
    wide_other = shift(wide_own, "co", 1)
    (narrow_rows,) = call(
        add_narrow_kernel, narrow_type, v(mine, narrow_far), "add_narrow", 1, order=[wide_own]
    )
    narrow_z = z_issue(narrow_rows)
    gate_up_grad, down_grad = call(
        finish_wide_kernel,
        [((2, 128, 8 * ff), f32, "early"), ((ff, width), f32, "early")],
        [places] + h(wide_own) + v(wide_other),
        "finish_wide",
        5,
        [pltpu.VMEM((2, 8 * ff, 128), f32)],
        beside=[narrow_rows],
    )
    narrow_own = stack(narrow_rows, narrow_z, "stack_narrow", 1, [down_grad])
    narrow_other = shift(narrow_own, "co", 1)
    qkv_grad, out_grad, mix_grad = call(
        finish_narrow_kernel,
        [((3, 128, width), f32, "early"), ((128, width), f32, "early"), ((2, 4, 6), f32)],
        [places] + h(narrow_own) + v(narrow_other),
        "finish_narrow",
        3,
    )
    return (
        out_streams[None], streams_grad[None], qkv_grad, out_grad, gate_up_grad, down_grad, mix_grad,
    )


def solution(mesh):
    fine = Mesh(
        np.asarray(mesh.devices).reshape([n for _, n in AXES]), tuple(name for name, _ in AXES)
    )
    in_specs = (
        P(SHARD, None, CTX, None),
        P(SHARD, CTX),
        P(),
        P(None, SHARD, None),
        P(SHARD, None),
        P(None, SHARD, None),
        P(SHARD, None),
        P(SHARD, None, CTX, None),
    )
    out_specs = (
        P(SHARD, None, CTX, None),
        P(SHARD, None, CTX, None),
        P(None, SHARD, None),
        P(SHARD, None),
        P(None, SHARD, None),
        P(SHARD, None),
        P(),
    )
    return jax.shard_map(shards, mesh=fine, in_specs=in_specs, out_specs=out_specs, check_vma=False)
```

```python
import jax
import jax.numpy as jnp
import numpy as np
from jax import lax
from jax.experimental import pallas as pl
from jax.experimental.pallas import tpu as pltpu
from jax.sharding import Mesh
from jax.sharding import PartitionSpec as P

HD = 64
TILE = 256
VMEM = 24 * 1024 * 1024
COST = 1.1e9
PIECE = 44
PLACE = 48
SLICE = 8 * PLACE
eps = 1e-05
rope_base = 1000000.0
neg_big = -1e30
bf16 = jnp.bfloat16
f32 = jnp.float32
smem = pl.BlockSpec(memory_space=pltpu.SMEM)
vmem = pl.BlockSpec(memory_space=pltpu.VMEM)
anywhere = pl.BlockSpec(memory_space=pl.ANY)
hbm = pl.BlockSpec(memory_space=pltpu.HBM)
raw = pl.BlockSpec(memory_space=pltpu.HBM)

AXES = (("z", 4), ("xh", 2), ("co", 2), ("xl", 2), ("y", 4))
SIZE = dict(AXES)
CTX = ("z", "xh", "co")
SHARD = ("xl", "y")
TEAM = ("co", "z")
HEAD_OF = [8 * (c % 2) + 2 * (c // 4) + (c // 2) % 2 for c in range(16)]


class Kept:
    def __init__(self):
        self.arrays = []

    def add(self, array):
        self.arrays.append(array)
        return array

    def __contains__(self, array):
        return any(array is other for other in self.arrays)


kept_arrays = Kept()


def shift(values, axis, amount):
    count = SIZE[axis]
    moved = lax.ppermute(values, axis, [(i, (i + amount) % count) for i in range(count)])
    if axis == "co" and values in kept_arrays:
        kept_arrays.add(moved)
    return moved


def z_issue(values):
    return [shift(values, "z", k) for k in range(1, 4)]


class Late:
    def __init__(self, copy, ref):
        self.copy, self.ref = copy, ref

    def wait(self):
        if self.copy is not None:
            self.copy.wait()
        return self.ref


class Early:
    def __init__(self, ref, target, sem):
        self.ref, self.target, self.sem = ref, target, sem

    def __getitem__(self, where):
        return self.ref[where]

    def __setitem__(self, where, value):
        self.ref[where] = value

    def send(self, *where):
        self.send_from(self.ref.at[where] if where else self.ref, *where)

    def send_from(self, source, *where):
        target = self.target.at[where] if where else self.target
        pltpu.make_async_copy(source, target, self.sem).start()


def call(kernel, outs, ins, name, us, scratch=(), order=(), beside=()):
    known = (smem, vmem, raw)
    stays = [value in kept_arrays and place not in (smem, raw) for value, place in ins]
    extra_ins = len(order) + len(beside)
    ends = len(ins), len(ins) + extra_ins, len(ins) + extra_ins + len(outs)
    near = [k for k, (_, place) in enumerate(ins) if place not in known and not stays[k]]
    far = [k for k, out in enumerate(outs) if len(out) > 2 and out[2] != "vmem"]

    def part(k):
        value, place = ins[k]
        if isinstance(place, tuple):
            return value.shape[:-1] + (place[2] - place[1],)
        return value.shape

    def body(*refs):
        given, results, rest = list(refs[: ends[0]]), list(refs[ends[1] : ends[2]]), refs[ends[2] :]
        rest, sems = (rest[:-1], rest[-1]) if near or far else (rest, None)
        loaded = rest[len(scratch) : len(scratch) + len(near)]
        staged = rest[len(scratch) + len(near) :]
        for k, (_, place) in enumerate(ins):
            if stays[k] and place == "late":
                given[k] = Late(None, given[k])
        copies, waits = [], []
        for j, (k, ref) in enumerate(zip(near, loaded)):
            source, place = given[k], ins[k][1]
            if isinstance(place, tuple):
                source = source.at[..., place[1] : place[2]]
            copies.append(pltpu.make_async_copy(source, ref, sems.at[j]))
            if (place[0] if isinstance(place, tuple) else place) == "hbm":
                waits.append(copies[-1])
                given[k] = ref
            else:
                given[k] = Late(copies[-1], ref)
        for copy in copies:
            copy.start()
        for copy in waits:
            copy.wait()
        copies = []
        for j, (k, ref) in enumerate(zip(far, staged)):
            sem = sems.at[len(near) + j]
            copies.append(pltpu.make_async_copy(ref, results[k], sem))
            results[k] = Early(ref, results[k], sem) if outs[k][2] == "early" else ref
        kernel(*given, *results, *rest[: len(scratch)])
        for copy, k in zip(copies, far):
            if outs[k][2] != "early":
                copy.start()
        for copy in copies:
            copy.wait()

    extra = [pltpu.VMEM(part(k), ins[k][0].dtype) for k in near]
    extra += [pltpu.VMEM(outs[k][0], outs[k][1]) for k in far]
    if near or far:
        extra.append(pltpu.SemaphoreType.DMA((len(near) + len(far),)))

    def in_hbm(value):
        return pltpu.with_memory_space_constraint(value, pltpu.HBM)

    def out_type(out):
        if len(out) > 2 and out[2] == "vmem":
            return pltpu.VMEM(out[0], out[1])
        if len(out) > 2:
            return pltpu.HBM(out[0], out[1])
        return jax.ShapeDtypeStruct(out[0], out[1])

    def in_vmem(value):
        return pltpu.with_memory_space_constraint(value, pltpu.VMEM)

    def spec(k):
        return vmem if stays[k] else ins[k][1] if ins[k][1] in known else hbm

    def placed(k):
        value, place = ins[k]
        return in_vmem(value) if stays[k] else value if place in (smem, vmem) else in_hbm(value)

    results = pl.pallas_call(
        body,
        out_shape=tuple(out_type(out) for out in outs),
        in_specs=[spec(k) for k in range(len(ins))]
        + [anywhere if value in kept_arrays else hbm for value in order]
        + [anywhere] * len(beside),
        out_specs=tuple(
            hbm if k in far else smem if out[1] == jnp.int32 else vmem
            for k, out in enumerate(outs)
        ),
        scratch_shapes=list(scratch) + extra,
        compiler_params=pltpu.CompilerParams(vmem_limit_bytes=VMEM),
        cost_estimate=pl.CostEstimate(
            flops=int(us * COST), bytes_accessed=0, transcendentals=0
        ),
        name=name,
    )(
        *[placed(k) for k in range(len(ins))],
        *[value if value in kept_arrays else in_hbm(value) for value in order],
        *beside,
    )
    for out, result in zip(outs, results):
        if len(out) > 2 and out[2] == "vmem":
            kept_arrays.add(result)
    return results


def contract(left, right, dims):
    return lax.dot_general(left, right, (dims, ((), ())), preferred_element_type=f32)


def normalize(values):
    centered = values - jnp.mean(values, axis=-1, keepdims=True)
    inverse = lax.rsqrt(jnp.mean(centered * centered, axis=-1, keepdims=True) + eps)
    return (centered * inverse, inverse)


def norm_back(grad, normed, inverse):
    return inverse * (
        grad
        - jnp.mean(grad, axis=-1, keepdims=True)
        - normed * jnp.mean(grad * normed, axis=-1, keepdims=True)
    )


def weighted(terms):
    total = None
    for weight, values in terms:
        part = weight * values
        total = part if total is None else total + part
    return total


def live_column(segments):
    wide = jnp.broadcast_to((segments[...] > 0).astype(f32), (128, 128))
    return wide.T[:, 0:1]


class Mix:
    def __init__(self, ref):
        self.p = [[ref[m, s, 0] for s in range(4)] for m in range(2)]
        self.r = [[[ref[m, s, 1 + r] for r in range(4)] for s in range(4)] for m in range(2)]
        self.g = [[ref[m, s, 5] for s in range(4)] for m in range(2)]

    def second_of_streams(self, r):
        return sum(self.p[1][s] * self.r[0][s][r] for s in range(4))

    def second_of_branch(self):
        return sum(self.p[1][s] * self.g[0][s] for s in range(4))


def core_add_kernel(own, received, first, *rest):
    first[...] = own[0].astype(f32) + received[0].astype(f32)
    for k, target in enumerate(rest, 1):
        target[...] = (own[k].astype(f32) + received[k].astype(f32)).astype(bf16)


def first_norm_kernel(mix_ref, streams, segments, out):
    mix = Mix(mix_ref)
    for c in range(4):
        rows = slice(32 * c, 32 * c + 32)
        first = weighted([(mix.p[0][s], streams[s, rows].astype(f32)) for s in range(4)])
        out[rows] = normalize(first)[0].astype(bf16)
    out[128:144] = jnp.zeros((16, 1024), bf16)
    out[128:144, 0:128] = jnp.broadcast_to(segments[...].astype(f32), (16, 128)).astype(bf16)


def pick_heads_kernel(places, weights, out, block):
    pltpu.sync_copy(
        weights.at[:, :, pl.ds(pl.multiple_of(places[4] * 128, 128), 128)], block
    )
    for s in range(8):
        out.send_from(block, s)


def pieces(d):
    start, place, result = PLACE * d, 0, []
    while place < PLACE:
        count = min(PLACE - place, 128 - start % 128)
        result.append((place, start // 128, start % 128, count))
        start, place = start + count, place + count
    return result


def pick_kernel(places, out_weight, down, gate_up, wide):
    team, core = places[4], places[2]
    own, _ = halves(core)
    wide[:, 0:512] = out_weight.wait()[:, own]
    start = jnp.minimum(team * PIECE // 16 * 16, 8 * PIECE - 64)
    place = lax.broadcasted_iota(jnp.int32, (PLACE, 1), 0)
    wanted = jnp.where(place < PIECE, place + (team * PIECE - start), -1)
    unit = lax.broadcasted_iota(jnp.int32, (1, 64), 1)
    picked = jnp.where(unit == wanted, 1.0, 0.0).astype(bf16)
    down = down.wait()[pl.ds(pl.multiple_of(start, 16), 64)]
    rows = contract(picked, down, ((1,), (0,))).astype(bf16)
    for d in range(8):
        for place, tile, start, count in pieces(d):
            lanes = slice(512 + 128 * tile, 512 + 128 * tile + 128)
            wide[start : start + count, lanes] = rows[
                place : place + count, 128 * d : 128 * d + 128
            ]
    wide.send(slice(None), slice(0, 896))
    units = gate_up.ref.shape[2] // 2
    unit = lax.broadcasted_iota(jnp.int32, (units, 1), 0)
    place = lax.broadcasted_iota(jnp.int32, (1, SLICE // 2), 1)
    piece = lax.rem(place, PLACE)
    wanted = (place // PLACE) * (8 * PIECE) + team * PIECE + piece
    wanted = jnp.where(piece < PIECE, wanted, -1)
    picked = jnp.where(unit == wanted, 1.0, 0.0).astype(bf16)
    gate_up = gate_up.wait()
    for j in range(2):
        columns = [
            contract(gate_up[j, :, units * k : units * k + units], picked, ((1,), (0,))).astype(bf16)
            for k in range(2)
        ]
        lanes = slice(896 + SLICE * j, 896 + SLICE * j + SLICE)
        wide[:, lanes] = jnp.concatenate(columns, axis=1)
        wide.send(slice(None), lanes)


def halves(core):
    own = pl.ds(pl.multiple_of(core * 512, 512), 512)
    other = pl.ds(pl.multiple_of((1 - core) * 512, 512), 512)
    return own, other


def pair_weights_kernel(near, far, out):
    out[0] = near[...]
    out[1] = far[...]


def unpack_out_kernel(places, weights, out):
    weights = weights.wait()
    for part in range(2):
        for y in range(4):
            s = 4 * lax.rem(places[3] // 4 + part, 2) + y
            out[pl.ds(pl.multiple_of(128 * s, 128), 128)] = weights[2 * y + part]


def unpack_kernel(places, weights, gate_up, down):
    weights = weights.wait()
    for part in range(2):
        for y in range(4):
            s = 4 * lax.rem(places[3] // 4 + part, 2) + y
            block = weights[2 * y + part]
            gate_up[pl.ds(pl.multiple_of(128 * s, 128), 128)] = block[:, 384:]
            for d in range(8):
                for place, tile, start, count in pieces(d):
                    row = pl.multiple_of(PLACE * s + place, 16)
                    down[pl.ds(row, count), 128 * d : 128 * d + 128] = block[
                        start : start + count, 128 * tile : 128 * tile + 128
                    ]


def grad_branch2_kernel(mix_ref, cotangent, segments, out):
    mix = Mix(mix_ref)
    live = live_column(segments)
    for c in range(4):
        rows = slice(32 * c, 32 * c + 32)
        total = weighted([(mix.g[1][s], cotangent[s, rows].astype(f32)) for s in range(4)])
        out[rows] = (live[rows] * total).astype(bf16)


def turn(values, cosine, sine):
    one, two = values[:32], values[32:]
    return jnp.concatenate([one * cosine - two * sine, two * cosine + one * sine], axis=0)


def turn_back(grad, cosine, sine):
    one, two = grad[:32], grad[32:]
    return jnp.concatenate([one * cosine + two * sine, two * cosine - one * sine], axis=0)


def turn_heads_kernel(weights, out):
    for j in range(3):
        rows = slice(128 * j, 128 * j + 128)
        for s in range(8):
            out[rows, 128 * s : 128 * s + 128] = weights[s, j].T
        out.send(rows)


def stack_kernel(first, second, third, fourth, out):
    for k, part in enumerate((first, second, third, fourth)):
        out[k] = part[...]


def project_kernel(places, own, other, wide, cosine, sine, kept, sent):
    half = places[1]

    def rows(head):
        return [wide[pl.ds(pl.multiple_of(128 * j + HD * head, HD), HD), :] for j in range(3)]

    mine = jnp.concatenate(rows(half) + rows(1 - half), axis=0)
    for near, tokens in enumerate((own, other)):
        tokens = ready(tokens)
        blocks = contract(mine, tokens[:, 0:128].reshape(512, 1024), ((1,), (1,)))
        for back in range(4):
            lanes = slice(back * TILE + near * 128, back * TILE + near * 128 + 128)
            block = blocks[:, 128 * back : 128 * back + 128]
            segs = tokens[back, 128:144, 0:128]
            cos, sin = cosine[0, :, lanes], sine[0, :, lanes]
            for target, base in ((kept, 0), (sent, 192)):
                query = turn(block[base : base + 64], cos, sin).astype(bf16)
                target[0:64, lanes] = (query.astype(f32) * 0.125).astype(bf16)
                target[64:128, lanes] = turn(block[base + 64 : base + 128], cos, sin).astype(bf16)
                target[128:192, lanes] = block[base + 128 : base + 192].astype(bf16)
                target[192:208, lanes] = segs


def pair_lanes(places, pair):
    back = lax.rem(places[0] - pair + 4, 4)
    return pl.ds(pl.multiple_of(back * TILE, TILE), TILE)


def in_order(places):
    return places[1], 1 - places[1]


def both(places, ref, rows, lanes):
    return jnp.concatenate([ref[part, rows, lanes] for part in in_order(places)], axis=1)


def pair_positions(places, pair, axis):
    local = lax.broadcasted_iota(jnp.int32, (TILE, 1) if axis == 0 else (1, TILE), axis)
    first = (local + places[2] * 128) % TILE + 2 * TILE * pair
    return jnp.concatenate([first, first + TILE], axis=axis)


def document_start(edges, place):
    start = jnp.zeros_like(place)
    for edge in edges:
        start = jnp.where(place >= edge, edge, start)
    return start


def pairs_of(edges, pair):
    return pair - document_start(edges, 2 * TILE * pair) // (2 * TILE) + 1


def attend_kernel(places, kept, received, qkv, context, context_wide, logsum, edges_out):
    core = places[2]
    qkv[0] = kept[0:192]
    qkv[1] = received[0:192]
    qkv.send()
    seg_own = kept[192:208].astype(f32)
    seg_far = received[192:208].astype(f32)
    edges = []
    for d in range(1, 5):
        count = jnp.float32(0)
        for seg in (seg_own, seg_far):
            inside = (seg > 0.5) & (seg < d + 0.5)
            count = count + jnp.sum(jnp.where(inside, 0.0625, 0.0))
        edge = count.astype(jnp.int32)
        edges_out[d - 1] = edge
        edges.append(edge)

    @pl.loop(0, 4)
    def _(q_pair):
        q_lanes = pair_lanes(places, q_pair)
        query = both(places, qkv, slice(0, HD), q_lanes)
        q_pos = pair_positions(places, q_pair, 1)
        start = document_start(edges, q_pos)

        def scores(key, pos, lanes):
            return jnp.where(pos >= start[:, lanes], contract(key, query[:, lanes], ((0,), (0,))), neg_big)

        def mix_values(value, weights):
            return contract(value, weights.astype(bf16), ((1,), (0,)))

        def step(back, carry):
            top, total, mixed = carry
            k_lanes = pair_lanes(places, q_pair - back)
            key = both(places, qkv, slice(HD, 2 * HD), k_lanes)
            raw = scores(key, pair_positions(places, q_pair - back, 0), slice(0, 2 * TILE))
            new_top = jnp.maximum(top, jnp.max(raw, axis=0, keepdims=True))
            weights = jnp.exp(raw - new_top)
            fade = jnp.exp(top - new_top)
            total = total * fade + jnp.sum(weights, axis=0, keepdims=True)
            value = both(places, qkv, slice(2 * HD, 3 * HD), k_lanes)
            return new_top, total, mixed * fade + mix_values(value, weights)

        late = slice(TILE, 2 * TILE)
        k_pos = pair_positions(places, q_pair, 0)
        seen = []
        for k, (part, lanes) in enumerate(zip(in_order(places), (slice(0, 2 * TILE), late))):
            pos = k_pos[k * TILE : k * TILE + TILE]
            raw = scores(qkv[part, HD : 2 * HD, q_lanes], pos, lanes)
            seen.append(jnp.where(pos <= q_pos[:, lanes], raw, neg_big))
        top = jnp.max(seen[0], axis=0, keepdims=True)
        top_late = jnp.maximum(top[:, late], jnp.max(seen[1], axis=0, keepdims=True))
        top = jnp.concatenate([top[:, :TILE], top_late], axis=1)
        weights = [jnp.exp(seen[0] - top), jnp.exp(seen[1] - top_late)]
        total, total_late = [jnp.sum(part, axis=0, keepdims=True) for part in weights]
        mixed, mixed_late = [
            mix_values(qkv[part, 2 * HD : 3 * HD, q_lanes], weights[k])
            for k, part in enumerate(in_order(places))
        ]
        total = jnp.concatenate([total[:, :TILE], total[:, late] + total_late], axis=1)
        mixed = jnp.concatenate([mixed[:, :TILE], mixed[:, late] + mixed_late], axis=1)
        top, total, mixed = lax.fori_loop(1, pairs_of(edges, q_pair), step, (top, total, mixed))
        mixed = mixed / total
        lasting = jnp.broadcast_to(top + jnp.log(total), (8, 2 * TILE))
        low = mixed.astype(bf16)
        for k, part in enumerate(in_order(places)):
            lanes = slice(k * TILE, k * TILE + TILE)
            context_wide[part, :, q_lanes] = mixed[:, lanes]
            logsum[part, :, q_lanes] = lasting[:, lanes]
            for near in range(2):
                place = 4 * q_pair + 2 * k + (core if near == 0 else 1 - core)
                context[place] = low[:, k * TILE + 128 * near : k * TILE + 128 * near + 128]
        context.send(pl.ds(4 * q_pair, 4))
        for result in (context_wide, logsum):
            result.send(slice(None), slice(None), q_lanes)


def attend_back_kernel(
    places, edge_ref, qkv, context_wide, logsum, grad_context, cosine, sine, columns,
    grads_own, grads_far, columns_out, dk_acc, dv_acc, grads,
):
    core = places[2]
    columns_out[...] = columns[...]
    columns_out.send()
    edges = [edge_ref[d] for d in range(4)]

    @pl.loop(0, 4)
    def _(q_pair):
        q_lanes = pair_lanes(places, q_pair)
        query = both(places, qkv, slice(0, HD), q_lanes)
        q_pos = pair_positions(places, q_pair, 1)
        start = document_start(edges, q_pos)
        norm = both(places, logsum, slice(0, 1), q_lanes)
        blocks = []
        for place in (core, 1 - core, 2 + core, 3 - core):
            blocks.append(grad_context[4 * q_pair + place])
        grad = jnp.concatenate(blocks, axis=1)
        delta = jnp.sum(
            grad.astype(f32) * both(places, context_wide, slice(0, HD), q_lanes),
            axis=0, keepdims=True,
        )

        def back_tile(part, k_lanes, k_pos, lanes, own):
            key = qkv[part, HD : 2 * HD, k_lanes]
            value = qkv[part, 2 * HD : 3 * HD, k_lanes]
            raw = contract(key, query[:, lanes], ((0,), (0,)))
            dprobs = contract(value, grad[:, lanes], ((0,), (0,)))
            seen = k_pos >= start[:, lanes]
            if own:
                seen = seen & (k_pos <= q_pos[:, lanes])
            probs = jnp.exp(jnp.where(seen, raw, neg_big) - norm[:, lanes])
            draw = (probs * (dprobs - delta[:, lanes])).astype(bf16)
            dv = contract(grad[:, lanes], probs.astype(bf16), ((1,), (1,)))
            dk = contract(query[:, lanes], draw, ((1,), (1,)))
            dv_acc[part, :, k_lanes] = dv if own else dv_acc[part, :, k_lanes] + dv
            dk_acc[part, :, k_lanes] = dk if own else dk_acc[part, :, k_lanes] + dk
            return contract(key, draw, ((1,), (0,)))

        def step(back, dq):
            k_lanes = pair_lanes(places, q_pair - back)
            k_pos = pair_positions(places, q_pair - back, 0)
            for k, part in enumerate(in_order(places)):
                pos = k_pos[k * TILE : k * TILE + TILE]
                dq = dq + back_tile(part, k_lanes, pos, slice(0, 2 * TILE), False)
            return dq

        early, late = in_order(places)
        k_pos = pair_positions(places, q_pair, 0)
        dq = back_tile(early, q_lanes, k_pos[:TILE], slice(0, 2 * TILE), True)
        dq_late = back_tile(late, q_lanes, k_pos[TILE:], slice(TILE, 2 * TILE), True)
        dq = jnp.concatenate([dq[:, :TILE], dq[:, TILE:] + dq_late], axis=1)
        dq = lax.fori_loop(1, pairs_of(edges, q_pair), step, dq) * 0.125
        for k, part in enumerate(in_order(places)):
            cos, sin = cosine[part, :, q_lanes], sine[part, :, q_lanes]
            lanes = slice(k * TILE, k * TILE + TILE)
            grads[part, :, q_lanes] = turn_back(dq[:, lanes], cos, sin).astype(bf16)

    for part, target in enumerate((grads_own, grads_far)):
        target[0:HD] = grads[part]
        dk = turn_back(dk_acc[part], cosine[part], sine[part])
        target[HD : 2 * HD] = dk.astype(bf16)
        target[2 * HD : 3 * HD] = dv_acc[part].astype(bf16)
        if part == 0:
            grads_own.send()


def post_attend_own_kernel(blocks, out_own, context, half):
    for c in range(16):
        context[HD * HEAD_OF[c] : HD * HEAD_OF[c] + HD] = blocks[c]
    half[...] = contract(context[...], out_own[...], ((0,), (0,)))


def post_attend_kernel(
    places, mix_ref, context, half, out_other, streams, segments, normed2, branch1
):
    mix = Mix(mix_ref)
    live = live_column(segments)
    own, other = halves(places[2])
    branch1[:, other] = live * contract(context[...], out_other.wait()[...], ((0,), (0,)))
    branch1[:, own] = live * half[...]
    branch1.send()
    streams = streams.wait()
    of_streams = [mix.second_of_streams(r) for r in range(4)]
    of_branch = mix.second_of_branch()
    for c in range(4):
        rows = slice(32 * c, 32 * c + 32)
        second = weighted(
            [(of_streams[r], streams[r, rows].astype(f32)) for r in range(4)]
            + [(of_branch, branch1[rows])]
        )
        normed2[rows] = normalize(second)[0].astype(bf16)


def ready(value):
    return value.wait() if isinstance(value, Late) else value


def feed_forward_kernel(normed, grad_branch, weights, down, grad_normed, hidden, grad_gate, grad_up):
    tokens = ready(normed)[...].reshape(512, 1024)
    weights = ready(weights)
    gate = contract(tokens, weights[:, 0:SLICE], ((1,), (0,)))
    up = contract(tokens, weights[:, SLICE : 2 * SLICE], ((1,), (0,)))
    sigma = jax.nn.sigmoid(gate)
    silu = gate * sigma
    hidden[...] = (silu * up).astype(bf16)
    hidden.send()
    grad = contract(
        ready(grad_branch)[...].reshape(512, 1024), ready(down)[...], ((1,), (1,))
    )
    grad_of_gate = (grad * up * sigma * (1.0 + gate * (1.0 - sigma))).astype(bf16)
    grad_of_up = (grad * silu).astype(bf16)
    grad_gate[...] = grad_of_gate
    grad_up[...] = grad_of_up
    grad_gate.send()
    grad_up.send()
    total = contract(grad_of_gate, weights[:, 0:SLICE], ((1,), (1,)))
    total = total + contract(grad_of_up, weights[:, SLICE : 2 * SLICE], ((1,), (1,)))
    grad_normed[...] = total.astype(bf16).reshape(4, 128, 1024)


def branch2_kernel(hidden_own, hidden_other, down, context, own, other, context_out):
    context_out[...] = context[...]
    own[...] = contract(hidden_own[...], down[...], ((1,), (0,))).astype(bf16).reshape(4, 128, 1024)
    other[...] = (
        contract(hidden_other[...], down[...], ((1,), (0,))).astype(bf16).reshape(4, 128, 1024)
    )


def wide_tiles_kernel(
    places, gate_own, normed_own, gate_other, normed_other, up_own, up_other,
    hidden_own, grad_own, hidden_other, grad_other, out,
):
    def tile_of(left_own, right_own, left_other, right_other):
        tile = contract(left_own.wait()[...], right_own().reshape(512, 1024), ((0,), (0,)))
        return tile + contract(
            left_other.wait()[...], right_other().reshape(512, 1024), ((0,), (0,))
        )

    def slot(s):
        return 2 * (s % 4) + lax.rem(s // 4 + places[3] // 4, 2)

    def columns(j, tile):
        rows = slice(SLICE * j, SLICE * j + SLICE)
        for s in range(8):
            out[slot(s), rows] = tile[:, 128 * s : 128 * s + 128].astype(bf16)
        out.send(slice(None), rows)

    first = tile_of(
        gate_own, lambda: normed_own.wait()[...], gate_other, lambda: normed_other.wait()[...]
    )
    columns(0, first)
    second = tile_of(
        up_own, lambda: normed_own.ref[...], up_other, lambda: normed_other.ref[...]
    )
    columns(1, second)
    tile = tile_of(
        hidden_own, lambda: grad_own.wait()[...], hidden_other, lambda: grad_other.wait()[...]
    ).astype(bf16)
    for s in range(8):
        rows = tile[PLACE * s : PLACE * s + PLACE]
        for d in range(8):
            start = 2 * SLICE + PLACE * d
            out[slot(s), start : start + PLACE] = rows[:, 128 * d : 128 * d + 128]
    out.send(slice(None), slice(2 * SLICE, 3 * SLICE))


def second_back_kernel(
    places, mix_ref, t0, t1, t2, t3, streams, branch1, cotangent, segments, out_own, out_other,
    grad_second, grad_columns, grad_context, low, turned,
):
    mix = Mix(mix_ref)
    live = live_column(segments)
    of_streams = [mix.second_of_streams(r) for r in range(4)]
    of_branch = mix.second_of_branch()
    of_grad = [sum(mix.g[0][s] * mix.r[1][q][s] for s in range(4)) for q in range(4)]
    for c in range(4):
        rows = slice(32 * c, 32 * c + 32)
        second = weighted(
            [(of_streams[r], streams[r, rows].astype(f32)) for r in range(4)]
            + [(of_branch, branch1[rows])]
        )
        normed, inverse = normalize(second)
        grad = (t0[rows] + t1[rows].astype(f32)) + (t2[rows].astype(f32) + t3[rows].astype(f32))
        back = norm_back(grad, normed, inverse)
        grad_second[rows] = back
        grad_second.send(rows)
        if c == 0:
            cotangent = cotangent.wait()
        branch = weighted(
            [(of_grad[q], cotangent[q, rows].astype(f32)) for q in range(4)] + [(of_branch, back)]
        )
        low[rows] = (live[rows] * branch).astype(bf16)
    for i in range(8):
        grad_columns[2 * (i % 4) + i // 4] = low[:, 128 * i : 128 * i + 128]
    grad_columns.send()
    own, other = halves(places[2])
    turned[...] = contract(out_own.wait()[...], low[:, own], ((1,), (1,)))
    turned[...] += contract(out_other.wait()[...], low[:, other], ((1,), (1,)))
    for c in range(16):
        grad_context[c] = turned[HD * HEAD_OF[c] : HD * HEAD_OF[c] + HD].astype(bf16)
        if c % 4 == 3:
            grad_context.send(pl.ds(c - 3, 4))


def mix_sums_kernel(
    mix_ref, t0, t1, t2, t3, streams, cotangent, branch1, grad_second, segments,
    out, branch2, acc,
):
    mix = Mix(mix_ref)
    live = live_column(segments)
    acc[...] = jnp.zeros_like(acc)
    for c in range(4):
        rows = slice(32 * c, 32 * c + 32)
        branch2[rows] = live[rows] * (
            (t0[rows] + t1[rows].astype(f32)) + (t2[rows].astype(f32) + t3[rows].astype(f32))
        )
    branch2.send()

    def fold(values):
        return sum(values[:8, 128 * j : 128 * j + 128] for j in range(4)) + sum(
            values[8:, 128 * j : 128 * j + 128] for j in range(4)
        )

    @pl.loop(0, 8)
    def _(r):
        rows = pl.ds(pl.multiple_of(r * 16, 16), 16)

        @pl.loop(0, 2)
        def _(l):
            lanes = pl.ds(pl.multiple_of(l * 512, 512), 512)
            hin = [streams[s, rows, lanes].astype(f32) for s in range(4)]
            branch, back = branch1[rows, lanes], grad_second[rows, lanes]
            last = branch2[rows, lanes]
            for q in range(4):
                top = cotangent[q, rows, lanes].astype(f32)
                for s in range(4):
                    acc[4 * q + s] += fold(top * hin[s])
                acc[16 + q] += fold(top * branch)
                acc[20 + q] += fold(top * last)
            for s in range(4):
                acc[24 + s] += fold(hin[s] * back)
            acc[28] += fold(branch * back)

    total = jnp.sum(acc[...], axis=1)

    def top_hin(q, s):
        return total[4 * q + s : 4 * q + s + 1]

    def top_branch(q):
        return total[16 + q : 17 + q]

    def back_hin(s):
        return total[24 + s : 25 + s]

    back_branch = total[28:29]
    for s in range(4):
        out[s * 6 : s * 6 + 1] = jnp.zeros((1, 128), f32)
        for r in range(4):
            row = s * 6 + 1 + r
            out[row : row + 1] = weighted(
                [(mix.r[1][q][s], top_hin(q, r)) for q in range(4)]
                + [(mix.p[1][s], back_hin(r))]
            )
            row = 24 + s * 6 + 1 + r
            out[row : row + 1] = weighted(
                [(mix.r[0][r][q], top_hin(s, q)) for q in range(4)]
                + [(mix.g[0][r], top_branch(s))]
            )
        row = s * 6 + 5
        out[row : row + 1] = weighted(
            [(mix.r[1][q][s], top_branch(q)) for q in range(4)] + [(mix.p[1][s], back_branch)]
        )
        row = 24 + s * 6
        out[row : row + 1] = weighted(
            [(mix.r[0][s][q], back_hin(q)) for q in range(4)] + [(mix.g[0][s], back_branch)]
        )
        row = 24 + s * 6 + 5
        out[row : row + 1] = total[20 + s : 21 + s]


def out_streams_kernel(mix_ref, streams, branch1, branch2, out):
    mix = Mix(mix_ref)
    of_streams = [
        [sum(mix.r[1][s][q] * mix.r[0][q][r] for q in range(4)) for r in range(4)]
        for s in range(4)
    ]
    of_branch = [sum(mix.r[1][s][q] * mix.g[0][q] for q in range(4)) for s in range(4)]
    for c in range(4):
        rows = slice(32 * c, 32 * c + 32)
        hin = [streams[s, rows].astype(f32) for s in range(4)]
        for s in range(4):
            total = weighted(
                [(of_streams[s][r], hin[r]) for r in range(4)]
                + [(of_branch[s], branch1[rows]), (mix.g[1][s], branch2[rows])]
            )
            out[s, rows] = total.astype(bf16)


def near_lanes(values, near):
    return jnp.concatenate(
        [values[:, TILE * k + 128 * near : TILE * k + 128 * near + 128] for k in range(4)], axis=1
    )


def pair_back_kernel(places, own, far, weights, grad, pair):
    half = places[1]
    own = own.wait()
    for j in range(3):
        rows = slice(HD * j, HD * j + HD)
        pair[pl.ds(pl.multiple_of(128 * j + HD * half, HD), HD), :] = own[rows]
        pair[pl.ds(pl.multiple_of(128 * j + HD * (1 - half), HD), HD), :] = far[rows]
    total = contract(near_lanes(pair, 1), weights.wait()[...], ((0,), (0,)))
    grad[...] = total.astype(bf16).reshape(4, 128, 1024)


def pair_back_own_kernel(pair, weights, grad):
    total = contract(near_lanes(pair, 0), weights[...], ((0,), (0,)))
    grad[...] = total.astype(bf16).reshape(4, 128, 1024)


def narrow_tiles_kernel(
    places, pair, normed_own, normed_other, columns, context_own, context_other, out
):
    z, core = places[0], places[2]
    pair = pair.wait()
    tile = jnp.zeros((384, 1024), f32)
    for near, tokens in enumerate((normed_own, normed_other)):
        tokens = tokens.wait()[:, 0:128].reshape(512, 1024)
        tile = tile + contract(near_lanes(pair, near), tokens, ((1,), (0,)))
    for s in range(8):
        out[s, 0:384] = tile[:, 128 * s : 128 * s + 128].astype(bf16)
    tile = jnp.zeros((128, 1024), f32)
    for near, contexts in enumerate((context_own, context_other)):
        contexts = ready(contexts)
        for back in range(4):
            source = columns[2 * lax.rem(z - back + 4, 4) + lax.rem(core + near, 2)]
            tile = tile + contract(source, contexts[back], ((0,), (1,)))
    for s in range(8):
        out[s, 384:512] = tile[:, 128 * s : 128 * s + 128].astype(bf16)


def fold_kernel(blocks, *outs):
    start = 0
    for out in outs:
        rows = slice(start, start + out.shape[0])
        total = blocks[0, rows].astype(f32)
        for s in range(1, 8):
            total = total + blocks[s, rows].astype(f32)
        out[...] = total.astype(bf16)
        start += out.shape[0]


def fold_narrow_kernel(blocks, out):
    total = blocks[0].astype(f32)
    for s in range(1, 8):
        total = total + blocks[s].astype(f32)
    out[0:512] = total[0:512].astype(bf16)
    high, low = two_parts(total[512:513] + total[513:514])
    out[512:528] = jnp.concatenate([high, low, jnp.zeros((14, 128), bf16)], axis=0)


def add_narrow_kernel(own, far, out):
    total = own[...].astype(f32) + far[...].astype(f32)
    out[0:512] = total[0:512].astype(bf16)
    high, low = two_parts(total[512:513] + total[513:514])
    out[512:528] = jnp.concatenate([high, low, jnp.zeros((14, 128), bf16)], axis=0)


def member(places, own, other, index):
    back = lax.rem(places[0] - index % 4 + 4, 4)
    return jnp.where(places[2] == index // 4, own[back].astype(f32), other[back].astype(f32))


def finish_wide_kernel(places, own, other, gate_up, down, rows):
    for i in range(8):
        block = member(places, own, other, i)
        for s in range(8):
            for j in range(2):
                start = SLICE * j + PLACE * s
                unit = 8 * PIECE * s + PIECE * i
                rows[j, unit : unit + PIECE] = block[start : start + PIECE]
        for d in range(8):
            start = 2 * SLICE + PLACE * d
            down[PIECE * i : PIECE * i + PIECE, 128 * d : 128 * d + 128] = block[
                start : start + PIECE
            ]
    down.send()
    for j in range(2):
        for k in range(rows.shape[1] // 128):
            lanes = slice(128 * k, 128 * k + 128)
            gate_up[j, :, lanes] = rows[j, lanes].T
        gate_up.send(j)


def finish_narrow_kernel(places, own, other, qkv, out, mix_grad):
    total = jnp.zeros((1, 128), f32)
    for i in range(8):
        block = member(places, own, other, i)
        total = total + (block[512:513] + block[513:514])
        for j in range(3):
            qkv[j, :, 128 * i : 128 * i + 128] = block[128 * j : 128 * j + 128].T
        out[:, 128 * i : 128 * i + 128] = block[384:512].T
        if i % 2:
            lanes = slice(128 * i - 128, 128 * i + 128)
            qkv.send(slice(None), slice(None), lanes)
            out.send(slice(None), lanes)
    for m in range(2):
        for s in range(4):
            lane = m * 24 + s * 6
            mix_grad[m, s : s + 1, :] = total[:, lane : lane + 6]


def two_parts(values):
    high = values.astype(bf16)
    return high, (values - high.astype(f32)).astype(bf16)


def first_back_kernel(
    mix_ref, t0, t1, t2, t3, streams, cotangent, grad_second, sums, tiles, streams_grad, out, mix_rows
):
    mix = Mix(mix_ref)
    of_top = [
        [sum(mix.r[1][q][s] * mix.r[0][s][r] for s in range(4)) for q in range(4)]
        for r in range(4)
    ]
    of_back = [sum(mix.r[0][s][r] * mix.p[1][s] for s in range(4)) for r in range(4)]
    total = [jnp.zeros((1, 1024), f32) for _ in range(4)]
    out.send_from(tiles.wait(), slice(None), slice(0, 512))
    cotangent, grad_second = cotangent.wait(), grad_second.wait()
    for c in range(4):
        rows = slice(32 * c, 32 * c + 32)
        hin = [streams[s, rows].astype(f32) for s in range(4)]
        top = [cotangent[s, rows].astype(f32) for s in range(4)]
        normed, inverse = normalize(weighted([(mix.p[0][s], hin[s]) for s in range(4)]))
        grad = (t0[rows] + t1[rows].astype(f32)) + (t2[rows].astype(f32) + t3[rows].astype(f32))
        back1 = norm_back(grad, normed, inverse)
        back2 = grad_second[rows]
        for r in range(4):
            value = weighted(
                [(of_top[r][q], top[q]) for q in range(4)]
                + [(of_back[r], back2), (mix.p[0][r], back1)]
            )
            streams_grad[r, rows] = value.astype(bf16)
            total[r] = total[r] + jnp.sum(hin[r] * back1, axis=0, keepdims=True)
        streams_grad.send(slice(None), rows)
    mix_rows[0:48] = sums.wait()[...]
    mix_rows[48:] = jnp.zeros((80, 128), f32)
    for s in range(4):
        row = sum(total[s][:, 128 * k : 128 * k + 128] for k in range(8))
        mix_rows[s * 6 : s * 6 + 1] = row
    high, low = two_parts(jnp.sum(mix_rows[...].T, axis=0, keepdims=True))
    rows = jnp.concatenate([high, low, jnp.zeros((14, 128), bf16)], axis=0)
    for s in range(8):
        out[s, 512:528] = rows
    out.send(slice(None), slice(512, 528))


def split_kernel(source, own, other):
    own[...] = source[0]
    other[...] = source[1]


def copy_kernel(source, out):
    out[...] = source[...]


def add4_kernel(one, two, three, four, out):
    out[...] = (one[...] + two[...]) + (three[...] + four[...])


def add2_kernel(one, two, out):
    out[...] = (one[...].astype(f32) + two[...].astype(f32)).astype(out.dtype)


def shards(
    streams, segments, stream_mix, qkv_weight, out_weight, gate_up_weight, down_weight, cotangent
):
    kept_arrays.arrays.clear()
    z, half, core = lax.axis_index("z"), lax.axis_index("xh"), lax.axis_index("co")
    team, row = lax.axis_index(TEAM), lax.axis_index(SHARD)
    width = streams.shape[3]
    ff = down_weight.shape[0]
    places = (jnp.stack([z, half, core, row, team]).astype(jnp.int32), smem)
    mix = (stream_mix, smem)
    streams, cotangent, segments = streams[0], cotangent[0], (segments, vmem)
    token = ((128, width), bf16)
    token4 = ((4, 128, width), bf16)

    def v(*values):
        return [(value, vmem) for value in values]

    def h(*values):
        return [(value, "hbm") for value in values]

    def l(*values):
        return [(value, "late") for value in values]

    def stack(values, parts, name, us=1, order=(), beside=(), in_hbm=False, place="hbm"):
        (result,) = call(
            stack_kernel,
            [((4,) + values.shape, bf16, place)],
            (h(values) if in_hbm else v(values)) + v(*parts),
            name,
            us,
            order=order,
            beside=beside,
        )
        return result

    (weights,) = call(
        pick_kernel,
        [((128, 896 + 2 * SLICE), bf16, "early")],
        [places] + l(out_weight, down_weight, gate_up_weight),
        "pick",
        4,
    )
    far_weights = shift(weights, "xl", 1)

    (normed1,) = call(
        first_norm_kernel,
        [((144, width), bf16)],
        [mix] + h(streams) + [segments],
        "first_norm",
        3,
        order=[weights],
    )
    (qkv_blocks,) = call(
        pick_heads_kernel,
        [((8, 3, 128, 128), bf16, "early")],
        [places, (qkv_weight, raw)],
        "pick_heads",
        2,
        [pltpu.VMEM((3, 128, 128), bf16)],
        beside=[normed1],
    )
    qkv_blocks = lax.all_to_all(qkv_blocks, SHARD, 0, 0, tiled=True)
    normed1_z = z_issue(normed1)
    (weights,) = call(
        pair_weights_kernel,
        [((2, 128, 896 + 2 * SLICE), bf16, "hbm")],
        h(weights) + v(far_weights),
        "pair_weights",
        1,
        beside=[normed1],
    )
    weights = lax.all_gather(weights, "y", axis=0, tiled=True)
    normed1_own = stack(normed1, normed1_z, "stack_normed1", 4)
    normed1_other = shift(normed1_own, "co", 1)
    freq = rope_base ** (-(jnp.arange(32, dtype=f32) * 2.0) / HD)
    back, near, place = jnp.arange(4), jnp.arange(2), jnp.arange(128)
    positions = (
        512 * ((z - back[None, :, None, None] + 4) % 4)
        + 256 * ((half + near[:, None, None, None]) % 2)
        + 128 * ((core + near[None, None, :, None]) % 2)
        + place[None, None, None, :]
    ).reshape(2, 1, 1024)
    angle = positions.astype(f32) * freq[None, :, None]
    cosine, sine = jnp.cos(angle), jnp.sin(angle)

    (pair_weights,) = call(
        turn_heads_kernel, [((384, width), bf16, "early")], v(qkv_blocks), "turn_heads", 1
    )
    kept, sent = call(
        project_kernel,
        [((208, 1024), bf16, "vmem"), ((208, 1024), bf16, "vmem")],
        [places] + l(normed1_own) + v(normed1_other) + h(pair_weights) + v(cosine, sine),
        "project",
        16,
    )
    received = shift(sent, "xh", 1)
    (grad_branch2,) = call(
        grad_branch2_kernel,
        [token],
        [mix] + h(cotangent) + [segments],
        "grad_branch2",
        0,
        order=[kept],
    )
    grad2_z = z_issue(grad_branch2)

    qkv, context_blocks, context_wide, logsum, edges = call(
        attend_kernel,
        [
            ((2, 192, 1024), bf16, "early"),
            ((16, HD, 128), bf16, "early"),
            ((2, HD, 1024), f32, "early"),
            ((2, 8, 1024), f32, "early"),
            ((4,), jnp.int32),
        ],
        [places] + h(kept) + v(received),
        "attend",
        12,
        beside=[grad_branch2],
    )
    context_mine = lax.all_to_all(context_blocks, CTX, 0, 0, tiled=True)

    grad2_own = stack(grad_branch2, grad2_z, "stack_grad2", 1, [context_blocks])
    grad2_other = shift(grad2_own, "co", 1)
    (out_own,) = call(
        unpack_out_kernel,
        [((width, 512), bf16, "vmem")],
        [places, (weights, ("late", 0, 512))],
        "unpack_out",
        3,
        order=[grad2_own],
    )
    out_other = shift(out_own, "co", 1)
    context, branch_half = call(
        post_attend_own_kernel,
        [((width, 128), bf16, "vmem"), ((128, 512), f32, "vmem")],
        v(context_mine) + h(out_own),
        "post_attend_own",
        15,
    )
    normed2, branch1 = call(
        post_attend_kernel,
        [token, ((128, width), f32, "early")],
        [places, mix]
        + h(context)
        + v(branch_half)
        + l(out_other, streams)
        + [segments],
        "post_attend",
        3,
    )
    normed2_z = z_issue(normed2)
    inner = ("late", 512, 896 + 2 * SLICE)
    gu_all, down = call(
        unpack_kernel,
        [((width, 2 * SLICE), bf16, "vmem"), ((SLICE, width), bf16, "vmem")],
        [places, (weights, inner)],
        "unpack",
        4,
        order=[out_own],
    )
    normed2_own = stack(normed2, normed2_z, "stack_normed2", order=[down])
    normed2_other = shift(normed2_own, "co", 1)
    acts = [token4 + ("vmem",)] + [((512, SLICE), bf16, "early")] * 3
    grad_own, hidden_own, gate_own, up_own = call(
        feed_forward_kernel,
        acts,
        l(normed2_own, grad2_own, gu_all, down),
        "feed_forward_own",
        5,
    )
    grad_other, hidden_other, gate_other, up_other = call(
        feed_forward_kernel,
        acts,
        v(normed2_other, grad2_other) + l(gu_all, down),
        "feed_forward_other",
        5,
        order=[hidden_own],
    )

    def core_add(own, other, name, order, beside=(), own_in_hbm=False):
        return call(
            core_add_kernel,
            [((128, width), f32, "vmem")] + [token] * 3,
            (h(own) if own_in_hbm else v(own)) + v(shift(other, "co", 1)),
            name,
            1,
            order=order,
            beside=beside,
        )

    def z_terms(terms):
        return [terms[0]] + [shift(term, "z", -k) for k, term in enumerate(terms[1:], 1)]

    half_own, half_other, context = call(
        branch2_kernel,
        [token4 + ("vmem",), token4 + ("vmem",), ((width, 128), bf16, "vmem")],
        h(hidden_own, hidden_other, down, context),
        "branch2",
        3,
        order=[hidden_other],
    )
    terms = core_add(grad_own, grad_other, "core_add_second", [half_own])
    grad_normed2 = z_terms(terms)
    context_z = z_issue(context)

    grad_second, grad_columns, grad_context = call(
        second_back_kernel,
        [
            ((128, width), f32, "early"),
            ((8, 128, 128), bf16, "early"),
            ((16, HD, 128), bf16, "early"),
        ],
        [places, mix]
        + h(grad_normed2[0])
        + v(*grad_normed2[1:])
        + h(streams, branch1)
        + l(cotangent)
        + [segments] + l(out_own, out_other),
        "second_back",
        5,
        [pltpu.VMEM((128, width), bf16), pltpu.VMEM((width, 128), f32)],
    )
    grad_context = lax.all_to_all(grad_context, CTX, 0, 0, tiled=True)

    (wide_tiles,) = call(
        wide_tiles_kernel,
        [((8, 3 * SLICE, 128), bf16, "early")],
        [places] + l(
            gate_own, normed2_own, gate_other, normed2_other, up_own, up_other,
            hidden_own, grad2_own, hidden_other, grad2_other,
        ),
        "wide_tiles",
        7,
        order=[grad_second],
    )
    wide_mine = lax.psum_scatter(wide_tiles, "y", scatter_dimension=0, tiled=True)

    terms = core_add(half_own, half_other, "core_add_branch2", [wide_tiles], own_in_hbm=True)
    branch2 = z_terms(terms)
    grads_own, grads_far, columns = call(
        attend_back_kernel,
        [((192, 1024), bf16, "early"), ((192, 1024), bf16, "vmem"), ((8, 128, 128), bf16, "early")],
        [places, (edges, smem)]
        + h(qkv, context_wide, logsum)
        + v(grad_context, cosine, sine)
        + h(grad_columns),
        "attend_back",
        40,
        [
            pltpu.VMEM((2, HD, 1024), f32),
            pltpu.VMEM((2, HD, 1024), f32),
            pltpu.VMEM((2, HD, 1024), bf16),
        ],
        [terms[0]],
    )
    received = shift(grads_far, "xh", 1)
    columns = lax.all_to_all(columns, ("z", "co"), 0, 0, tiled=True)
    sums, branch2 = call(
        mix_sums_kernel,
        [((48, 128), f32, "vmem"), ((128, width), f32, "early")],
        [mix]
        + h(branch2[0])
        + v(*branch2[1:])
        + h(streams, cotangent, branch1, grad_second)
        + [segments],
        "mix_sums",
        7,
        [pltpu.VMEM((32, 8, 128), f32)],
        [grads_own],
        context_z,
    )
    context_own = stack(context, context_z, "stack_context", 1, [sums], in_hbm=True, place="vmem")
    context_other = shift(context_own, "co", 1)
    wide_type = ((3 * SLICE, 128), bf16)
    wide_mine, wide_far = call(
        split_kernel, [wide_type, wide_type], h(wide_mine), "split_wide", 1, order=[context_own]
    )
    wide_far = shift(wide_far, "xl", 1)
    grad_other, pair = call(
        pair_back_kernel,
        [token4 + ("vmem",), ((384, 1024), bf16, "vmem")],
        [places] + l(grads_own) + v(received) + l(pair_weights),
        "pair_back",
        4,
        order=[context_own],
        beside=[columns, wide_mine],
    )
    (grad_own,) = call(
        pair_back_own_kernel, [token4 + ("vmem",)], h(pair, pair_weights), "pair_back_own", 3
    )
    terms = core_add(grad_own, grad_other, "core_add_first", [])
    grad_normed1 = z_terms(terms)

    (narrow_tiles,) = call(
        narrow_tiles_kernel,
        [((8, 512, 128), bf16, "vmem")],
        [places]
        + l(pair, normed1_own, normed1_other)
        + v(columns)
        + l(context_own)
        + v(context_other),
        "narrow_tiles",
        6,
        order=[terms[0]],
    )
    narrow_order = narrow_tiles
    (wide_rows,) = call(
        add2_kernel, [wide_type], v(wide_mine, wide_far), "add_wide_xl", 1, order=[narrow_order], beside=grad_normed1[1:]
    )
    wide_far = shift(wide_rows, "xh", 1)
    streams_grad, narrow_tiles = call(
        first_back_kernel,
        [token4 + ("early",), ((8, 528, 128), bf16, "early")],
        [mix]
        + h(grad_normed1[0])
        + v(*grad_normed1[1:])
        + h(streams)
        + l(cotangent, grad_second, sums, narrow_tiles),
        "first_back",
        6,
        [pltpu.VMEM((128, 128), f32)],
    )
    narrow_tiles = lax.all_to_all(narrow_tiles, SHARD, 0, 0, tiled=True)

    (wide_rows,) = call(
        add2_kernel, [wide_type], v(wide_rows, wide_far), "add_wide", 1, order=[streams_grad]
    )
    wide_z = z_issue(wide_rows)
    (out_streams,) = call(
        out_streams_kernel,
        [token4 + ("hbm",)],
        [mix] + h(streams, branch1, branch2),
        "out_streams",
        8,
        beside=[wide_rows],
    )
    narrow_type = [((528, 128), bf16)]
    (mine,) = call(fold_narrow_kernel, narrow_type, v(narrow_tiles), "fold_narrow", 1, order=[out_streams])
    narrow_far = shift(mine, "xh", 1)
    wide_own = stack(wide_rows, wide_z, "stack_wide", 1, beside=[mine])
    wide_other = shift(wide_own, "co", 1)
    (narrow_rows,) = call(
        add_narrow_kernel, narrow_type, v(mine, narrow_far), "add_narrow", 1, order=[wide_own]
    )
    narrow_z = z_issue(narrow_rows)
    gate_up_grad, down_grad = call(
        finish_wide_kernel,
        [((2, 128, 8 * ff), f32, "early"), ((ff, width), f32, "early")],
        [places] + h(wide_own) + v(wide_other),
        "finish_wide",
        5,
        [pltpu.VMEM((2, 8 * ff, 128), f32)],
        beside=[narrow_rows],
    )
    narrow_own = stack(narrow_rows, narrow_z, "stack_narrow", 1, [down_grad])
    narrow_other = shift(narrow_own, "co", 1)
    qkv_grad, out_grad, mix_grad = call(
        finish_narrow_kernel,
        [((3, 128, width), f32, "early"), ((128, width), f32, "early"), ((2, 4, 6), f32)],
        [places] + h(narrow_own) + v(narrow_other),
        "finish_narrow",
        3,
    )
    return (
        out_streams[None], streams_grad[None], qkv_grad, out_grad, gate_up_grad, down_grad, mix_grad,
    )


def solution(mesh):
    fine = Mesh(
        np.asarray(mesh.devices).reshape([n for _, n in AXES]), tuple(name for name, _ in AXES)
    )
    in_specs = (
        P(SHARD, None, CTX, None),
        P(SHARD, CTX),
        P(),
        P(None, SHARD, None),
        P(SHARD, None),
        P(None, SHARD, None),
        P(SHARD, None),
        P(SHARD, None, CTX, None),
    )
    out_specs = (
        P(SHARD, None, CTX, None),
        P(SHARD, None, CTX, None),
        P(None, SHARD, None),
        P(SHARD, None),
        P(None, SHARD, None),
        P(SHARD, None),
        P(),
    )
    return jax.shard_map(shards, mesh=fine, in_specs=in_specs, out_specs=out_specs, check_vma=False)
```
